128 devices in a mesh: dp: 64 (over y, z_hi, x, core), mp: 2 (over z_lo).
Axes of the slice: x: 4, y: 4, z: 4 (z_hi: 2, z_lo: 2; z = z_hi * 2 + z_lo), core: 2. Of those that a mesh axis runs over, the one named last changes fastest.
Arguments:
- img_feat: bfloat16 [13312, 1152], P('dp'), may hold values from -16 to 16
- img_head: bfloat16 [1152, 1152], P(None, 'mp'), may hold values from -0.1875 to 0.1875
- txt_feat: bfloat16 [13312, 1152], P('dp'), may hold values from -6 to 6
- txt_head: bfloat16 [1152, 1152], P('mp'), may hold values from -0.1875 to 0.1875
Outputs:
- grad_img: float32 [13312, 1152], P('dp', 'mp')
- grad_img_head: float32 [1152, 1152], P('dp', 'mp')
- grad_txt: float32 [13312, 1152], P('dp', 'mp')
- grad_txt_head: float32 [1152, 1152], P('mp', 'dp')
The draws below stay inside these ranges and needn't reach their ends.
All inputs are finite; a program needn't handle non-finite values.
Results may differ from the reference program's by a relative error of at most 0.014.
Values may be sent and summed in bfloat16 or wider, within the bound.
A program may use at most 128 MiB of HBM per device.

```python
import jax
import jax.numpy as jnp
from jax import lax

D = 1152
PAIRS = 208
BATCH = 13312
N_DP = 64


def spiked(array, stream_key, source, target, parts, factor):
    def block_of(dim):
        return (jnp.arange(array.shape[dim]) // (array.shape[dim] // parts)).reshape((-1,) + (1,) * (array.ndim - 1 - dim))

    near = jax.random.permutation(stream_key, parts)[block_of(target)]
    far = (block_of(target) + parts // 2) % parts
    return jnp.where((block_of(source) == near) | (block_of(source) == far), factor * array, array)


def block_levels(stream_key, dims, cuts, least, top_value):
    gain, own = 1.0, jax.random.fold_in(stream_key, 6)
    for position, blocks in cuts:
        draws = jnp.exp(jax.random.uniform(jax.random.fold_in(own, position), (blocks,), jnp.float32, least / len(cuts), top_value / len(cuts)))
        gain = gain * jnp.repeat(draws, dims[position] // blocks).reshape([-1 if axis == position else 1 for axis in range(len(dims))])
    return gain


def scatter_about(stream_key, shape, width, limit, cuts=(), kind=jnp.bfloat16):
    entries = width * jax.random.normal(stream_key, shape, jnp.float32)
    if cuts:
        entries = entries * block_levels(stream_key, shape, cuts, -0.22, 0.18)
    return jnp.clip(entries, -limit, limit).astype(kind)


def gaussian_with(stream_key, extent, spread, reach, cuts, heavy, kind=jnp.bfloat16):
    array = spread * jax.random.normal(stream_key, extent, jnp.float32)
    if cuts:
        array = array * block_levels(stream_key, extent, cuts, -0.22, 0.18)
    return jnp.clip(spiked(array, jax.random.fold_in(stream_key, 3), *heavy), -reach, reach).astype(kind)


def setup_inputs(seed: int = 0) -> dict:
    arg_keys = jax.random.split(jax.random.key(seed), 5)
    return {
        "img_feat": gaussian_with(arg_keys[0], (BATCH, D), 1.0, 16.0, ((0, 64),), (0, 1, 64, 4.0)),
        "img_head": scatter_about(arg_keys[1], (D, D), D ** -0.5, 0.1875, ((1, 2),)),
        "txt_feat": scatter_about(arg_keys[2], (BATCH, D), 1.0, 6.0, ((0, 64),)),
        "txt_head": scatter_about(arg_keys[3], (D, D), D ** -0.5, 0.1875, ((0, 2),)),
    }


LOGIT_SCALE = 10.0
LOGIT_BIAS = -2.5
NORM_EPS = 1e-06

def reference(img_feat, img_head, txt_feat, txt_head):
    img_proj = jnp.dot(img_feat, img_head, preferred_element_type=jnp.float32).astype(jnp.bfloat16)
    img_wide = img_proj.astype(jnp.float32)
    img_scale = lax.rsqrt(lax.optimization_barrier(jnp.sum(img_wide * img_wide, -1, keepdims=True)) + NORM_EPS)
    img_emb = (img_wide * img_scale).astype(jnp.bfloat16)
    txt_wide = txt_feat.astype(jnp.float32)
    row_mean = lax.optimization_barrier(jnp.mean(txt_wide, -1, keepdims=True))
    centered = txt_wide - row_mean
    txt_rscale = lax.rsqrt(lax.optimization_barrier(jnp.mean(centered * centered, -1, keepdims=True)) + NORM_EPS)
    txt_norm = centered * txt_rscale
    txt_norm_b = txt_norm.astype(jnp.bfloat16)
    txt_proj = jnp.dot(txt_norm_b, txt_head, preferred_element_type=jnp.float32)
    txt_scale = lax.rsqrt(lax.optimization_barrier(jnp.sum(txt_proj * txt_proj, -1, keepdims=True)) + NORM_EPS)
    txt_emb = (txt_proj * txt_scale).astype(jnp.bfloat16)
    all_ids = jnp.arange(BATCH, dtype=jnp.int32)

    def block(carried, start):
        rows = lax.dynamic_slice_in_dim(img_emb, start, PAIRS, 0)
        row_ids = start + jnp.arange(PAIRS, dtype=jnp.int32)
        scores = jnp.dot(rows, txt_emb.T, preferred_element_type=jnp.float32)
        logits = LOGIT_SCALE * scores + LOGIT_BIAS
        match = (row_ids[:, None] == all_ids[None, :]).astype(jnp.float32)
        weights = (jax.nn.sigmoid(logits) - match).astype(jnp.bfloat16)
        grad_rows = LOGIT_SCALE * jnp.dot(weights, txt_emb, preferred_element_type=jnp.float32)
        carried = carried + LOGIT_SCALE * jnp.dot(weights.T, rows, preferred_element_type=jnp.float32)
        return (carried, grad_rows)
    starts = jnp.arange(N_DP, dtype=jnp.int32) * PAIRS
    txt_emb_grad, blocks = lax.scan(block, jnp.zeros((BATCH, D), jnp.float32), starts)
    img_emb_grad = blocks.reshape(BATCH, D)
    img_dot = lax.optimization_barrier(jnp.sum(img_wide * img_emb_grad, -1, keepdims=True))
    img_proj_grad = (img_scale * img_emb_grad - img_scale ** 3 * img_wide * img_dot).astype(jnp.bfloat16)
    grad_img_head = jnp.dot(img_feat.T, img_proj_grad, preferred_element_type=jnp.float32)
    grad_img = jnp.dot(img_proj_grad, img_head.T, preferred_element_type=jnp.float32)
    txt_dot = lax.optimization_barrier(jnp.sum(txt_proj * txt_emb_grad, -1, keepdims=True))
    txt_proj_grad = (txt_scale * txt_emb_grad - txt_scale ** 3 * txt_proj * txt_dot).astype(jnp.bfloat16)
    grad_txt_head = jnp.dot(txt_norm_b.T, txt_proj_grad, preferred_element_type=jnp.float32)
    norm_grad = jnp.dot(txt_proj_grad, txt_head.T, preferred_element_type=jnp.float32)
    first_mean = lax.optimization_barrier(jnp.mean(norm_grad, -1, keepdims=True))
    second_mean = lax.optimization_barrier(jnp.mean(norm_grad * txt_norm, -1, keepdims=True))
    grad_txt = txt_rscale * (norm_grad - first_mean - txt_norm * second_mean)
    return (grad_img, grad_img_head, grad_txt, grad_txt_head)
```

```python
import types

import jax
import jax.numpy as jnp
from jax import lax
from jax.experimental import pallas as pl
from jax.experimental.pallas import tpu as pltpu
from jax.sharding import PartitionSpec as P

LOGIT_SCALE = 10.0
LOGIT_BIAS = -2.5
NORM_EPS = 1e-06

NX = 4
NY = 4
NZ = 2
NC = 2
D = 1152
HALF = D // 2
PAIRS = 208
OWN = PAIRS // 2
WIN = 112
STEP = PAIRS - WIN
TC = NZ * WIN
IMGS = NX * PAIRS
YROWS = D // NY
ZROWS = YROWS // NZ
LAST = ZROWS // (NX * NC)
FIN = 32

NN = ((1,), (0,))
NT = ((1,), (1,))
TN = ((0,), (0,))
BF = jnp.bfloat16
F32 = jnp.float32

SCRATCH = {
    "nhf": ((PAIRS, HALF), F32),
    "nhb": ((PAIRS, HALF), BF),
    "rs": ((PAIRS, 128), F32),
    "tpart": ((PAIRS, D), F32),
    "tsend": ((WIN, D), BF),
    "trecv": ((WIN, D), BF),
    "u": ((2, 8, D), F32),
    "tproj": ((WIN, D), F32),
    "tsc": ((WIN, 128), F32),
    "ih": ((2, PAIRS, HALF), BF),
    "iproj": ((PAIRS, D), BF),
    "isc": ((PAIRS, 128), F32),
    "img": ((IMGS, D), BF),
    "txt": ((NY, NC, TC, D), BF),
    "w": ((NY, NC, IMGS, TC), BF),
    "gi": ((IMGS, D), F32),
    "xsend": ((NX, PAIRS, D), BF),
    "xrecv": ((NX, PAIRS, D), BF),
    "gtcsend": ((NY, TC, D), BF),
    "gtcrecv": ((NY, TC, D), BF),
    "gt": ((TC, D), F32),
    "gtsum": ((TC, D), F32),
    "ysend": ((NY, TC, D), BF),
    "yrecv": ((NY, TC, D), BF),
    "zsend": ((WIN, D), BF),
    "zrecv": ((WIN, D), BF),
    "tw": ((2, WIN, D), BF),
    "sw": ((2, WIN, 128), F32),
    "tpg": ((PAIRS, D), BF),
    "sec": ((PAIRS, 128), F32),
    "ghalf": ((PAIRS, HALF), F32),
    "izsend": ((PAIRS, HALF), BF),
    "izrecv": ((PAIRS, HALF), BF),
    "dots": ((2, PAIRS, 128), F32),
    "pg": ((PAIRS, HALF), BF),
    "gip": ((PAIRS, D), F32),
    "gsend": ((PAIRS, HALF), BF),
    "grecv": ((PAIRS, HALF), BF),
    "hs": ((NC, D, HALF), BF),
    "hcrecv": ((D, HALF), BF),
    "hysend": ((D, HALF), BF),
    "hyrecv": ((NY, YROWS, HALF), BF),
    "hown": ((YROWS, HALF), F32),
    "hzsend": ((ZROWS, HALF), BF),
    "hzrecv": ((ZROWS, HALF), BF),
    "hx": ((ZROWS, HALF), BF),
    "fin": ((NC, NX, FIN, HALF), BF),
}

SENDS = {}
total_sends = 0
for group, many in (
    ("t", 1), ("u", 1), ("ih", 1), ("img", NX), ("txty", NY), ("txtz", 1), ("txty2", NY), ("txtc", NY),
    ("x", NX), ("iz", 1), ("dots", 1), ("gtc", NY), ("y", NY), ("z", 1), ("tw", 1), ("sw", 1), ("g", 1),
    ("hc", 1), ("hy", NY), ("hz", 1), ("fin", NX * NC),
):
    SENDS[group] = total_sends
    total_sends += many

RECVS = {}
total_recvs = 0
for group, many in (
    ("t", 1), ("u", 1), ("ih", 1), ("img", NX), ("txt", NY * NZ), ("txtc", NY),
    ("x", NX), ("iz", 1), ("dots", 1), ("gtc", NY), ("y", NY), ("z", 1), ("tw", 1), ("sw", 1), ("g", 1),
    ("hc", 1), ("hy", NY), ("hz", 1), ("fin", NX * NC),
):
    RECVS[group] = total_recvs
    total_recvs += many


def dot(a, b, dims):
    return lax.dot_general(a, b, (dims, ((), ())), preferred_element_type=F32)


def rows(i, first=0):
    return pl.ds(pl.multiple_of(first + i * 16, 16), 16)


def rowsum(v):
    return jnp.sum(v, -1, keepdims=True)


def wide(v):
    return jnp.broadcast_to(v, (v.shape[0], 128))


def each(count, body):
    lax.fori_loop(0, count, lambda i, c: (body(i), c)[1], 0)


def kernel(img_feat, img_head, txt_feat, txt_head, g_img, g_ih, g_txt, g_th, *scratch):
    s = types.SimpleNamespace(**dict(zip(SCRATCH, scratch)))
    ssem, rsem = scratch[len(SCRATCH) :]
    dp, m = lax.axis_index("dp"), lax.axis_index("mp")
    core = lax.rem(dp, NC)
    x = lax.rem(dp // NC, NX)
    zh = lax.rem(dp // (NC * NX), NZ)
    y = dp // (NC * NX * NZ)
    om, oc, oz = 1 - m, 1 - core, 1 - zh

    def dev(yy=None, zz=None, xx=None, cc=None, mm=None):
        yy = y if yy is None else yy
        zz = zh if zz is None else zz
        xx = x if xx is None else xx
        cc = core if cc is None else cc
        mm = m if mm is None else mm
        return (((yy * NZ + zz) * NX + xx) * NC + cc, mm)

    mate, twin, far = dev(mm=om), dev(cc=oc), dev(zz=oz)

    def copy(src, dst, group, send_at, recv_at, to, recv_group=None):
        return pltpu.make_async_remote_copy(
            src_ref=src,
            dst_ref=dst,
            send_sem=ssem.at[SENDS[group] + send_at],
            recv_sem=rsem.at[RECVS[recv_group or group] + recv_at],
            device_id=to,
            device_id_type=pl.DeviceIdType.MESH,
        )

    def other(base, by, size):
        return lax.rem(base + by, size)

    def pick(whole, which):
        return jnp.where(which == 0, whole[:, :HALF], whole[:, HALF:])

    barrier = pltpu.get_barrier_semaphore()
    friends = [mate, twin, far]
    friends += [dev(yy=other(y, d, NY)) for d in range(1, NY)]
    friends += [dev(xx=other(x, d, NX), cc=c) for d in range(1, NX) for c in (core, oc)]
    for friend in friends:
        pl.semaphore_signal(barrier, inc=1, device_id=friend, device_id_type=pl.DeviceIdType.MESH)

    def norm(i):
        r = rows(i)
        t = txt_feat[r, :].astype(F32)
        c = t - rowsum(t) * (1.0 / D)
        rs = lax.rsqrt(rowsum(c * c) * (1.0 / D) + NORM_EPS)
        half = pick(c * rs, m)
        s.nhf[r, :] = half
        s.nhb[r, :] = half.astype(BF)
        s.rs[r, :] = wide(rs)

    each(PAIRS // 16, norm)
    s.tpart[...] = dot(s.nhb[...], txt_head[...], NN)

    def tosend(i):
        s.tsend[rows(i), :] = s.tpart[rows(i, om * STEP), :].astype(BF)

    each(WIN // 16, tosend)
    pl.semaphore_wait(barrier, len(friends))
    t_copy = copy(s.tsend, s.trecv, "t", 0, 0, mate)
    t_copy.start()
    s.u[m] = dot(jnp.ones((8, HALF), BF), txt_head[...], NN)
    u_copy = copy(s.u.at[m], s.u.at[m], "u", 0, 0, mate)
    u_copy.start()

    s.ih[m] = dot(img_feat[...], img_head[...], NN).astype(BF)
    ih_copy = copy(s.ih.at[m], s.ih.at[m], "ih", 0, 0, mate)
    ih_copy.start()

    t_copy.wait_recv()

    def embed_text(i):
        p = s.tpart[rows(i, m * STEP), :] + s.trecv[rows(i), :].astype(F32)
        sc = lax.rsqrt(rowsum(p * p) + NORM_EPS)
        row = m * STEP + i * 16 + lax.broadcasted_iota(jnp.int32, (16, 1), 0)
        mine = (row >= m * OWN) & (row < m * OWN + OWN)
        s.tproj[rows(i), :] = p
        s.tsc[rows(i), :] = wide(sc)
        s.txt[y, core, rows(i, zh * WIN), :] = jnp.where(mine, p * sc, 0.0).astype(BF)

    each(WIN // 16, embed_text)

    def part(yy, zz):
        return s.txt.at[yy, core, pl.ds(pl.multiple_of(zz * WIN, 16), WIN)]

    def text_y(d):
        yy = other(y, d, NY)
        return copy(part(y, zh), part(y, zh), "txty", d, y * NZ + zh, dev(yy=yy), "txt")

    def text_y2(d):
        yy = other(y, d, NY)
        return copy(part(y, oz), part(y, oz), "txty2", d, y * NZ + oz, dev(yy=yy), "txt")

    def text_c(k, yy):
        return copy(s.txt.at[yy, core], s.txt.at[yy, core], "txtc", k, yy, twin)

    def text_arrival(yy, zz):
        return copy(part(yy, zz), part(yy, zz), "txty", 0, yy * NZ + zz, far, "txt")

    text_z = copy(part(y, zh), part(y, zh), "txtz", 0, y * NZ + zh, far, "txt")
    text_z.start()
    for d in (1, 3, 2):
        text_y(d).start()

    ih_copy.wait_recv()

    def embed_image(i):
        r = rows(i)
        p = jnp.concatenate([s.ih[0, r, :].astype(F32), s.ih[1, r, :].astype(F32)], axis=1)
        sc = lax.rsqrt(rowsum(p * p) + NORM_EPS)
        s.iproj[r, :] = p.astype(BF)
        s.isc[r, :] = wide(sc)
        s.img[rows(i, x * PAIRS), :] = (p * sc).astype(BF)

    each(PAIRS // 16, embed_image)

    def images(xx):
        return pl.ds(pl.multiple_of(xx * PAIRS, 16), PAIRS)

    def image_copy(d, slot, to):
        return copy(s.img.at[images(slot)], s.img.at[images(slot)], "img", d, slot, to)

    for d in (1, 3, 2):
        image_copy(d, x, dev(xx=other(x, d, NX))).start()

    def zero(i):
        s.gi[rows(i), :] = jnp.zeros((16, D), F32)

    each(IMGS // 16, zero)
    text_arrival(y, oz).wait_recv()
    for d in (1, 3, 2):
        text_y2(d).start()
    text_c(0, y).start()

    def order(k):
        return k + k // 2 - 2 * (k // 3)

    def block(step):
        k, h = step // 2, lax.rem(step, 2)
        yy = other(y, order(k), NY)
        cc = lax.rem(core + h, NC)

        @pl.when((h == 0) & (k > 0))
        def _():
            text_arrival(yy, 0).wait_recv()
            text_arrival(yy, 1).wait_recv()
            text_c(k, yy).start()

        @pl.when(h == 1)
        def _():
            copy(s.txt.at[yy, oc], s.txt.at[yy, oc], "txtc", 0, yy, twin).wait_recv()

        delta = jnp.where(step == 0, x * PAIRS + m * STEP - zh * WIN, 1 << 20)

        def piece(j):
            xx = other(x, order(j), NX)

            @pl.when((step == 0) & (j > 0))
            def _():
                image_copy(0, xx, twin).wait_recv()

            texts = s.txt[yy, cc]
            scores = dot(s.img[images(xx), :], texts, NT)
            weights = 0.5 + 0.5 * jnp.tanh((0.5 * LOGIT_SCALE) * scores + 0.5 * LOGIT_BIAS)
            row = xx * PAIRS + lax.broadcasted_iota(jnp.int32, (PAIRS, TC), 0)
            col = lax.broadcasted_iota(jnp.int32, (PAIRS, TC), 1)
            match = (row - col == delta) & (col >= zh * WIN) & (col < zh * WIN + WIN)
            weights = (weights - match.astype(F32)).astype(BF)
            s.w[yy, cc, images(xx), :] = weights
            s.gi[images(xx), :] += dot(weights, texts, NN)

        each(NX, piece)

    each(NY * NC, block)

    def image_back(d, slot, to):
        return copy(s.xsend.at[slot], s.xrecv.at[x], "x", d, x, to)

    for d in (2, 1, 3):
        xx = other(x, d, NX)

        def cast(i, xx=xx):
            s.xsend[xx, rows(i), :] = s.gi[rows(i, xx * PAIRS), :].astype(BF)

        each(PAIRS // 16, cast)
        image_back(d, xx, dev(xx=xx)).start()

    def text_back_c(yy):
        return copy(s.gtcsend.at[yy], s.gtcrecv.at[yy], "gtc", yy, yy, twin)

    def text_back_y(d, yy, to):
        return copy(s.ysend.at[yy], s.yrecv.at[y], "y", d, y, to)

    def text_grad(k):
        d = lax.rem(2 + 2 * NY - order(k), NY)
        d = jnp.where(k == 3, 0, jnp.where(k == 0, 2, 2 * k - 1))
        yy = other(y, d, NY)
        s.gtcsend[yy] = dot(s.w[yy, oc], s.img[...], TN).astype(BF)
        text_back_c(yy).start()
        s.gt[...] = dot(s.w[yy, core], s.img[...], TN)
        text_back_c(yy).wait_recv()

        @pl.when(k < 3)
        def _():
            def add(i):
                s.ysend[yy, rows(i), :] = (s.gt[rows(i), :] + s.gtcrecv[yy, rows(i), :].astype(F32)).astype(BF)

            each(TC // 16, add)
            text_back_y(d, yy, dev(yy=yy)).start()

        @pl.when(k == 3)
        def _():
            def add(i):
                s.gtsum[rows(i), :] = s.gt[rows(i), :] + s.gtcrecv[yy, rows(i), :].astype(F32)

            each(TC // 16, add)

    each(NY, text_grad)

    for d in (1, 3, 2):
        copy(s.xsend.at[0], s.xrecv.at[other(x, d, NX)], "x", 0, other(x, d, NX), twin).wait_recv()

    def image_sum(i):
        r = rows(i)
        g = s.gi[rows(i, x * PAIRS), :]
        for d in (1, 3, 2):
            g = g + s.xrecv[other(x, d, NX), r, :].astype(F32)
        g = LOGIT_SCALE * g
        s.dots[m, r, :] = wide(rowsum(g * s.iproj[r, :].astype(F32)))
        s.ghalf[r, :] = pick(g, m)
        s.izsend[r, :] = pick(g, om).astype(BF)

    each(PAIRS // 16, image_sum)
    iz_copy = copy(s.izsend, s.izrecv, "iz", 0, 0, mate)
    dots_copy = copy(s.dots.at[m], s.dots.at[m], "dots", 0, 0, mate)
    dots_copy.start()
    iz_copy.start()

    for d in (1, 3, 2):
        copy(s.ysend.at[0], s.yrecv.at[other(y, d, NY)], "y", 0, other(y, d, NY), twin).wait_recv()

    def text_sum(r):
        g = s.gtsum[r, :]
        for d in (1, 3, 2):
            g = g + s.yrecv[other(y, d, NY), r, :].astype(F32)
        return g

    def text_far(i):
        s.zsend[rows(i), :] = text_sum(rows(i, oz * WIN)).astype(BF)

    each(WIN // 16, text_far)
    z_copy = copy(s.zsend, s.zrecv, "z", 0, 0, far)
    z_copy.start()

    def text_near(i):
        s.gt[rows(i), :] = text_sum(rows(i, zh * WIN))

    each(WIN // 16, text_near)

    dots_copy.wait_recv()
    iz_copy.wait_recv()

    def image_grad(i):
        r = rows(i)
        g = s.ghalf[r, :] + s.izrecv[r, :].astype(F32)
        sc = s.isc[r, :][:, :1]
        total = (s.dots[0, r, :] + s.dots[1, r, :])[:, :1]
        p = pick(s.iproj[r, :].astype(F32), m)
        s.pg[r, :] = (sc * g - (sc * sc * sc) * p * total).astype(BF)

    each(PAIRS // 16, image_grad)
    s.gip[...] = dot(s.pg[...], img_head[...], NT)

    def image_out(i):
        s.gsend[rows(i), :] = pick(s.gip[rows(i), :], om).astype(BF)

    each(PAIRS // 16, image_out)
    g_copy = copy(s.gsend, s.grecv, "g", 0, 0, mate)

    z_copy.wait_recv()

    def text_own(i):
        r = rows(i)
        g = LOGIT_SCALE * (s.gt[r, :] + s.zrecv[r, :].astype(F32))
        p = s.tproj[r, :]
        sc = s.tsc[r, :][:, :1]
        v = sc * g - (sc * sc * sc) * p * rowsum(p * g)
        row = m * STEP + i * 16 + lax.broadcasted_iota(jnp.int32, (16, 1), 0)
        mine = (row >= m * OWN) & (row < m * OWN + OWN)
        v = jnp.where(mine, v, 0.0).astype(BF)
        s.tw[m, r, :] = v
        s.sw[m, r, :] = wide(rowsum(v.astype(F32) * p))

    each(WIN // 16, text_own)
    tw_copy = copy(s.tw.at[m], s.tw.at[m], "tw", 0, 0, mate)
    sw_copy = copy(s.sw.at[m], s.sw.at[m], "sw", 0, 0, mate)
    tw_copy.start()
    sw_copy.start()
    g_copy.start()
    s.hs[0] = dot(img_feat[...], s.pg[...], TN).astype(BF)
    tw_copy.wait_recv()
    sw_copy.wait_recv()
    u_copy.wait_recv()

    def merge(i):
        lo, hi = jnp.minimum(i, 6), jnp.maximum(i - 6, 0)
        v = jnp.where(i <= 6, s.tw[0, rows(lo), :].astype(F32), 0.0)
        v = v + jnp.where(i >= 6, s.tw[1, rows(hi), :].astype(F32), 0.0)
        s.tpg[rows(i), :] = v.astype(BF)
        v = jnp.where(i <= 6, s.sw[0, rows(lo), :], 0.0)
        s.sec[rows(i), :] = v + jnp.where(i >= 6, s.sw[1, rows(hi), :], 0.0)

    each(PAIRS // 16, merge)
    s.hs[1] = dot(s.tpg[...], s.nhb[...], TN).astype(BF)
    hc_copy = copy(s.hs.at[oc], s.hcrecv, "hc", 0, 0, twin)
    hc_copy.start()

    g_txt[...] = dot(s.tpg[...], txt_head[...], NT)

    def text_input(i):
        r = rows(i)
        u = (s.u[0] + s.u[1])[:1, :]
        first = rowsum(s.tpg[r, :].astype(F32) * u) * (1.0 / D)
        second = s.sec[r, :][:, :1] * (1.0 / D)
        g_txt[r, :] = s.rs[r, :][:, :1] * (g_txt[r, :] - first - s.nhf[r, :] * second)

    each(PAIRS // 16, text_input)

    hc_copy.wait_recv()

    def head_sum(r):
        return s.hs[core, r, :].astype(F32) + s.hcrecv[r, :].astype(F32)

    def head_y(d, to):
        yy = other(y, d, NY)
        src = s.hysend.at[pl.ds(pl.multiple_of(yy * YROWS, 16), YROWS)]
        return copy(src, s.hyrecv.at[y], "hy", d, y, to)

    for d in (2, 1, 3):
        yy = other(y, d, NY)

        def cast_head(i, yy=yy):
            r = rows(i, yy * YROWS)
            s.hysend[r, :] = head_sum(r).astype(BF)

        each(YROWS // 16, cast_head)
        head_y(d, dev(yy=yy)).start()

    def head_own(i):
        s.hown[rows(i), :] = head_sum(rows(i, y * YROWS))

    each(YROWS // 16, head_own)

    g_copy.wait_recv()

    def image_input(i):
        r = rows(i)
        g_img[r, :] = pick(s.gip[r, :], m) + s.grecv[r, :].astype(F32)

    each(PAIRS // 16, image_input)

    for d in (1, 3, 2):
        yy = other(y, d, NY)
        copy(s.hyrecv.at[0], s.hyrecv.at[yy], "hy", 0, yy, twin).wait_recv()

    def head_all(r):
        g = s.hown[r, :]
        for d in (1, 3, 2):
            g = g + s.hyrecv[other(y, d, NY), r, :].astype(F32)
        return g

    def head_far(i):
        s.hzsend[rows(i), :] = head_all(rows(i, oz * ZROWS)).astype(BF)

    each(ZROWS // 16, head_far)
    hz_copy = copy(s.hzsend, s.hzrecv, "hz", 0, 0, far)
    hz_copy.start()

    def head_near(i):
        r = rows(i, zh * ZROWS)
        s.hown[r, :] = head_all(r)

    each(ZROWS // 16, head_near)
    hz_copy.wait_recv()

    def head_last(i):
        v = s.hown[rows(i, zh * ZROWS), :] + s.hzrecv[rows(i), :].astype(F32)
        s.hx[rows(i), :] = v.astype(BF)

    each(ZROWS // 16, head_last)

    def window(xx, cc):
        return pl.ds(pl.multiple_of((xx * NC + cc) * 16, 16), FIN)

    def fin_copy(xx, cc):
        at = xx * NC + cc
        return copy(s.hx.at[window(xx, cc)], s.fin.at[core, x], "fin", at, core * NX + x, dev(xx=xx, cc=cc))

    others = [(other(x, d, NX), c) for d in range(NX) for c in (core, oc)][1:]
    for xx, cc in others:
        fin_copy(xx, cc).start()
    s.fin[core, x] = s.hx[window(x, core), :]
    for xx, cc in others:
        copy(s.fin.at[cc, xx], s.fin.at[cc, xx], "fin", 0, cc * NX + xx, twin).wait_recv()

    skip = lax.rem(FIN - 2 * (x * NC + core), FIN)

    def last(head):
        v = s.fin[head, 0].astype(F32)
        for xx in range(1, NX):
            v = v + s.fin[head, xx].astype(F32)
        return pltpu.roll(v, skip, 0)

    g_ih[...] = last(0)[:LAST, :]
    g_th[...] = jnp.transpose(last(1))[:, :LAST]

    for c in (t_copy, u_copy, ih_copy, text_z, iz_copy, dots_copy, z_copy, tw_copy, sw_copy, g_copy, hc_copy, hz_copy):
        c.wait_send()
    for d in range(1, 4):
        text_y(d).wait_send()
        text_y2(d).wait_send()
        image_copy(d, x, twin).wait_send()
        image_back(d, other(x, d, NX), twin).wait_send()
        text_back_y(d, other(y, d, NY), twin).wait_send()
        head_y(d, twin).wait_send()
    for k in range(NY):
        text_c(k, y).wait_send()
        text_back_c(other(y, k, NY)).wait_send()
    for xx, cc in others:
        fin_copy(xx, cc).wait_send()


def per_device(img_feat, img_head, txt_feat, txt_head):
    vmem = pl.BlockSpec(memory_space=pltpu.VMEM)
    return pl.pallas_call(
        kernel,
        out_shape=(
            jax.ShapeDtypeStruct((PAIRS, HALF), F32),
            jax.ShapeDtypeStruct((LAST, HALF), F32),
            jax.ShapeDtypeStruct((PAIRS, HALF), F32),
            jax.ShapeDtypeStruct((HALF, LAST), F32),
        ),
        in_specs=[vmem] * 4,
        out_specs=(vmem,) * 4,
        scratch_shapes=[pltpu.VMEM(shape, kind) for shape, kind in SCRATCH.values()]
        + [pltpu.SemaphoreType.DMA((total_sends,)), pltpu.SemaphoreType.DMA((total_recvs,))],
        compiler_params=pltpu.CompilerParams(
            collective_id=0, has_side_effects=True, vmem_limit_bytes=60 * 1024 * 1024
        ),
        cost_estimate=pl.CostEstimate(flops=14 * 10**9, bytes_accessed=5 * 10**6, transcendentals=0),
    )(img_feat, img_head, txt_feat, txt_head)


def solution(mesh):
    in_specs = (P("dp", None), P(None, "mp"), P("dp", None), P("mp", None))
    out_specs = (P("dp", "mp"), P("dp", "mp"), P("dp", "mp"), P("mp", "dp"))
    return jax.shard_map(
        per_device, mesh=mesh, in_specs=in_specs, out_specs=out_specs, check_vma=False
    )
```

```python
import types

import jax
import jax.numpy as jnp
from jax import lax
from jax.experimental import pallas as pl
from jax.experimental.pallas import tpu as pltpu
from jax.sharding import PartitionSpec as P

LOGIT_SCALE = 10.0
LOGIT_BIAS = -2.5
NORM_EPS = 1e-06

NX = 4
NY = 4
NZ = 2
NC = 2
D = 1152
HALF = D // 2
PAIRS = 208
OWN = PAIRS // 2
WIN = 112
STEP = PAIRS - WIN
TC = NZ * WIN
IMGS = NX * PAIRS
YROWS = D // NY
ZROWS = YROWS // NZ
LAST = ZROWS // (NX * NC)
FIN = 32

NN = ((1,), (0,))
NT = ((1,), (1,))
TN = ((0,), (0,))
BF = jnp.bfloat16
F32 = jnp.float32

SCRATCH = {
    "tf": ((PAIRS, D), BF),
    "th": ((HALF, D), BF),
    "imf": ((PAIRS, D), BF),
    "iht": ((HALF, D), BF),
    "nhf": ((PAIRS, HALF), F32),
    "nhb": ((PAIRS, HALF), BF),
    "rs": ((PAIRS, 128), F32),
    "tpart": ((PAIRS, D), F32),
    "tsend": ((WIN, D), BF),
    "trecv": ((WIN, D), BF),
    "u": ((2, 8, D), F32),
    "tproj": ((WIN, D), F32),
    "tsc": ((WIN, 128), F32),
    "imh": ((NX, 2, PAIRS, HALF), BF),
    "isc": ((PAIRS, 128), F32),
    "img": ((IMGS, D), BF),
    "txt": ((NY, NC, TC, D), BF),
    "w": ((NY, NC, IMGS, TC), BF),
    "gi": ((IMGS, D), F32),
    "xsend": ((3, PAIRS, D), BF),
    "xa": ((WIN, D), BF),
    "xb": ((STEP, D), BF),
    "xr": ((2, PAIRS, D), BF),
    "gtcsend": ((NY, TC, D), BF),
    "gtcrecv": ((NY, TC, D), BF),
    "gt": ((NY, TC, D), F32),
    "ysend": ((3, TC, D), BF),
    "ya": ((WIN, D), BF),
    "yb": ((WIN, D), BF),
    "yr": ((2, TC, D), BF),
    "zsend": ((WIN, D), BF),
    "zrecv": ((WIN, D), BF),
    "gown": ((WIN, D), F32),
    "tw": ((2, WIN, D), BF),
    "sw": ((2, WIN, 128), F32),
    "tpg": ((PAIRS, D), BF),
    "sec": ((PAIRS, 128), F32),
    "ghalf": ((PAIRS, HALF), F32),
    "izsend": ((PAIRS, HALF), BF),
    "izrecv": ((PAIRS, HALF), BF),
    "dots": ((2, PAIRS, 128), F32),
    "pg": ((PAIRS, HALF), BF),
    "gip": ((PAIRS, D), F32),
    "gsend": ((PAIRS, HALF), BF),
    "grecv": ((PAIRS, HALF), BF),
    "hs": ((NC, D, HALF), BF),
    "hcrecv": ((D, HALF), BF),
    "hysend": ((3, YROWS, HALF), BF),
    "ha": ((ZROWS, HALF), BF),
    "hb": ((ZROWS, HALF), BF),
    "hr": ((2, YROWS, HALF), BF),
    "hown": ((YROWS, HALF), F32),
    "hzsend": ((ZROWS, HALF), BF),
    "hzrecv": ((ZROWS, HALF), BF),
    "hx": ((ZROWS, HALF), BF),
    "fin": ((NC, NX, FIN, HALF), BF),
}

GROUPS = (
    ("t", 1), ("u", 1), ("img", NX * 2), ("txt", NY * NZ), ("txtc", NY), ("xa", 1), ("xb", 1), ("xr", 2),
    ("iz", 1), ("dots", 1), ("gtc", NY), ("ya", 1), ("yb", 1), ("yr", 2), ("z", 1), ("tw", 1), ("sw", 1),
    ("g", 1), ("hc", 1), ("ha", 1), ("hb", 1), ("hr", 2), ("hz", 1), ("fin", NX * NC),
)
RECVS = {}
total_recvs = 0
for group, many in GROUPS:
    RECVS[group] = total_recvs
    total_recvs += many
total_sends = 80


def dot(a, b, dims):
    return lax.dot_general(a, b, (dims, ((), ())), preferred_element_type=F32)


def rows(i, first=0):
    return pl.ds(pl.multiple_of(first + i * 16, 16), 16)


def rowsum(v):
    return jnp.sum(v, -1, keepdims=True)


def wide(v):
    return jnp.broadcast_to(v, (v.shape[0], 128))


def each(count, body):
    lax.fori_loop(0, count, lambda i, c: (body(i), c)[1], 0)


def kernel(img_feat, img_head_t, txt_feat, txt_head, g_img, g_ih, g_txt, g_th, *scratch):
    s = types.SimpleNamespace(**dict(zip(SCRATCH, scratch)))
    ssem, rsem, lsem = scratch[len(SCRATCH) :]
    dp, m = lax.axis_index("dp"), lax.axis_index("mp")
    core = lax.rem(dp, NC)
    x = lax.rem(dp // NC, NX)
    zh = lax.rem(dp // (NC * NX), NZ)
    y = dp // (NC * NX * NZ)
    om, oc, oz = 1 - m, 1 - core, 1 - zh

    loads = [
        pltpu.make_async_copy(src, dst, lsem.at[at])
        for at, (src, dst) in enumerate(
            ((txt_feat, s.tf), (txt_head, s.th), (img_feat, s.imf), (img_head_t, s.iht))
        )
    ]
    for load in loads:
        load.start()

    def dev(yy=None, zz=None, xx=None, cc=None, mm=None):
        yy = y if yy is None else yy
        zz = zh if zz is None else zz
        xx = x if xx is None else xx
        cc = core if cc is None else cc
        mm = m if mm is None else mm
        return (((yy * NZ + zz) * NX + xx) * NC + cc, mm)

    def other(base, by, size):
        return lax.rem(base + by, size)

    x1, x2, x3 = (other(x, d, NX) for d in (1, 2, 3))
    y1, y2, y3 = (other(y, d, NY) for d in (1, 2, 3))
    mate, twin, far = dev(mm=om), dev(cc=oc), dev(zz=oz, mm=om)
    xup, xdown, yup, ydown = dev(xx=x1), dev(xx=x3), dev(yy=y1), dev(yy=y3)

    used = [0]
    sent = []

    def copy(src, dst, group, at, to):
        used[0] += 1
        return pltpu.make_async_remote_copy(
            src_ref=src,
            dst_ref=dst,
            send_sem=ssem.at[used[0] - 1],
            recv_sem=rsem.at[RECVS[group] + at],
            device_id=to,
            device_id_type=pl.DeviceIdType.MESH,
        )

    def send(c):
        c.start()
        sent.append(c)
        return c

    def arrived(ref, group, at=0):
        pltpu.make_async_remote_copy(
            src_ref=ref,
            dst_ref=ref,
            send_sem=ssem.at[0],
            recv_sem=rsem.at[RECVS[group] + at],
            device_id=twin,
            device_id_type=pl.DeviceIdType.MESH,
        ).wait_recv()

    def pick(whole, which):
        return jnp.where(which == 0, whole[:, :HALF], whole[:, HALF:])

    barrier = pltpu.get_barrier_semaphore()
    friends = [mate, twin, far, dev(zz=oz), xup, xdown, yup, ydown]
    friends += [dev(xx=x2)] + [dev(xx=xx, cc=oc) for xx in (x1, x2, x3)]
    for friend in friends:
        pl.semaphore_signal(barrier, inc=1, device_id=friend, device_id_type=pl.DeviceIdType.MESH)

    loads[0].wait()

    def norm(i):
        r = rows(i)
        t = s.tf[r, :].astype(F32)
        c = t - rowsum(t) * (1.0 / D)
        rs = lax.rsqrt(rowsum(c * c) * (1.0 / D) + NORM_EPS)
        half = pick(c * rs, m)
        s.nhf[r, :] = half
        s.nhb[r, :] = half.astype(BF)
        s.rs[r, :] = wide(rs)

    each(PAIRS // 16, norm)
    loads[1].wait()
    s.tpart[...] = dot(s.nhb[...], s.th[...], NN)

    def tosend(i):
        s.tsend[rows(i), :] = s.tpart[rows(i, om * STEP), :].astype(BF)

    each(WIN // 16, tosend)
    pl.semaphore_wait(barrier, len(friends))
    send(copy(s.tsend, s.trecv, "t", 0, mate))

    loads[2].wait()
    loads[3].wait()
    s.imh[x, m] = dot(s.imf[...], s.iht[...], NT).astype(BF)

    def send_image(xx, half, to):
        send(copy(s.imh.at[xx, half], s.imh.at[xx, half], "img", xx * 2 + half, to))

    def image_arrived(xx, half):
        arrived(s.imh.at[xx, half], "img", xx * 2 + half)

    for to in (mate, xup, xdown):
        send_image(x, m, to)
    s.u[m] = dot(jnp.ones((8, HALF), BF), s.th[...], NN)
    send(copy(s.u.at[m], s.u.at[m], "u", 0, mate))

    arrived(s.trecv, "t")

    def embed_text(i):
        p = s.tpart[rows(i, m * STEP), :] + s.trecv[rows(i), :].astype(F32)
        sc = lax.rsqrt(rowsum(p * p) + NORM_EPS)
        row = m * STEP + i * 16 + lax.broadcasted_iota(jnp.int32, (16, 1), 0)
        mine = (row >= m * OWN) & (row < m * OWN + OWN)
        s.tproj[rows(i), :] = p
        s.tsc[rows(i), :] = wide(sc)
        s.txt[y, core, rows(i, zh * WIN), :] = jnp.where(mine, p * sc, 0.0).astype(BF)

    each(WIN // 16, embed_text)

    def part(yy, zz):
        return s.txt.at[yy, core, pl.ds(pl.multiple_of(zz * WIN, 16), WIN)]

    def send_text(yy, zz, to):
        send(copy(part(yy, zz), part(yy, zz), "txt", yy * NZ + zz, to))

    def text_arrived(yy, zz):
        arrived(part(yy, zz), "txt", yy * NZ + zz)

    def send_twin(yy):
        send(copy(s.txt.at[yy, core], s.txt.at[yy, core], "txtc", yy, twin))

    def twin_arrived(yy):
        arrived(s.txt.at[yy, oc], "txtc", yy)

    for to in (far, yup, ydown):
        send_text(y, zh, to)

    image_arrived(x, om)
    send_image(x, om, xup)
    send_image(x, om, xdown)

    def embed_images(xx, own=False):
        def embed(i):
            r = rows(i)
            p = jnp.concatenate([s.imh[xx, 0, r, :].astype(F32), s.imh[xx, 1, r, :].astype(F32)], axis=1)
            sc = lax.rsqrt(rowsum(p * p) + NORM_EPS)
            if own:
                s.isc[r, :] = wide(sc)
            s.img[rows(i, xx * PAIRS), :] = (p * sc).astype(BF)

        each(PAIRS // 16, embed)

    embed_images(x, own=True)

    def images(xx):
        return pl.ds(pl.multiple_of(xx * PAIRS, 16), PAIRS)

    def zero(i):
        s.gi[rows(i), :] = jnp.zeros((16, D), F32)

    each(IMGS // 16, zero)
    text_arrived(y, oz)
    send_text(y, oz, yup)
    send_text(y, oz, ydown)
    send_twin(y)

    def order(k):
        return k + k // 2 - 2 * (k // 3)

    def unit(k, h, j, own=False):
        yy, cc, xx = other(y, order(k), NY), other(core, h, NC), other(x, order(j), NX)
        texts = s.txt[yy, cc]
        scores = dot(s.img[images(xx), :], texts, NT)
        weights = 0.5 + 0.5 * jnp.tanh((0.5 * LOGIT_SCALE) * scores + 0.5 * LOGIT_BIAS)
        if own:
            row = lax.broadcasted_iota(jnp.int32, (PAIRS, TC), 0)
            col = lax.broadcasted_iota(jnp.int32, (PAIRS, TC), 1)
            match = (row - col == m * STEP - zh * WIN) & (col >= zh * WIN) & (col < zh * WIN + WIN)
            weights = weights - match.astype(F32)
        weights = weights.astype(BF)
        s.w[yy, cc, images(xx), :] = weights
        s.gi[images(xx), :] += dot(weights, texts, NN)

    def grads(yy, cc):
        return dot(s.w[yy, cc], s.img[...], TN)

    unit(0, 0, 0, own=True)
    image_arrived(x1, 0)
    send_image(x1, 0, xdown)
    image_arrived(x3, 1)
    send_image(x3, 1, xup)
    twin_arrived(y)
    unit(0, 1, 0)
    image_arrived(x1, 1)
    image_arrived(x3, 0)
    embed_images(x1)
    embed_images(x3)
    each(4, lambda i: unit(0, lax.rem(i, 2), 1 + i // 2))
    text_arrived(y1, 0)
    send_text(y1, 0, ydown)
    text_arrived(y3, 1)
    send_text(y3, 1, yup)
    text_arrived(y1, 1)
    send_twin(y1)
    text_arrived(y3, 0)
    send_twin(y3)
    each(6, lambda i: unit(1 + i // 3, 0, lax.rem(i, 3)))
    twin_arrived(y1)
    twin_arrived(y3)
    each(6, lambda i: unit(1 + i // 3, 1, lax.rem(i, 3)))
    image_arrived(x2, 0)
    image_arrived(x2, 1)
    embed_images(x2)
    each(6, lambda i: unit(i // 2, lax.rem(i, 2), 3))

    def send_back_twin(yy):
        send(copy(s.gtcsend.at[yy], s.gtcrecv.at[yy], "gtc", yy, twin))

    def back_twin_arrived(yy):
        arrived(s.gtcrecv.at[yy], "gtc", yy)

    def text_grad(k):
        yy = other(y, order(k), NY)
        s.gtcsend[yy] = grads(yy, oc).astype(BF)
        s.gt[yy] = grads(yy, core)

    each(3, text_grad)
    for yy in (y1, y3, y):
        send_back_twin(yy)

    text_arrived(y2, 0)
    text_arrived(y2, 1)
    send_twin(y2)
    each(4, lambda i: unit(3, 0, 3 - i))
    twin_arrived(y2)
    unit(3, 1, 3)

    def cast(at, xx, add=None, first=0, count=PAIRS):
        def body(i):
            v = s.gi[rows(i, xx * PAIRS + first), :]
            if add is not None:
                v = v + add[rows(i), :].astype(F32)
            s.xsend[at, rows(i, first), :] = v.astype(BF)

        each(count // 16, body)

    cast(0, x2)
    send(copy(s.xsend.at[0, pl.ds(0, WIN)], s.xa, "xa", 0, xup))
    send(copy(s.xsend.at[0, pl.ds(WIN, STEP)], s.xb, "xb", 0, xdown))
    each(3, lambda i: unit(3, 1, 2 - i))
    cast(1, x1, first=WIN, count=STEP)
    cast(2, x3, first=0, count=WIN)
    s.gtcsend[y2] = grads(y2, oc).astype(BF)
    send_back_twin(y2)
    s.gt[y2] = grads(y2, core)
    back_twin_arrived(y2)

    def cast_y(at, yy, add=None, zz=0):
        def body(i):
            r = rows(i, zz * WIN)
            v = s.gt[yy, r, :] + s.gtcrecv[yy, r, :].astype(F32)
            if add is not None:
                v = v + add[rows(i), :].astype(F32)
            s.ysend[at, r, :] = v.astype(BF)

        each(WIN // 16, body)

    cast_y(0, y2, zz=0)
    send(copy(s.ysend.at[0, pl.ds(0, WIN)], s.ya, "ya", 0, yup))
    cast_y(0, y2, zz=1)
    send(copy(s.ysend.at[0, pl.ds(WIN, WIN)], s.yb, "yb", 0, ydown))
    arrived(s.xa, "xa")
    cast(1, x1, add=s.xa, first=0, count=WIN)
    send(copy(s.xsend.at[1], s.xr.at[0], "xr", 0, xup))
    arrived(s.xb, "xb")
    cast(2, x3, add=s.xb, first=WIN, count=STEP)
    send(copy(s.xsend.at[2], s.xr.at[1], "xr", 1, xdown))
    for yy in (y1, y3, y):
        back_twin_arrived(yy)
    cast_y(1, y1, zz=1)
    cast_y(2, y3, zz=0)
    arrived(s.ya, "ya")
    cast_y(1, y1, add=s.ya, zz=0)
    send(copy(s.ysend.at[1], s.yr.at[0], "yr", 0, yup))
    arrived(s.yb, "yb")
    cast_y(2, y3, add=s.yb, zz=1)
    send(copy(s.ysend.at[2], s.yr.at[1], "yr", 1, ydown))

    arrived(s.xr.at[0], "xr", 0)
    arrived(s.xr.at[1], "xr", 1)

    def projection(r):
        return jnp.concatenate([s.imh[x, 0, r, :].astype(F32), s.imh[x, 1, r, :].astype(F32)], axis=1)

    def image_sum(i):
        r = rows(i)
        g = s.gi[rows(i, x * PAIRS), :] + s.xr[0, r, :].astype(F32) + s.xr[1, r, :].astype(F32)
        g = LOGIT_SCALE * g
        s.dots[m, r, :] = wide(rowsum(g * projection(r)))
        s.ghalf[r, :] = pick(g, m)
        s.izsend[r, :] = pick(g, om).astype(BF)

    each(PAIRS // 16, image_sum)
    send(copy(s.dots.at[m], s.dots.at[m], "dots", 0, mate))
    send(copy(s.izsend, s.izrecv, "iz", 0, mate))

    arrived(s.yr.at[0], "yr", 0)
    arrived(s.yr.at[1], "yr", 1)

    def text_sum(r):
        g = s.gt[y, r, :] + s.gtcrecv[y, r, :].astype(F32)
        return g + s.yr[0, r, :].astype(F32) + s.yr[1, r, :].astype(F32)

    def text_far(i):
        s.zsend[rows(i), :] = text_sum(rows(i, oz * WIN)).astype(BF)

    each(WIN // 16, text_far)
    send(copy(s.zsend, s.zrecv, "z", 0, far))

    def text_near(i):
        s.gown[rows(i), :] = text_sum(rows(i, zh * WIN))

    each(WIN // 16, text_near)

    arrived(s.dots.at[om], "dots")
    arrived(s.izrecv, "iz")

    def image_grad(i):
        r = rows(i)
        g = s.ghalf[r, :] + s.izrecv[r, :].astype(F32)
        sc = s.isc[r, :][:, :1]
        total = (s.dots[0, r, :] + s.dots[1, r, :])[:, :1]
        p = s.imh[x, m, r, :].astype(F32)
        s.pg[r, :] = (sc * g - (sc * sc * sc) * p * total).astype(BF)

    each(PAIRS // 16, image_grad)
    s.gip[...] = dot(s.pg[...], s.iht[...], NN)

    def image_out(i):
        s.gsend[rows(i), :] = pick(s.gip[rows(i), :], om).astype(BF)

    each(PAIRS // 16, image_out)

    arrived(s.zrecv, "z")

    def text_own(i):
        r = rows(i)
        g = LOGIT_SCALE * (s.gown[r, :] + s.zrecv[r, :].astype(F32))
        p = s.tproj[r, :]
        sc = s.tsc[r, :][:, :1]
        v = sc * g - (sc * sc * sc) * p * rowsum(p * g)
        row = m * STEP + i * 16 + lax.broadcasted_iota(jnp.int32, (16, 1), 0)
        mine = (row >= m * OWN) & (row < m * OWN + OWN)
        v = jnp.where(mine, v, 0.0).astype(BF)
        s.tw[m, r, :] = v
        s.sw[m, r, :] = wide(rowsum(v.astype(F32) * p))

    each(WIN // 16, text_own)
    send(copy(s.tw.at[m], s.tw.at[m], "tw", 0, mate))
    send(copy(s.sw.at[m], s.sw.at[m], "sw", 0, mate))
    send(copy(s.gsend, s.grecv, "g", 0, mate))
    s.hs[0] = dot(s.imf[...], s.pg[...], TN).astype(BF)
    arrived(s.tw.at[om], "tw")
    arrived(s.sw.at[om], "sw")
    arrived(s.u.at[om], "u")

    def merge(i):
        lo, hi = jnp.minimum(i, 6), jnp.maximum(i - 6, 0)
        v = jnp.where(i <= 6, s.tw[0, rows(lo), :].astype(F32), 0.0)
        v = v + jnp.where(i >= 6, s.tw[1, rows(hi), :].astype(F32), 0.0)
        s.tpg[rows(i), :] = v.astype(BF)
        v = jnp.where(i <= 6, s.sw[0, rows(lo), :], 0.0)
        s.sec[rows(i), :] = v + jnp.where(i >= 6, s.sw[1, rows(hi), :], 0.0)

    each(PAIRS // 16, merge)
    s.hs[1] = dot(s.tpg[...], s.nhb[...], TN).astype(BF)
    send(copy(s.hs.at[oc], s.hcrecv, "hc", 0, twin))

    g_txt[...] = dot(s.tpg[...], s.th[...], NT)

    def text_input(i):
        r = rows(i)
        u = (s.u[0] + s.u[1])[:1, :]
        first = rowsum(s.tpg[r, :].astype(F32) * u) * (1.0 / D)
        second = s.sec[r, :][:, :1] * (1.0 / D)
        g_txt[r, :] = s.rs[r, :][:, :1] * (g_txt[r, :] - first - s.nhf[r, :] * second)

    each(PAIRS // 16, text_input)

    arrived(s.hcrecv, "hc")

    def head_sum(r):
        return s.hs[core, r, :].astype(F32) + s.hcrecv[r, :].astype(F32)

    def cast_head(at, yy, add=None, zz=0):
        def body(i):
            v = head_sum(rows(i, yy * YROWS + zz * ZROWS))
            if add is not None:
                v = v + add[rows(i), :].astype(F32)
            s.hysend[at, rows(i, zz * ZROWS), :] = v.astype(BF)

        each(ZROWS // 16, body)

    cast_head(0, y2, zz=0)
    send(copy(s.hysend.at[0, pl.ds(0, ZROWS)], s.ha, "ha", 0, yup))
    cast_head(0, y2, zz=1)
    send(copy(s.hysend.at[0, pl.ds(ZROWS, ZROWS)], s.hb, "hb", 0, ydown))
    cast_head(1, y1, zz=1)
    cast_head(2, y3, zz=0)

    def head_own(i):
        s.hown[rows(i), :] = head_sum(rows(i, y * YROWS))

    each(YROWS // 16, head_own)
    arrived(s.ha, "ha")
    cast_head(1, y1, add=s.ha, zz=0)
    send(copy(s.hysend.at[1], s.hr.at[0], "hr", 0, yup))
    arrived(s.hb, "hb")
    cast_head(2, y3, add=s.hb, zz=1)
    send(copy(s.hysend.at[2], s.hr.at[1], "hr", 1, ydown))

    arrived(s.grecv, "g")

    def image_input(i):
        r = rows(i)
        g_img[r, :] = pick(s.gip[r, :], m) + s.grecv[r, :].astype(F32)

    each(PAIRS // 16, image_input)

    arrived(s.hr.at[0], "hr", 0)
    arrived(s.hr.at[1], "hr", 1)

    def head_all(r):
        return s.hown[r, :] + s.hr[0, r, :].astype(F32) + s.hr[1, r, :].astype(F32)

    def head_far(i):
        s.hzsend[rows(i), :] = head_all(rows(i, oz * ZROWS)).astype(BF)

    each(ZROWS // 16, head_far)
    send(copy(s.hzsend, s.hzrecv, "hz", 0, dev(zz=oz)))

    def head_near(i):
        r = rows(i, zh * ZROWS)
        s.hown[r, :] = head_all(r)

    each(ZROWS // 16, head_near)
    arrived(s.hzrecv, "hz")

    def head_last(i):
        v = s.hown[rows(i, zh * ZROWS), :] + s.hzrecv[rows(i), :].astype(F32)
        s.hx[rows(i), :] = v.astype(BF)

    each(ZROWS // 16, head_last)

    def window(xx, cc):
        return pl.ds(pl.multiple_of((xx * NC + cc) * 16, 16), FIN)

    others = [(other(x, d, NX), c) for d in range(NX) for c in (core, oc)][1:]
    for xx, cc in others:
        send(copy(s.hx.at[window(xx, cc)], s.fin.at[core, x], "fin", core * NX + x, dev(xx=xx, cc=cc)))
    s.fin[core, x] = s.hx[window(x, core), :]
    for xx, cc in others:
        arrived(s.fin.at[cc, xx], "fin", cc * NX + xx)

    skip = lax.rem(FIN - 2 * (x * NC + core), FIN)

    def last(head):
        v = s.fin[head, 0].astype(F32)
        for xx in range(1, NX):
            v = v + s.fin[head, xx].astype(F32)
        return pltpu.roll(v, skip, 0)

    g_ih[...] = last(0)[:LAST, :]
    g_th[...] = last(1)[:LAST, :]

    for c in sent:
        c.wait_send()


def per_device(img_feat, img_head, txt_feat, txt_head):
    vmem = pl.BlockSpec(memory_space=pltpu.VMEM)
    g_img, g_ih, g_txt, g_th = pl.pallas_call(
        kernel,
        out_shape=(
            jax.ShapeDtypeStruct((PAIRS, HALF), F32),
            jax.ShapeDtypeStruct((LAST, HALF), F32),
            jax.ShapeDtypeStruct((PAIRS, HALF), F32),
            jax.ShapeDtypeStruct((LAST, HALF), F32),
        ),
        in_specs=[pl.BlockSpec(memory_space=pl.ANY)] * 4,
        out_specs=(vmem,) * 4,
        scratch_shapes=[pltpu.VMEM(shape, kind) for shape, kind in SCRATCH.values()]
        + [pltpu.SemaphoreType.DMA((total_sends,)), pltpu.SemaphoreType.DMA((total_recvs,))]
        + [pltpu.SemaphoreType.DMA((4,))],
        compiler_params=pltpu.CompilerParams(
            collective_id=0, has_side_effects=True, vmem_limit_bytes=60 * 1024 * 1024
        ),
        cost_estimate=pl.CostEstimate(flops=14 * 10**9, bytes_accessed=5 * 10**6, transcendentals=0),
    )(img_feat, img_head.T, txt_feat, txt_head)
    return g_img, g_ih, g_txt, g_th.T


def solution(mesh):
    in_specs = (P("dp", None), P(None, "mp"), P("dp", None), P("mp", None))
    out_specs = (P("dp", "mp"), P("dp", "mp"), P("dp", "mp"), P("mp", "dp"))
    return jax.shard_map(
        per_device, mesh=mesh, in_specs=in_specs, out_specs=out_specs, check_vma=False
    )
```

```python
import types

import jax
import jax.numpy as jnp
from jax import lax
from jax.experimental import pallas as pl
from jax.experimental.pallas import tpu as pltpu
from jax.sharding import PartitionSpec as P

LOGIT_SCALE = 10.0
LOGIT_BIAS = -2.5
NORM_EPS = 1e-06

NX = 4
NY = 4
NZ = 2
NC = 2
D = 1152
HALF = D // 2
PAIRS = 208
OWN = PAIRS // 2
WIN = 112
STEP = PAIRS - WIN
TC = NZ * WIN
IMGS = NX * PAIRS
YROWS = D // NY
ZROWS = YROWS // NZ
LAST = ZROWS // (NX * NC)
XWIN = 48
XHALF = NY * NZ * XWIN // 2
FIN = 32
BLOCK = IMGS // 2

NN = ((1,), (0,))
NT = ((1,), (1,))
TN = ((0,), (0,))
BF = jnp.bfloat16
F32 = jnp.float32

SCRATCH = {
    "tf": ((PAIRS, D), BF),
    "th": ((HALF, D), BF),
    "imf": ((PAIRS, D), BF),
    "iht": ((HALF, D), BF),
    "nhf": ((PAIRS, HALF), F32),
    "nhb": ((PAIRS, HALF), BF),
    "rs": ((PAIRS, 128), F32),
    "tpart": ((PAIRS, D), F32),
    "tsend": ((WIN, D), BF),
    "trecv": ((WIN, D), BF),
    "u": ((2, 8, D), F32),
    "tproj": ((WIN, D), F32),
    "tsc": ((WIN, 128), F32),
    "imh": ((NX, 2, PAIRS, HALF), BF),
    "isc": ((PAIRS, 128), F32),
    "img": ((IMGS, D), BF),
    "txt": ((NY, NC * TC, D), BF),
    "w": ((NY, IMGS, NC * TC), BF),
    "gi": ((IMGS, D), F32),
    "xsend": ((3, PAIRS, D), BF),
    "xa": ((WIN, D), BF),
    "xb": ((STEP, D), BF),
    "xr": ((2, PAIRS, D), BF),
    "gtcsend": ((NY, TC, D), BF),
    "gtcrecv": ((NY, TC, D), BF),
    "gt": ((NY, TC, D), F32),
    "gtall": ((NC * TC, D), F32),
    "ysend": ((3, TC, D), BF),
    "ya": ((WIN, D), BF),
    "yb": ((WIN, D), BF),
    "yr": ((2, TC, D), BF),
    "zsend": ((WIN, D), BF),
    "zrecv": ((WIN, D), BF),
    "gown": ((WIN, D), F32),
    "tw": ((2, WIN, D), BF),
    "sw": ((2, WIN, 128), F32),
    "tpg": ((PAIRS, D), BF),
    "sec": ((PAIRS, 128), F32),
    "ghalf": ((PAIRS, HALF), F32),
    "izsend": ((PAIRS, HALF), BF),
    "izrecv": ((PAIRS, HALF), BF),
    "dots": ((2, PAIRS, 128), F32),
    "pg": ((PAIRS, HALF), BF),
    "gip": ((PAIRS, D), F32),
    "gsend": ((PAIRS, HALF), BF),
    "grecv": ((PAIRS, HALF), BF),
    "imft": ((PAIRS, D), BF),
    "nhbt": ((PAIRS, HALF), BF),
    "pgt": ((PAIRS, HALF), BF),
    "tpgt": ((PAIRS, D), BF),
    "h": ((D, HALF), F32),
    "h1send": ((3, 2, XHALF, HALF), BF),
    "h1ab": ((2, XHALF, HALF), BF),
    "h1r": ((2, 2, XHALF, HALF), BF),
    "h1": ((2 * XHALF, HALF), F32),
    "h2send": ((3, 2, XWIN, HALF), BF),
    "h2ab": ((2, XWIN, HALF), BF),
    "h2r": ((2, 2, XWIN, HALF), BF),
    "h2": ((2 * XWIN, HALF), F32),
    "h3send": ((XWIN, HALF), BF),
    "h3recv": ((XWIN, HALF), BF),
    "h4": ((XWIN, HALF), F32),
    "finr": ((FIN, HALF), F32),
}

GROUPS = (
    ("t", 1), ("u", 1), ("img", NX * 2), ("txt", NY * NZ), ("txtc", NY), ("xa", 1), ("xb", 1), ("xr", 2),
    ("iz", 1), ("dots", 1), ("gtc", NY), ("ya", 1), ("yb", 1), ("yr", 2), ("z", 1), ("tw", 1), ("sw", 1),
    ("g", 1), ("imft", 1), ("nhbt", 1), ("pgt", 1), ("tpgt", 1),
    ("h1ab", 2), ("h1r", 2), ("h2ab", 2), ("h2r", 2), ("h3", 1), ("fin", 1),
)
RECVS = {}
total_recvs = 0
for group, many in GROUPS:
    RECVS[group] = total_recvs
    total_recvs += many
total_sends = 80


def dot(a, b, dims):
    return lax.dot_general(a, b, (dims, ((), ())), preferred_element_type=F32)


def rows(i, first=0):
    return pl.ds(pl.multiple_of(first + i * 16, 16), 16)


def rowsum(v):
    return jnp.sum(v, -1, keepdims=True)


def wide(v):
    return jnp.broadcast_to(v, (v.shape[0], 128))


def each(count, body):
    lax.fori_loop(0, count, lambda i, c: (body(i), c)[1], 0)


def kernel(img_feat, img_head_t, txt_feat, txt_head, g_img, g_ih, g_txt, g_th, *scratch):
    s = types.SimpleNamespace(**dict(zip(SCRATCH, scratch)))
    ssem, rsem, lsem = scratch[len(SCRATCH) :]
    dp, m = lax.axis_index("dp"), lax.axis_index("mp")
    core = lax.rem(dp, NC)
    x = lax.rem(dp // NC, NX)
    zh = lax.rem(dp // (NC * NX), NZ)
    y = dp // (NC * NX * NZ)
    om, oc, oz = 1 - m, 1 - core, 1 - zh

    loads = [
        pltpu.make_async_copy(src, dst, lsem.at[at])
        for at, (src, dst) in enumerate(
            ((txt_feat, s.tf), (txt_head, s.th), (img_feat, s.imf), (img_head_t, s.iht))
        )
    ]
    for load in loads:
        load.start()

    def dev(yy=None, zz=None, xx=None, cc=None, mm=None):
        yy = y if yy is None else yy
        zz = zh if zz is None else zz
        xx = x if xx is None else xx
        cc = core if cc is None else cc
        mm = m if mm is None else mm
        return (((yy * NZ + zz) * NX + xx) * NC + cc, mm)

    def other(base, by, size):
        return lax.rem(base + by, size)

    x1, x2, x3 = (other(x, d, NX) for d in (1, 2, 3))
    y1, y2, y3 = (other(y, d, NY) for d in (1, 2, 3))
    mate, twin, far = dev(mm=om), dev(cc=oc), dev(zz=oz, mm=om)
    xup, xdown, yup, ydown = dev(xx=x1), dev(xx=x3), dev(yy=y1), dev(yy=y3)

    used = [0]
    sent = []

    def copy(src, dst, group, at, to):
        used[0] += 1
        return pltpu.make_async_remote_copy(
            src_ref=src,
            dst_ref=dst,
            send_sem=ssem.at[used[0] - 1],
            recv_sem=rsem.at[RECVS[group] + at],
            device_id=to,
            device_id_type=pl.DeviceIdType.MESH,
        )

    def send(c):
        c.start()
        sent.append(c)
        return c

    def arrived(ref, group, at=0):
        pltpu.make_async_remote_copy(
            src_ref=ref,
            dst_ref=ref,
            send_sem=ssem.at[0],
            recv_sem=rsem.at[RECVS[group] + at],
            device_id=twin,
            device_id_type=pl.DeviceIdType.MESH,
        ).wait_recv()

    def pick(whole, which):
        return jnp.where(which == 0, whole[:, :HALF], whole[:, HALF:])

    barrier = pltpu.get_barrier_semaphore()
    friends = [mate, twin, far, dev(zz=oz), xup, xdown, yup, ydown]
    for friend in friends:
        pl.semaphore_signal(barrier, inc=1, device_id=friend, device_id_type=pl.DeviceIdType.MESH)

    loads[0].wait()

    def norm(i):
        r = rows(i)
        t = s.tf[r, :].astype(F32)
        c = t - rowsum(t) * (1.0 / D)
        rs = lax.rsqrt(rowsum(c * c) * (1.0 / D) + NORM_EPS)
        half = pick(c * rs, m)
        s.nhf[r, :] = half
        s.nhb[r, :] = half.astype(BF)
        s.rs[r, :] = wide(rs)

    each(PAIRS // 16, norm)
    loads[1].wait()
    s.tpart[...] = dot(s.nhb[...], s.th[...], NN)

    def tosend(i):
        s.tsend[rows(i), :] = s.tpart[rows(i, om * STEP), :].astype(BF)

    each(WIN // 16, tosend)
    pl.semaphore_wait(barrier, len(friends))
    send(copy(s.tsend, s.trecv, "t", 0, mate))

    loads[2].wait()
    loads[3].wait()
    s.imh[x, m] = dot(s.imf[...], s.iht[...], NT).astype(BF)

    def send_image(xx, half, to):
        send(copy(s.imh.at[xx, half], s.imh.at[xx, half], "img", xx * 2 + half, to))

    def image_arrived(xx, half):
        arrived(s.imh.at[xx, half], "img", xx * 2 + half)

    for to in (mate, xup, xdown):
        send_image(x, m, to)
    s.u[m] = dot(jnp.ones((8, HALF), BF), s.th[...], NN)
    send(copy(s.u.at[m], s.u.at[m], "u", 0, mate))

    nhb_copy = copy(s.nhb, s.nhbt, "nhbt", 0, twin)
    imf_copy = copy(s.imf, s.imft, "imft", 0, twin)
    pg_copy = copy(s.pg, s.pgt, "pgt", 0, twin)
    tpg_copy = copy(s.tpg, s.tpgt, "tpgt", 0, twin)

    @pl.when(core == 0)
    def _():
        nhb_copy.start()

    @pl.when(core == 1)
    def _():
        imf_copy.start()

    arrived(s.trecv, "t")

    def embed_text(i):
        p = s.tpart[rows(i, m * STEP), :] + s.trecv[rows(i), :].astype(F32)
        sc = lax.rsqrt(rowsum(p * p) + NORM_EPS)
        row = m * STEP + i * 16 + lax.broadcasted_iota(jnp.int32, (16, 1), 0)
        mine = (row >= m * OWN) & (row < m * OWN + OWN)
        s.tproj[rows(i), :] = p
        s.tsc[rows(i), :] = wide(sc)
        s.txt[y, rows(i, core * TC + zh * WIN), :] = jnp.where(mine, p * sc, 0.0).astype(BF)

    each(WIN // 16, embed_text)

    def part(yy, zz):
        return s.txt.at[yy, pl.ds(pl.multiple_of(core * TC + zz * WIN, 16), WIN)]

    def side(yy, cc):
        return s.txt.at[yy, pl.ds(pl.multiple_of(cc * TC, 16), TC)]

    def send_text(yy, zz, to):
        send(copy(part(yy, zz), part(yy, zz), "txt", yy * NZ + zz, to))

    def text_arrived(yy, zz):
        arrived(part(yy, zz), "txt", yy * NZ + zz)

    def send_twin(yy):
        send(copy(side(yy, core), side(yy, core), "txtc", yy, twin))

    def twin_arrived(yy):
        arrived(side(yy, oc), "txtc", yy)

    for to in (far, yup, ydown):
        send_text(y, zh, to)

    image_arrived(x, om)
    send_image(x, om, xup)
    send_image(x, om, xdown)

    def embed_images(xx, at, own=False):
        def embed(i):
            r = rows(i)
            p = jnp.concatenate([s.imh[xx, 0, r, :].astype(F32), s.imh[xx, 1, r, :].astype(F32)], axis=1)
            sc = lax.rsqrt(rowsum(p * p) + NORM_EPS)
            if own:
                s.isc[r, :] = wide(sc)
            s.img[rows(i, at * PAIRS), :] = (p * sc).astype(BF)

        each(PAIRS // 16, embed)

    embed_images(x, 0, own=True)

    def zero(i):
        s.gi[rows(i), :] = jnp.zeros((16, D), F32)

    each(IMGS // 16, zero)
    text_arrived(y, oz)
    send_text(y, oz, yup)
    send_text(y, oz, ydown)
    send_twin(y)

    def unit(yy, half, own=False):
        r = pl.ds(pl.multiple_of(half * BLOCK, 16), BLOCK)
        texts = s.txt[yy]
        scores = dot(s.img[r, :], texts, NT)
        weights = 0.5 + 0.5 * jnp.tanh((0.5 * LOGIT_SCALE) * scores + 0.5 * LOGIT_BIAS)
        if own:
            row = lax.broadcasted_iota(jnp.int32, (BLOCK, NC * TC), 0)
            col = lax.broadcasted_iota(jnp.int32, (BLOCK, NC * TC), 1)
            first = core * TC + zh * WIN
            match = (row - col == m * STEP - first) & (col >= first) & (col < first + WIN)
            weights = weights - match.astype(F32)
        weights = weights.astype(BF)
        s.w[yy, r, :] = weights
        s.gi[r, :] += dot(weights, texts, NN)

    image_arrived(x1, 0)
    send_image(x1, 0, xdown)
    image_arrived(x3, 1)
    send_image(x3, 1, xup)
    image_arrived(x1, 1)
    embed_images(x1, 1)
    twin_arrived(y)
    unit(y, 0, own=True)
    image_arrived(x3, 0)
    embed_images(x3, 2)
    text_arrived(y1, 0)
    send_text(y1, 0, ydown)
    text_arrived(y3, 1)
    send_text(y3, 1, yup)
    text_arrived(y1, 1)
    send_twin(y1)
    text_arrived(y3, 0)
    send_twin(y3)
    image_arrived(x2, 0)
    image_arrived(x2, 1)
    embed_images(x2, 3)
    unit(y, 1)
    twin_arrived(y1)
    twin_arrived(y3)
    each(4, lambda i: unit(other(y, 1 + i // 2 * 2, NY), lax.rem(i, 2)))

    text_arrived(y2, 0)
    text_arrived(y2, 1)
    send_twin(y2)
    twin_arrived(y2)
    unit(y2, 1)

    def cast(at, place, add=None, first=0, count=PAIRS):
        def body(i):
            v = s.gi[rows(i, place * PAIRS + first), :]
            if add is not None:
                v = v + add[rows(i), :].astype(F32)
            s.xsend[at, rows(i, first), :] = v.astype(BF)

        each(count // 16, body)

    cast(0, 3)
    send(copy(s.xsend.at[0, pl.ds(0, WIN)], s.xa, "xa", 0, xup))
    send(copy(s.xsend.at[0, pl.ds(WIN, STEP)], s.xb, "xb", 0, xdown))
    unit(y2, 0)

    def text_grad(yy):
        s.gtall[...] = dot(s.w[yy], s.img[...], TN)

        def out(i):
            s.gtcsend[yy, rows(i), :] = s.gtall[rows(i, oc * TC), :].astype(BF)
            s.gt[yy, rows(i), :] = s.gtall[rows(i, core * TC), :]

        each(TC // 16, out)

    def send_back_twin(yy):
        send(copy(s.gtcsend.at[yy], s.gtcrecv.at[yy], "gtc", yy, twin))

    def back_twin_arrived(yy):
        arrived(s.gtcrecv.at[yy], "gtc", yy)

    text_grad(y2)
    send_back_twin(y2)
    text_grad(y1)
    send_back_twin(y1)
    back_twin_arrived(y2)

    def cast_y(at, yy, add=None, zz=0):
        def body(i):
            r = rows(i, zz * WIN)
            v = s.gt[yy, r, :] + s.gtcrecv[yy, r, :].astype(F32)
            if add is not None:
                v = v + add[rows(i), :].astype(F32)
            s.ysend[at, r, :] = v.astype(BF)

        each(WIN // 16, body)

    cast_y(0, y2, zz=0)
    send(copy(s.ysend.at[0, pl.ds(0, WIN)], s.ya, "ya", 0, yup))
    cast_y(0, y2, zz=1)
    send(copy(s.ysend.at[0, pl.ds(WIN, WIN)], s.yb, "yb", 0, ydown))
    cast(1, 1, first=WIN, count=STEP)
    cast(2, 2, first=0, count=WIN)
    arrived(s.xa, "xa")
    cast(1, 1, add=s.xa, first=0, count=WIN)
    send(copy(s.xsend.at[1], s.xr.at[0], "xr", 0, xup))
    arrived(s.xb, "xb")
    cast(2, 2, add=s.xb, first=WIN, count=STEP)
    send(copy(s.xsend.at[2], s.xr.at[1], "xr", 1, xdown))

    def rest(k):
        text_grad(other(y, 3 + k, NY))

    each(2, rest)
    send_back_twin(y3)
    send_back_twin(y)
    back_twin_arrived(y1)
    cast_y(1, y1, zz=1)
    arrived(s.ya, "ya")
    cast_y(1, y1, add=s.ya, zz=0)
    send(copy(s.ysend.at[1], s.yr.at[0], "yr", 0, yup))
    back_twin_arrived(y3)
    cast_y(2, y3, zz=0)
    arrived(s.yb, "yb")
    cast_y(2, y3, add=s.yb, zz=1)
    send(copy(s.ysend.at[2], s.yr.at[1], "yr", 1, ydown))
    back_twin_arrived(y)

    arrived(s.xr.at[0], "xr", 0)
    arrived(s.xr.at[1], "xr", 1)

    def projection(r):
        return jnp.concatenate([s.imh[x, 0, r, :].astype(F32), s.imh[x, 1, r, :].astype(F32)], axis=1)

    def image_sum(i):
        r = rows(i)
        g = s.gi[rows(i), :] + s.xr[0, r, :].astype(F32) + s.xr[1, r, :].astype(F32)
        g = LOGIT_SCALE * g
        s.dots[m, r, :] = wide(rowsum(g * projection(r)))
        s.ghalf[r, :] = pick(g, m)
        s.izsend[r, :] = pick(g, om).astype(BF)

    each(PAIRS // 16, image_sum)
    send(copy(s.dots.at[m], s.dots.at[m], "dots", 0, mate))
    send(copy(s.izsend, s.izrecv, "iz", 0, mate))

    arrived(s.yr.at[0], "yr", 0)
    arrived(s.yr.at[1], "yr", 1)

    def text_sum(r):
        g = s.gt[y, r, :] + s.gtcrecv[y, r, :].astype(F32)
        return g + s.yr[0, r, :].astype(F32) + s.yr[1, r, :].astype(F32)

    def text_far(i):
        s.zsend[rows(i), :] = text_sum(rows(i, oz * WIN)).astype(BF)

    each(WIN // 16, text_far)
    send(copy(s.zsend, s.zrecv, "z", 0, far))

    def text_near(i):
        s.gown[rows(i), :] = text_sum(rows(i, zh * WIN))

    each(WIN // 16, text_near)

    arrived(s.dots.at[om], "dots")
    arrived(s.izrecv, "iz")

    def image_grad(i):
        r = rows(i)
        g = s.ghalf[r, :] + s.izrecv[r, :].astype(F32)
        sc = s.isc[r, :][:, :1]
        total = (s.dots[0, r, :] + s.dots[1, r, :])[:, :1]
        p = s.imh[x, m, r, :].astype(F32)
        s.pg[r, :] = (sc * g - (sc * sc * sc) * p * total).astype(BF)

    each(PAIRS // 16, image_grad)

    @pl.when(core == 1)
    def _():
        pg_copy.start()

    s.gip[...] = dot(s.pg[...], s.iht[...], NN)

    def image_out(i):
        s.gsend[rows(i), :] = pick(s.gip[rows(i), :], om).astype(BF)

    each(PAIRS // 16, image_out)

    arrived(s.zrecv, "z")

    def text_own(i):
        r = rows(i)
        g = LOGIT_SCALE * (s.gown[r, :] + s.zrecv[r, :].astype(F32))
        p = s.tproj[r, :]
        sc = s.tsc[r, :][:, :1]
        v = sc * g - (sc * sc * sc) * p * rowsum(p * g)
        row = m * STEP + i * 16 + lax.broadcasted_iota(jnp.int32, (16, 1), 0)
        mine = (row >= m * OWN) & (row < m * OWN + OWN)
        v = jnp.where(mine, v, 0.0).astype(BF)
        s.tw[m, r, :] = v
        s.sw[m, r, :] = wide(rowsum(v.astype(F32) * p))

    each(WIN // 16, text_own)
    send(copy(s.tw.at[m], s.tw.at[m], "tw", 0, mate))
    send(copy(s.sw.at[m], s.sw.at[m], "sw", 0, mate))
    send(copy(s.gsend, s.grecv, "g", 0, mate))

    class Ring:
        def __init__(self, load, count, bufs, groups, up, down, chunks):
            self.load, self.count, self.chunks = load, count, chunks
            self.out, self.ab, self.back = bufs
            self.groups = groups
            self.used = pl.ds(0, count * 16)
            n = self.used
            self.copies = [
                copy(self.out.at[0, 0, n], self.ab.at[0, n], groups[0], 0, up),
                copy(self.out.at[0, 1, n], self.ab.at[1, n], groups[0], 1, down),
                copy(self.out.at[1, :, n], self.back.at[0, :, n], groups[1], 0, up),
                copy(self.out.at[2, :, n], self.back.at[1, :, n], groups[1], 1, down),
            ]

        def cast(self, at, chunk, half, add=None):
            def body(i):
                v = self.load(chunk, half, i)
                if add is not None:
                    v = v + self.ab[add, rows(i), :].astype(F32)
                self.out[at, half, rows(i), :] = v.astype(BF)

            each(self.count, body)

        def begin(self):
            for half in (0, 1):
                self.cast(0, self.chunks[2], half)
                self.copies[half].start()

        def finish(self, store):
            self.cast(1, self.chunks[1], 1)
            self.cast(2, self.chunks[3], 0)
            arrived(self.ab.at[0, self.used], self.groups[0], 0)
            self.cast(1, self.chunks[1], 0, add=0)
            self.copies[2].start()
            arrived(self.ab.at[1, self.used], self.groups[0], 1)
            self.cast(2, self.chunks[3], 1, add=1)
            self.copies[3].start()
            arrived(self.back.at[0, :, self.used], self.groups[1], 0)
            arrived(self.back.at[1, :, self.used], self.groups[1], 1)
            for half in (0, 1):

                def total(i, half=half):
                    v = self.load(self.chunks[0], half, i) + self.back[0, half, rows(i), :].astype(F32)
                    store(half, i, v + self.back[1, half, rows(i), :].astype(F32))

                each(self.count, total)
            for c in self.copies:
                c.wait_send()

    def store_first(count):
        def store(half, i, v):
            s.h1[rows(i, half * count * 16), :] = v

        return store

    def store_second(half, i, v):
        s.h2[rows(i, half * XWIN), :] = v

    bufs1, bufs2 = (s.h1send, s.h1ab, s.h1r), (s.h2send, s.h2ab, s.h2r)
    xs, ys = (x, x1, x2, x3), (y, y1, y2, y3)
    tall = ZROWS // 16
    image_first = Ring(
        lambda c, half, i: s.h[rows(i, c * YROWS + half * ZROWS), :],
        tall, bufs1, ("h1ab", "h1r"), yup, ydown, ys,
    )
    image_second = Ring(
        lambda c, half, i: s.h1[rows(i, half * ZROWS + c * 32), :],
        XWIN // 16, bufs2, ("h2ab", "h2r"), xup, xdown, xs,
    )
    text_first = Ring(
        lambda c, half, i: s.h[rows(lax.rem(i, 3), (half * NY + i // 3) * ZROWS + c * 32), :],
        XHALF // 16, bufs1, ("h1ab", "h1r"), xup, xdown, xs,
    )
    text_second = Ring(
        lambda c, half, i: s.h1[rows(i, (c * NZ + half) * XWIN), :],
        XWIN // 16, bufs2, ("h2ab", "h2r"), yup, ydown, ys,
    )

    @pl.when(core == 0)
    def _():
        arrived(s.imft, "imft")
        arrived(s.pgt, "pgt")
        s.h[...] = dot(s.imf[...], s.pg[...], TN) + dot(s.imft[...], s.pgt[...], TN)
        image_first.begin()

    arrived(s.tw.at[om], "tw")
    arrived(s.sw.at[om], "sw")
    arrived(s.u.at[om], "u")

    def merge(i):
        lo, hi = jnp.minimum(i, 6), jnp.maximum(i - 6, 0)
        v = jnp.where(i <= 6, s.tw[0, rows(lo), :].astype(F32), 0.0)
        v = v + jnp.where(i >= 6, s.tw[1, rows(hi), :].astype(F32), 0.0)
        s.tpg[rows(i), :] = v.astype(BF)
        v = jnp.where(i <= 6, s.sw[0, rows(lo), :], 0.0)
        s.sec[rows(i), :] = v + jnp.where(i >= 6, s.sw[1, rows(hi), :], 0.0)

    each(PAIRS // 16, merge)

    @pl.when(core == 0)
    def _():
        tpg_copy.start()

    @pl.when(core == 1)
    def _():
        arrived(s.nhbt, "nhbt")
        arrived(s.tpgt, "tpgt")
        s.h[...] = dot(s.tpg[...], s.nhb[...], TN) + dot(s.tpgt[...], s.nhbt[...], TN)
        text_first.begin()

    g_txt[...] = dot(s.tpg[...], s.th[...], NT)

    def text_input(i):
        r = rows(i)
        u = (s.u[0] + s.u[1])[:1, :]
        first = rowsum(s.tpg[r, :].astype(F32) * u) * (1.0 / D)
        second = s.sec[r, :][:, :1] * (1.0 / D)
        g_txt[r, :] = s.rs[r, :][:, :1] * (g_txt[r, :] - first - s.nhf[r, :] * second)

    each(PAIRS // 16, text_input)

    arrived(s.grecv, "g")

    def image_input(i):
        r = rows(i)
        g_img[r, :] = pick(s.gip[r, :], m) + s.grecv[r, :].astype(F32)

    each(PAIRS // 16, image_input)

    @pl.when(core == 0)
    def _():
        image_first.finish(store_first(tall))
        image_second.begin()
        image_second.finish(store_second)
        nhb_copy.wait_send()
        tpg_copy.wait_send()

    @pl.when(core == 1)
    def _():
        text_first.finish(store_first(XHALF // 16))
        text_second.begin()
        text_second.finish(store_second)
        imf_copy.wait_send()
        pg_copy.wait_send()

    def head_far(i):
        s.h3send[rows(i), :] = s.h2[rows(i, oz * XWIN), :].astype(BF)

    each(XWIN // 16, head_far)
    send(copy(s.h3send, s.h3recv, "h3", 0, dev(zz=oz)))
    arrived(s.h3recv, "h3")

    def head_near(i):
        s.h4[rows(i), :] = s.h2[rows(i, zh * XWIN), :] + s.h3recv[rows(i), :].astype(F32)

    each(XWIN // 16, head_near)
    theirs = s.h4.at[pl.ds(pl.multiple_of(oc * 16, 16), FIN)]
    send(copy(theirs, s.finr, "fin", 0, twin))
    own = pltpu.roll(s.h4[...], lax.rem(XWIN - 4 * x - LAST * core, XWIN), 0)[:LAST, :]
    arrived(s.finr, "fin")
    got = pltpu.roll(s.finr[...], lax.rem(FIN - 4 * x - 2 * core, FIN), 0)[:LAST, :]
    g_ih[...] = jnp.where(core == 0, own, got)
    g_th[...] = jnp.where(core == 0, got, own)

    for c in sent:
        c.wait_send()


def per_device(img_feat, img_head, txt_feat, txt_head):
    vmem = pl.BlockSpec(memory_space=pltpu.VMEM)
    g_img, g_ih, g_txt, g_th = pl.pallas_call(
        kernel,
        out_shape=(
            jax.ShapeDtypeStruct((PAIRS, HALF), F32),
            jax.ShapeDtypeStruct((LAST, HALF), F32),
            jax.ShapeDtypeStruct((PAIRS, HALF), F32),
            jax.ShapeDtypeStruct((LAST, HALF), F32),
        ),
        in_specs=[pl.BlockSpec(memory_space=pl.ANY)] * 4,
        out_specs=(vmem,) * 4,
        scratch_shapes=[pltpu.VMEM(shape, kind) for shape, kind in SCRATCH.values()]
        + [pltpu.SemaphoreType.DMA((total_sends,)), pltpu.SemaphoreType.DMA((total_recvs,))]
        + [pltpu.SemaphoreType.DMA((4,))],
        compiler_params=pltpu.CompilerParams(
            collective_id=0, has_side_effects=True, vmem_limit_bytes=60 * 1024 * 1024
        ),
        cost_estimate=pl.CostEstimate(flops=14 * 10**9, bytes_accessed=5 * 10**6, transcendentals=0),
    )(img_feat, img_head.T, txt_feat, txt_head)
    return g_img, g_ih, g_txt, g_th.T


def solution(mesh):
    in_specs = (P("dp", None), P(None, "mp"), P("dp", None), P("mp", None))
    out_specs = (P("dp", "mp"), P("dp", "mp"), P("dp", "mp"), P("mp", "dp"))
    return jax.shard_map(
        per_device, mesh=mesh, in_specs=in_specs, out_specs=out_specs, check_vma=False
    )
```

```python
import types

import jax
import jax.numpy as jnp
from jax import lax
from jax.experimental import pallas as pl
from jax.experimental.pallas import tpu as pltpu
from jax.sharding import PartitionSpec as P

LOGIT_SCALE = 10.0
LOGIT_BIAS = -2.5
NORM_EPS = 1e-06

NX = 4
NY = 4
NZ = 2
NC = 2
D = 1152
HALF = D // 2
PAIRS = 208
OWN = PAIRS // 2
WIN = 112
STEP = PAIRS - WIN
TC = NZ * WIN
IMGS = NX * PAIRS
YROWS = D // NY
ZROWS = YROWS // NZ
LAST = ZROWS // (NX * NC)
XWIN = 48
XHALF = NY * NZ * XWIN // 2
FIN = 32
BLOCK = IMGS // 2
CUT = 64
IMAGE_PARTS = ((0, WIN), (WIN, STEP))
TEXT_PARTS = ((0, CUT), (CUT, WIN - CUT))

NN = ((1,), (0,))
NT = ((1,), (1,))
TN = ((0,), (0,))
BF = jnp.bfloat16
F32 = jnp.float32

SCRATCH = {
    "tf": ((PAIRS, D), BF),
    "th": ((HALF, D), BF),
    "imf": ((PAIRS, D), BF),
    "iht": ((HALF, D), BF),
    "nhf": ((PAIRS, HALF), F32),
    "nhb": ((PAIRS, HALF), BF),
    "rs": ((PAIRS, 128), F32),
    "tpart": ((PAIRS, D), F32),
    "tsend": ((WIN, D), BF),
    "trecv": ((WIN, D), BF),
    "u": ((2, 8, D), F32),
    "tproj": ((WIN, D), F32),
    "tsc": ((WIN, 128), F32),
    "imh": ((NX, 2, PAIRS, HALF), BF),
    "isc": ((PAIRS, 128), F32),
    "img": ((IMGS, D), BF),
    "txt": ((NY, NC * TC, D), BF),
    "w": ((NY, IMGS, NC * TC), BF),
    "gi": ((IMGS, D), F32),
    "xsend": ((3, PAIRS, D), BF),
    "xa": ((WIN, D), BF),
    "xb": ((STEP, D), BF),
    "xr": ((2, PAIRS, D), BF),
    "gtcsend": ((NY, TC, D), BF),
    "gtcrecv": ((NY, TC, D), BF),
    "gt": ((NY, TC, D), F32),
    "gtall": ((NC * TC, D), F32),
    "ysend": ((3, TC, D), BF),
    "ya": ((NZ, CUT, D), BF),
    "yb": ((NZ, WIN - CUT, D), BF),
    "yr": ((2, TC, D), BF),
    "zsend": ((WIN, D), BF),
    "zrecv": ((WIN, D), BF),
    "gown": ((WIN, D), F32),
    "tw": ((2, WIN, D), BF),
    "sw": ((2, WIN, 128), F32),
    "tpg": ((PAIRS, D), BF),
    "ghalf": ((PAIRS, HALF), F32),
    "izsend": ((PAIRS, HALF), BF),
    "izrecv": ((PAIRS, HALF), BF),
    "dots": ((2, PAIRS, 128), F32),
    "pg": ((PAIRS, HALF), BF),
    "gip": ((PAIRS, D), F32),
    "gsend": ((PAIRS, HALF), BF),
    "grecv": ((PAIRS, HALF), BF),
    "imft": ((PAIRS, D), BF),
    "nhbt": ((PAIRS, HALF), BF),
    "pgt": ((PAIRS, HALF), BF),
    "tpgt": ((PAIRS, D), BF),
    "h": ((D, HALF), F32),
    "h1send": ((3, 2, XHALF, HALF), BF),
    "h1ab": ((2, XHALF, HALF), BF),
    "h1r": ((2, 2, XHALF, HALF), BF),
    "h1": ((2 * XHALF, HALF), F32),
    "h2send": ((3, 2, XWIN, HALF), BF),
    "h2ab": ((2, XWIN, HALF), BF),
    "h2r": ((2, 2, XWIN, HALF), BF),
    "h2": ((2 * XWIN, HALF), F32),
    "h3send": ((XWIN, HALF), BF),
    "h3recv": ((XWIN, HALF), BF),
    "h4": ((XWIN, HALF), F32),
    "finr": ((FIN, HALF), F32),
}

GROUPS = (
    ("t", 1), ("u", 1), ("img", NX * 4), ("txt", NY * NZ * 2), ("txtc", NY), ("xa", 1), ("xb", 1), ("xr", 4),
    ("iz", 1), ("dots", 1), ("gtc", NY), ("ya", 2), ("yb", 2), ("yr", 8), ("z", 2), ("tw", 2), ("sw", 1),
    ("g", 1), ("imft", 1), ("nhbt", 1), ("pgt", 1), ("tpgt", 1),
    ("h1ab", 2), ("h1r", 4), ("h2ab", 2), ("h2r", 4), ("h3", 1), ("fin", 1),
)
RECVS = {}
total_recvs = 0
for group, many in GROUPS:
    RECVS[group] = total_recvs
    total_recvs += many
total_sends = 128


def dot(a, b, dims):
    return lax.dot_general(a, b, (dims, ((), ())), preferred_element_type=F32)


def rows(i, first=0):
    return pl.ds(pl.multiple_of(first + i * 16, 16), 16)


def rowsum(v):
    return jnp.sum(v, -1, keepdims=True)


def wide(v):
    return jnp.broadcast_to(v, (v.shape[0], 128))


def each(count, body):
    lax.fori_loop(0, count, lambda i, c: (body(i), c)[1], 0)


def kernel(img_feat, img_head_t, txt_feat, txt_head, g_img, g_ih, g_txt, g_th, *scratch):
    s = types.SimpleNamespace(**dict(zip(SCRATCH, scratch)))
    ssem, rsem, lsem = scratch[len(SCRATCH) :]
    dp, m = lax.axis_index("dp"), lax.axis_index("mp")
    core = lax.rem(dp, NC)
    x = lax.rem(dp // NC, NX)
    zh = lax.rem(dp // (NC * NX), NZ)
    y = dp // (NC * NX * NZ)
    om, oc, oz = 1 - m, 1 - core, 1 - zh

    loads = [
        pltpu.make_async_copy(src, dst, lsem.at[at])
        for at, (src, dst) in enumerate(
            ((txt_feat, s.tf), (txt_head, s.th), (img_feat, s.imf), (img_head_t, s.iht))
        )
    ]
    for load in loads:
        load.start()

    def dev(yy=None, zz=None, xx=None, cc=None, mm=None):
        yy = y if yy is None else yy
        zz = zh if zz is None else zz
        xx = x if xx is None else xx
        cc = core if cc is None else cc
        mm = m if mm is None else mm
        return (((yy * NZ + zz) * NX + xx) * NC + cc, mm)

    def other(base, by, size):
        return lax.rem(base + by, size)

    x1, x2, x3 = (other(x, d, NX) for d in (1, 2, 3))
    y1, y2, y3 = (other(y, d, NY) for d in (1, 2, 3))
    mate, twin, far = dev(mm=om), dev(cc=oc), dev(zz=oz, mm=om)
    xup, xdown, yup, ydown = dev(xx=x1), dev(xx=x3), dev(yy=y1), dev(yy=y3)

    used = [0]
    sent = []

    def copy(src, dst, group, at, to):
        used[0] += 1
        return pltpu.make_async_remote_copy(
            src_ref=src,
            dst_ref=dst,
            send_sem=ssem.at[used[0] - 1],
            recv_sem=rsem.at[RECVS[group] + at],
            device_id=to,
            device_id_type=pl.DeviceIdType.MESH,
        )

    def send(c):
        c.start()
        sent.append(c)
        return c

    def arrived(ref, group, at=0):
        pltpu.make_async_remote_copy(
            src_ref=ref,
            dst_ref=ref,
            send_sem=ssem.at[0],
            recv_sem=rsem.at[RECVS[group] + at],
            device_id=twin,
            device_id_type=pl.DeviceIdType.MESH,
        ).wait_recv()

    def pick(whole, which):
        return jnp.where(which == 0, whole[:, :HALF], whole[:, HALF:])

    barrier = pltpu.get_barrier_semaphore()
    friends = [mate, twin, far, dev(zz=oz), xup, xdown, yup, ydown]
    for friend in friends:
        pl.semaphore_signal(barrier, inc=1, device_id=friend, device_id_type=pl.DeviceIdType.MESH)

    loads[0].wait()

    def norm(i):
        r = rows(i)
        t = s.tf[r, :].astype(F32)
        c = t - rowsum(t) * (1.0 / D)
        rs = lax.rsqrt(rowsum(c * c) * (1.0 / D) + NORM_EPS)
        half = pick(c * rs, m)
        s.nhf[r, :] = half
        s.nhb[r, :] = half.astype(BF)
        s.rs[r, :] = wide(rs)

    each(PAIRS // 16, norm)
    loads[1].wait()
    s.tpart[...] = dot(s.nhb[...], s.th[...], NN)

    def tosend(i):
        s.tsend[rows(i), :] = s.tpart[rows(i, om * STEP), :].astype(BF)

    each(WIN // 16, tosend)
    pl.semaphore_wait(barrier, len(friends))
    send(copy(s.tsend, s.trecv, "t", 0, mate))

    loads[2].wait()
    loads[3].wait()
    s.imh[x, m] = dot(s.imf[...], s.iht[...], NT).astype(BF)

    def image_part(xx, half, cut):
        if cut is None:
            return s.imh.at[xx, half]
        return s.imh.at[xx, half, pl.ds(*IMAGE_PARTS[cut])]

    def send_image(xx, half, to, cut=None):
        ref = image_part(xx, half, cut)
        send(copy(ref, ref, "img", xx * 4 + half * 2 + (cut or 0), to))

    def image_arrived(xx, half, cut=None):
        arrived(image_part(xx, half, cut), "img", xx * 4 + half * 2 + (cut or 0))

    def forward_image(half):
        image_arrived(x1, half)
        send_image(x1, half, xdown, 0)
        image_arrived(x3, half)
        send_image(x3, half, xup, 1)

    for to in (mate, xup, xdown):
        send_image(x, m, to)
    s.u[m] = dot(jnp.ones((8, HALF), BF), s.th[...], NN)
    send(copy(s.u.at[m], s.u.at[m], "u", 0, mate))

    nhb_copy = copy(s.nhb, s.nhbt, "nhbt", 0, twin)
    imf_copy = copy(s.imf, s.imft, "imft", 0, twin)
    pg_copy = copy(s.pg, s.pgt, "pgt", 0, twin)
    tpg_copy = copy(s.tpg, s.tpgt, "tpgt", 0, twin)

    @pl.when(core == 0)
    def _():
        nhb_copy.start()

    @pl.when(core == 1)
    def _():
        imf_copy.start()

    arrived(s.trecv, "t")

    def embed_text(i):
        p = s.tpart[rows(i, m * STEP), :] + s.trecv[rows(i), :].astype(F32)
        sc = lax.rsqrt(rowsum(p * p) + NORM_EPS)
        row = m * STEP + i * 16 + lax.broadcasted_iota(jnp.int32, (16, 1), 0)
        mine = (row >= m * OWN) & (row < m * OWN + OWN)
        s.tproj[rows(i), :] = p
        s.tsc[rows(i), :] = wide(sc)
        s.txt[y, rows(i, core * TC + zh * WIN), :] = jnp.where(mine, p * sc, 0.0).astype(BF)

    each(WIN // 16, embed_text)

    def part(yy, zz, cut=None):
        first, count = (0, WIN) if cut is None else TEXT_PARTS[cut]
        return s.txt.at[yy, pl.ds(pl.multiple_of(core * TC + zz * WIN + first, 16), count)]

    def side(yy, cc):
        return s.txt.at[yy, pl.ds(pl.multiple_of(cc * TC, 16), TC)]

    def send_text(yy, zz, to, cut=None):
        ref = part(yy, zz, cut)
        send(copy(ref, ref, "txt", yy * 4 + zz * 2 + (cut or 0), to))

    def text_arrived(yy, zz, cut=None):
        arrived(part(yy, zz, cut), "txt", yy * 4 + zz * 2 + (cut or 0))

    def forward_text(zz):
        text_arrived(y1, zz)
        send_text(y1, zz, ydown, 0)
        text_arrived(y3, zz)
        send_text(y3, zz, yup, 1)

    def send_twin(yy):
        send(copy(side(yy, core), side(yy, core), "txtc", yy, twin))

    def twin_arrived(yy):
        arrived(side(yy, oc), "txtc", yy)

    for to in (far, yup, ydown):
        send_text(y, zh, to)

    def zero(i):
        s.gi[rows(i), :] = jnp.zeros((16, D), F32)

    each(IMGS // 16, zero)
    forward_image(m)

    image_arrived(x, om)
    send_image(x, om, xup)
    send_image(x, om, xdown)

    def embed_images(xx, at, own=False):
        def embed(i):
            r = rows(i)
            p = jnp.concatenate([s.imh[xx, 0, r, :].astype(F32), s.imh[xx, 1, r, :].astype(F32)], axis=1)
            sc = lax.rsqrt(rowsum(p * p) + NORM_EPS)
            if own:
                s.isc[r, :] = wide(sc)
            s.img[rows(i, at * PAIRS), :] = (p * sc).astype(BF)

        each(PAIRS // 16, embed)

    embed_images(x, 0, own=True)

    text_arrived(y, oz)
    send_text(y, oz, yup)
    send_text(y, oz, ydown)
    send_twin(y)
    forward_text(zh)

    def unit(yy, half, own=False):
        r = pl.ds(pl.multiple_of(half * BLOCK, 16), BLOCK)
        texts = s.txt[yy]
        scores = dot(s.img[r, :], texts, NT)
        weights = 0.5 + 0.5 * jnp.tanh((0.5 * LOGIT_SCALE) * scores + 0.5 * LOGIT_BIAS)
        if own:
            row = lax.broadcasted_iota(jnp.int32, (BLOCK, NC * TC), 0)
            col = lax.broadcasted_iota(jnp.int32, (BLOCK, NC * TC), 1)
            first = core * TC + zh * WIN
            match = (row - col == m * STEP - first) & (col >= first) & (col < first + WIN)
            weights = weights - match.astype(F32)
        weights = weights.astype(BF)
        s.w[yy, r, :] = weights
        s.gi[r, :] += dot(weights, texts, NN)

    forward_image(om)
    embed_images(x1, 1)
    embed_images(x3, 2)
    forward_text(oz)
    send_twin(y1)
    send_twin(y3)
    twin_arrived(y)
    unit(y, 0, own=True)
    twin_arrived(y1)
    twin_arrived(y3)
    each(2, lambda i: unit(other(y, 1 + 2 * i, NY), 0))
    for zz in range(NZ):
        for half in (0, 1):
            text_arrived(y2, zz, half)
    send_twin(y2)
    for half in (0, 1):
        for cut in (0, 1):
            image_arrived(x2, half, cut)
    embed_images(x2, 3)
    each(3, lambda i: unit(other(y, i + i // 2, NY), 1))

    twin_arrived(y2)
    unit(y2, 1)

    def cast(at, place, add=None, first=0, count=PAIRS):
        def body(i):
            v = s.gi[rows(i, place * PAIRS + first), :]
            if add is not None:
                v = v + add[rows(i), :].astype(F32)
            s.xsend[at, rows(i, first), :] = v.astype(BF)

        each(count // 16, body)

    for half in (0, 1):
        first, count = IMAGE_PARTS[half]
        cast(0, 3, first=first, count=count)
        to, at = ((xup, s.xa), (xdown, s.xb))[half]
        send(copy(s.xsend.at[0, pl.ds(first, count)], at, ("xa", "xb")[half], 0, to))

    def image_back(at, place, half, to, add=None):
        first, count = IMAGE_PARTS[half]
        cast(at, place, add=add, first=first, count=count)
        r = pl.ds(first, count)
        send(copy(s.xsend.at[at, r], s.xr.at[at - 1, r], "xr", (at - 1) * 2 + half, to))

    image_back(2, 2, 0, xdown)
    unit(y2, 0)
    image_back(1, 1, 1, xup)

    def text_grad(yy):
        s.gtall[...] = dot(s.w[yy], s.img[...], TN)

        def out(i):
            s.gtcsend[yy, rows(i), :] = s.gtall[rows(i, oc * TC), :].astype(BF)
            s.gt[yy, rows(i), :] = s.gtall[rows(i, core * TC), :]

        each(TC // 16, out)

    def send_back_twin(yy):
        send(copy(s.gtcsend.at[yy], s.gtcrecv.at[yy], "gtc", yy, twin))

    def back_twin_arrived(yy):
        arrived(s.gtcrecv.at[yy], "gtc", yy)

    text_grad(y2)
    send_back_twin(y2)
    text_grad(y1)
    send_back_twin(y1)
    arrived(s.xa, "xa")
    image_back(1, 1, 0, xup, add=s.xa)
    arrived(s.xb, "xb")
    image_back(2, 2, 1, xdown, add=s.xb)
    back_twin_arrived(y2)

    def text_back(at, yy, zz, half, dst, group, index, to, add=None):
        first, count = TEXT_PARTS[half]

        def body(i):
            r = rows(i, zz * WIN + first)
            v = s.gt[yy, r, :] + s.gtcrecv[yy, r, :].astype(F32)
            if add is not None:
                v = v + add[zz, rows(i), :].astype(F32)
            s.ysend[at, r, :] = v.astype(BF)

        each(count // 16, body)
        r = pl.ds(pl.multiple_of(zz * WIN + first, 16), count)
        send(copy(s.ysend.at[at, r], dst(r), group, index, to))

    def text_back_to(at, yy, zz, half, to, add=None):
        text_back(at, yy, zz, half, lambda r: s.yr.at[at - 1, r], "yr", (at - 1) * 4 + zz * 2 + half, to, add)

    for zz in (oz, zh):
        text_back(0, y2, zz, 0, lambda r, zz=zz: s.ya.at[zz], "ya", zz, yup)
        text_back(0, y2, zz, 1, lambda r, zz=zz: s.yb.at[zz], "yb", zz, ydown)
    text_grad(y3)
    send_back_twin(y3)
    back_twin_arrived(y1)
    for zz in (oz, zh):
        text_back_to(1, y1, zz, 1, yup)
    back_twin_arrived(y3)
    for zz in (oz, zh):
        text_back_to(2, y3, zz, 0, ydown)
    text_grad(y)
    send_back_twin(y)
    for zz in (oz, zh):
        arrived(s.ya.at[zz], "ya", zz)
        text_back_to(1, y1, zz, 0, yup, add=s.ya)
        arrived(s.yb.at[zz], "yb", zz)
        text_back_to(2, y3, zz, 1, ydown, add=s.yb)
    back_twin_arrived(y)

    for way in (0, 1):
        for half in (0, 1):
            arrived(s.xr.at[way, pl.ds(*IMAGE_PARTS[half])], "xr", way * 2 + half)

    def projection(r):
        return jnp.concatenate([s.imh[x, 0, r, :].astype(F32), s.imh[x, 1, r, :].astype(F32)], axis=1)

    def image_sum(i):
        r = rows(i)
        g = s.gi[rows(i), :] + s.xr[0, r, :].astype(F32) + s.xr[1, r, :].astype(F32)
        g = LOGIT_SCALE * g
        s.dots[m, r, :] = wide(rowsum(g * projection(r)))
        s.ghalf[r, :] = pick(g, m)
        s.izsend[r, :] = pick(g, om).astype(BF)

    each(PAIRS // 16, image_sum)
    send(copy(s.dots.at[m], s.dots.at[m], "dots", 0, mate))
    send(copy(s.izsend, s.izrecv, "iz", 0, mate))

    def back_arrived(zz):
        for way in (0, 1):
            for half in (0, 1):
                first, count = TEXT_PARTS[half]
                r = pl.ds(pl.multiple_of(zz * WIN + first, 16), count)
                arrived(s.yr.at[way, r], "yr", way * 4 + zz * 2 + half)

    def text_sum(r):
        g = s.gt[y, r, :] + s.gtcrecv[y, r, :].astype(F32)
        return g + s.yr[0, r, :].astype(F32) + s.yr[1, r, :].astype(F32)

    def text_far(i):
        s.zsend[rows(i), :] = text_sum(rows(i, oz * WIN)).astype(BF)

    back_arrived(oz)
    for half in (0, 1):
        first, count = TEXT_PARTS[half]
        each(count // 16, lambda i, first=first: text_far(i + first // 16))
        r = pl.ds(first, count)
        send(copy(s.zsend.at[r], s.zrecv.at[r], "z", half, far))
    back_arrived(zh)

    def text_near(i):
        s.gown[rows(i), :] = text_sum(rows(i, zh * WIN))

    each(WIN // 16, text_near)


    def text_own(i):
        r = rows(i)
        g = LOGIT_SCALE * (s.gown[r, :] + s.zrecv[r, :].astype(F32))
        p = s.tproj[r, :]
        sc = s.tsc[r, :][:, :1]
        v = sc * g - (sc * sc * sc) * p * rowsum(p * g)
        row = m * STEP + i * 16 + lax.broadcasted_iota(jnp.int32, (16, 1), 0)
        mine = (row >= m * OWN) & (row < m * OWN + OWN)
        v = jnp.where(mine, v, 0.0).astype(BF)
        s.tw[m, r, :] = v
        s.sw[m, r, :] = wide(rowsum(v.astype(F32) * p))

    for half in (0, 1):
        first, count = TEXT_PARTS[half]
        r = pl.ds(first, count)
        arrived(s.zrecv.at[r], "z", half)
        each(count // 16, lambda i, first=first: text_own(i + first // 16))
        send(copy(s.tw.at[m, r], s.tw.at[m, r], "tw", half, mate))
    send(copy(s.sw.at[m], s.sw.at[m], "sw", 0, mate))

    arrived(s.dots.at[om], "dots")
    arrived(s.izrecv, "iz")

    def image_grad(i):
        r = rows(i)
        g = s.ghalf[r, :] + s.izrecv[r, :].astype(F32)
        sc = s.isc[r, :][:, :1]
        total = (s.dots[0, r, :] + s.dots[1, r, :])[:, :1]
        p = s.imh[x, m, r, :].astype(F32)
        s.pg[r, :] = (sc * g - (sc * sc * sc) * p * total).astype(BF)

    each(PAIRS // 16, image_grad)

    @pl.when(core == 1)
    def _():
        pg_copy.start()

    class Ring:
        def __init__(self, load, count, bufs, groups, up, down, chunks):
            self.load, self.count, self.chunks = load, count, chunks
            self.out, self.ab, self.back = bufs
            self.groups = groups
            self.used = pl.ds(0, count * 16)
            n = self.used
            self.copies = [
                copy(self.out.at[0, 0, n], self.ab.at[0, n], groups[0], 0, up),
                copy(self.out.at[0, 1, n], self.ab.at[1, n], groups[0], 1, down),
                copy(self.out.at[1, 1, n], self.back.at[0, 1, n], groups[1], 1, up),
                copy(self.out.at[2, 0, n], self.back.at[1, 0, n], groups[1], 2, down),
                copy(self.out.at[1, 0, n], self.back.at[0, 0, n], groups[1], 0, up),
                copy(self.out.at[2, 1, n], self.back.at[1, 1, n], groups[1], 3, down),
            ]

        def cast(self, at, chunk, half, add=None):
            def body(i):
                v = self.load(chunk, half, i)
                if add is not None:
                    v = v + self.ab[add, rows(i), :].astype(F32)
                self.out[at, half, rows(i), :] = v.astype(BF)

            each(self.count, body)

        def begin(self):
            for half in (0, 1):
                self.cast(0, self.chunks[2], half)
                self.copies[half].start()
            self.cast(1, self.chunks[1], 1)
            self.copies[2].start()
            self.cast(2, self.chunks[3], 0)
            self.copies[3].start()

        def pass_on(self):
            arrived(self.ab.at[0, self.used], self.groups[0], 0)
            self.cast(1, self.chunks[1], 0, add=0)
            self.copies[4].start()
            arrived(self.ab.at[1, self.used], self.groups[0], 1)
            self.cast(2, self.chunks[3], 1, add=1)
            self.copies[5].start()

        def finish(self, store):
            for way in (0, 1):
                for half in (0, 1):
                    arrived(self.back.at[way, half, self.used], self.groups[1], way * 2 + half)
            for half in (0, 1):

                def total(i, half=half):
                    v = self.load(self.chunks[0], half, i) + self.back[0, half, rows(i), :].astype(F32)
                    store(half, i, v + self.back[1, half, rows(i), :].astype(F32))

                each(self.count, total)
            for c in self.copies:
                c.wait_send()

    def store_first(count):
        def store(half, i, v):
            s.h1[rows(i, half * count * 16), :] = v

        return store

    def store_second(half, i, v):
        s.h2[rows(i, half * XWIN), :] = v

    bufs1, bufs2 = (s.h1send, s.h1ab, s.h1r), (s.h2send, s.h2ab, s.h2r)
    xs, ys = (x, x1, x2, x3), (y, y1, y2, y3)
    tall = ZROWS // 16
    image_first = Ring(
        lambda c, half, i: s.h[rows(i, c * YROWS + half * ZROWS), :],
        tall, bufs1, ("h1ab", "h1r"), yup, ydown, ys,
    )
    image_second = Ring(
        lambda c, half, i: s.h1[rows(i, half * ZROWS + c * 32), :],
        XWIN // 16, bufs2, ("h2ab", "h2r"), xup, xdown, xs,
    )
    text_first = Ring(
        lambda c, half, i: s.h[rows(lax.rem(i, 3), (half * NY + i // 3) * ZROWS + c * 32), :],
        XHALF // 16, bufs1, ("h1ab", "h1r"), xup, xdown, xs,
    )
    text_second = Ring(
        lambda c, half, i: s.h1[rows(i, (c * NZ + half) * XWIN), :],
        XWIN // 16, bufs2, ("h2ab", "h2r"), yup, ydown, ys,
    )

    @pl.when(core == 0)
    def _():
        arrived(s.imft, "imft")
        arrived(s.pgt, "pgt")
        s.h[...] = dot(s.imf[...], s.pg[...], TN) + dot(s.imft[...], s.pgt[...], TN)
        image_first.begin()
        image_first.pass_on()

    for half in (0, 1):
        arrived(s.tw.at[om, pl.ds(*TEXT_PARTS[half])], "tw", half)

    def merge(i):
        lo, hi = jnp.minimum(i, 6), jnp.maximum(i - 6, 0)
        v = jnp.where(i <= 6, s.tw[0, rows(lo), :].astype(F32), 0.0)
        v = v + jnp.where(i >= 6, s.tw[1, rows(hi), :].astype(F32), 0.0)
        s.tpg[rows(i), :] = v.astype(BF)

    each(PAIRS // 16, merge)

    @pl.when(core == 0)
    def _():
        tpg_copy.start()

    @pl.when(core == 1)
    def _():
        arrived(s.nhbt, "nhbt")
        arrived(s.tpgt, "tpgt")
        s.h[...] = dot(s.tpg[...], s.nhb[...], TN) + dot(s.tpgt[...], s.nhbt[...], TN)
        text_first.begin()

    s.gip[...] = dot(s.pg[...], s.iht[...], NN)

    def image_out(i):
        s.gsend[rows(i), :] = pick(s.gip[rows(i), :], om).astype(BF)

    each(PAIRS // 16, image_out)

    send(copy(s.gsend, s.grecv, "g", 0, mate))

    @pl.when(core == 1)
    def _():
        text_first.pass_on()

    arrived(s.sw.at[om], "sw")
    arrived(s.u.at[om], "u")
    g_txt[...] = dot(s.tpg[...], s.th[...], NT)

    def text_input(i):
        r = rows(i)
        u = (s.u[0] + s.u[1])[:1, :]
        first = rowsum(s.tpg[r, :].astype(F32) * u) * (1.0 / D)
        lo, hi = jnp.minimum(i, 6), jnp.maximum(i - 6, 0)
        second = jnp.where(i <= 6, s.sw[0, rows(lo), :], 0.0) + jnp.where(i >= 6, s.sw[1, rows(hi), :], 0.0)
        second = second[:, :1] * (1.0 / D)
        g_txt[r, :] = s.rs[r, :][:, :1] * (g_txt[r, :] - first - s.nhf[r, :] * second)

    each(PAIRS // 16, text_input)

    arrived(s.grecv, "g")

    def image_input(i):
        r = rows(i)
        g_img[r, :] = pick(s.gip[r, :], m) + s.grecv[r, :].astype(F32)

    each(PAIRS // 16, image_input)

    @pl.when(core == 0)
    def _():
        image_first.finish(store_first(tall))
        image_second.begin()
        image_second.pass_on()
        image_second.finish(store_second)
        nhb_copy.wait_send()
        tpg_copy.wait_send()

    @pl.when(core == 1)
    def _():
        text_first.finish(store_first(XHALF // 16))
        text_second.begin()
        text_second.pass_on()
        text_second.finish(store_second)
        imf_copy.wait_send()
        pg_copy.wait_send()

    def head_far(i):
        s.h3send[rows(i), :] = s.h2[rows(i, oz * XWIN), :].astype(BF)

    each(XWIN // 16, head_far)
    send(copy(s.h3send, s.h3recv, "h3", 0, dev(zz=oz)))
    arrived(s.h3recv, "h3")

    def head_near(i):
        s.h4[rows(i), :] = s.h2[rows(i, zh * XWIN), :] + s.h3recv[rows(i), :].astype(F32)

    each(XWIN // 16, head_near)
    theirs = s.h4.at[pl.ds(pl.multiple_of(oc * 16, 16), FIN)]
    send(copy(theirs, s.finr, "fin", 0, twin))
    own = pltpu.roll(s.h4[...], lax.rem(XWIN - 4 * x - LAST * core, XWIN), 0)[:LAST, :]
    arrived(s.finr, "fin")
    got = pltpu.roll(s.finr[...], lax.rem(FIN - 4 * x - 2 * core, FIN), 0)[:LAST, :]
    g_ih[...] = jnp.where(core == 0, own, got)
    g_th[...] = jnp.where(core == 0, got, own)

    for c in sent:
        c.wait_send()


def per_device(img_feat, img_head, txt_feat, txt_head):
    vmem = pl.BlockSpec(memory_space=pltpu.VMEM)
    g_img, g_ih, g_txt, g_th = pl.pallas_call(
        kernel,
        out_shape=(
            jax.ShapeDtypeStruct((PAIRS, HALF), F32),
            jax.ShapeDtypeStruct((LAST, HALF), F32),
            jax.ShapeDtypeStruct((PAIRS, HALF), F32),
            jax.ShapeDtypeStruct((LAST, HALF), F32),
        ),
        in_specs=[pl.BlockSpec(memory_space=pl.ANY)] * 4,
        out_specs=(vmem,) * 4,
        scratch_shapes=[pltpu.VMEM(shape, kind) for shape, kind in SCRATCH.values()]
        + [pltpu.SemaphoreType.DMA((total_sends,)), pltpu.SemaphoreType.DMA((total_recvs,))]
        + [pltpu.SemaphoreType.DMA((4,))],
        compiler_params=pltpu.CompilerParams(
            collective_id=0, has_side_effects=True, vmem_limit_bytes=60 * 1024 * 1024
        ),
        cost_estimate=pl.CostEstimate(flops=14 * 10**9, bytes_accessed=5 * 10**6, transcendentals=0),
    )(img_feat, img_head.T, txt_feat, txt_head)
    return g_img, g_ih, g_txt, g_th.T


def solution(mesh):
    in_specs = (P("dp", None), P(None, "mp"), P("dp", None), P("mp", None))
    out_specs = (P("dp", "mp"), P("dp", "mp"), P("dp", "mp"), P("mp", "dp"))
    return jax.shard_map(
        per_device, mesh=mesh, in_specs=in_specs, out_specs=out_specs, check_vma=False
    )
```

```python
import types

import jax
import jax.numpy as jnp
from jax import lax
from jax.experimental import pallas as pl
from jax.experimental.pallas import tpu as pltpu
from jax.sharding import PartitionSpec as P

LOGIT_SCALE = 10.0
LOGIT_BIAS = -2.5
NORM_EPS = 1e-06

NX = 4
NY = 4
NZ = 2
NC = 2
D = 1152
HALF = D // 2
PAIRS = 208
OWN = PAIRS // 2
WIN = 112
STEP = PAIRS - WIN
TC = NZ * WIN
IMGS = NX * PAIRS
YROWS = D // NY
ZROWS = YROWS // NZ
LAST = ZROWS // (NX * NC)
XWIN = 48
XHALF = NY * NZ * XWIN // 2
FIN = 32
CUT = 64
IMAGE_PARTS = ((0, WIN), (WIN, STEP))
TEXT_PARTS = ((0, CUT), (CUT, WIN - CUT))
Z_PARTS = ((0, 32), (32, 32), (64, 48))

COLUMNS = ((0, 256), (256, HALF - 256))

NN = ((1,), (0,))
NT = ((1,), (1,))
TN = ((0,), (0,))
BF = jnp.bfloat16
F32 = jnp.float32

SCRATCH = {
    "tf": ((PAIRS, D), BF),
    "th": ((HALF, D), BF),
    "imf": ((PAIRS, D), BF),
    "iht": ((HALF, D), BF),
    "nhf": ((PAIRS, HALF), F32),
    "nhb": ((PAIRS, HALF), BF),
    "rs": ((PAIRS, 128), F32),
    "tpart": ((PAIRS, D), F32),
    "tsend": ((WIN, D), BF),
    "trecv": ((WIN, D), BF),
    "u": ((2, 8, D), F32),
    "tproj": ((WIN, D), F32),
    "tsc": ((WIN, 128), F32),
    "imh": ((NX, 2, PAIRS, HALF), BF),
    "isc": ((PAIRS, 128), F32),
    "img": ((IMGS, D), BF),
    "txt": ((NY, NC * TC, D), BF),
    "w": ((NY, IMGS, NC * TC), BF),
    "gi": ((IMGS, D), F32),
    "xsend": ((3, PAIRS, D), BF),
    "xa": ((WIN, D), BF),
    "xb": ((STEP, D), BF),
    "xr": ((2, PAIRS, D), BF),
    "gtcsend": ((NY, TC, D), BF),
    "gtcrecv": ((NY, TC, D), BF),
    "gt": ((NY, TC, D), F32),
    "gtall": ((NC * TC, D), F32),
    "ysend": ((3, TC, D), BF),
    "ya": ((NZ, CUT, D), BF),
    "yb": ((NZ, WIN - CUT, D), BF),
    "yr": ((2, TC, D), BF),
    "zsend": ((WIN, D), BF),
    "zrecv": ((WIN, D), BF),
    "gown": ((WIN, D), F32),
    "tw": ((2, WIN, D), BF),
    "sw": ((2, WIN, 128), F32),
    "tpg": ((PAIRS, D), BF),
    "ghalf": ((PAIRS, HALF), F32),
    "izsend": ((PAIRS, HALF), BF),
    "izrecv": ((PAIRS, HALF), BF),
    "dots": ((2, PAIRS, 128), F32),
    "pg": ((PAIRS, HALF), BF),
    "gip": ((PAIRS, D), F32),
    "gsend": ((PAIRS, HALF), BF),
    "grecv": ((PAIRS, HALF), BF),
    "imft": ((PAIRS, D), BF),
    "nhbt": ((PAIRS, HALF), BF),
    "pgt": ((PAIRS, HALF), BF),
    "tpgt": ((PAIRS, D), BF),
    "h": ((D, HALF), F32),
    "h1send": ((3, 2, XHALF, HALF), BF),
    "h1r": ((3, 2, XHALF, HALF), BF),
    "h1": ((2 * XHALF, HALF), F32),
    "h2send": ((3, 2, XWIN, HALF), BF),
    "h2r": ((3, 2, XWIN, HALF), BF),
    "h2": ((2 * XWIN, HALF), F32),
    "h3send": ((XWIN, HALF), BF),
    "h3recv": ((XWIN, HALF), BF),
    "h4": ((XWIN, HALF), F32),
    "finr": ((FIN, HALF), F32),
}

GROUPS = (
    ("t", 2), ("u", 1), ("img", NX * 4), ("txt", NY * NZ * 2), ("txtc", NY * NZ), ("xa", 1), ("xb", 1), ("xr", 4),
    ("iz", 1), ("dots", 1), ("gtc", NY), ("ya", 2), ("yb", 2), ("yr", 8), ("z", 3), ("tw", 3), ("sw", 1),
    ("g", 1), ("imft", 1), ("nhbt", 1), ("pgt", 1), ("tpgt", 1),
    ("h1r", 6), ("h2r", 6), ("h3", 1), ("fin", 1),
)
RECVS = {}
total_recvs = 0
for group, many in GROUPS:
    RECVS[group] = total_recvs
    total_recvs += many
total_sends = 160


def dot(a, b, dims):
    return lax.dot_general(a, b, (dims, ((), ())), preferred_element_type=F32)


def rows(i, first=0):
    return pl.ds(pl.multiple_of(first + i * 16, 16), 16)


def rowsum(v):
    return jnp.sum(v, -1, keepdims=True)


def wide(v):
    return jnp.broadcast_to(v, (v.shape[0], 128))


def each(count, body):
    lax.fori_loop(0, count, lambda i, c: (body(i), c)[1], 0)


def kernel(img_feat, img_head_t, txt_feat, txt_head, g_img, g_ih, g_txt, g_th, *scratch):
    s = types.SimpleNamespace(**dict(zip(SCRATCH, scratch)))
    ssem, rsem, lsem = scratch[len(SCRATCH) :]
    dp, m = lax.axis_index("dp"), lax.axis_index("mp")
    core = lax.rem(dp, NC)
    x = lax.rem(dp // NC, NX)
    zh = lax.rem(dp // (NC * NX), NZ)
    y = dp // (NC * NX * NZ)
    om, oc, oz = 1 - m, 1 - core, 1 - zh

    loads = [
        pltpu.make_async_copy(src, dst, lsem.at[at])
        for at, (src, dst) in enumerate(
            ((txt_feat, s.tf), (txt_head, s.th), (img_feat, s.imf), (img_head_t, s.iht))
        )
    ]
    for load in loads:
        load.start()

    def dev(yy=None, zz=None, xx=None, cc=None, mm=None):
        yy = y if yy is None else yy
        zz = zh if zz is None else zz
        xx = x if xx is None else xx
        cc = core if cc is None else cc
        mm = m if mm is None else mm
        return (((yy * NZ + zz) * NX + xx) * NC + cc, mm)

    def other(base, by, size):
        return lax.rem(base + by, size)

    x1, x2, x3 = (other(x, d, NX) for d in (1, 2, 3))
    y1, y2, y3 = (other(y, d, NY) for d in (1, 2, 3))
    mate, twin, far = dev(mm=om), dev(cc=oc), dev(zz=oz, mm=om)
    xup, xdown, yup, ydown = dev(xx=x1), dev(xx=x3), dev(yy=y1), dev(yy=y3)

    used = [0]
    sent = []

    def copy(src, dst, group, at, to):
        used[0] += 1
        return pltpu.make_async_remote_copy(
            src_ref=src,
            dst_ref=dst,
            send_sem=ssem.at[used[0] - 1],
            recv_sem=rsem.at[RECVS[group] + at],
            device_id=to,
            device_id_type=pl.DeviceIdType.MESH,
        )

    def send(c):
        c.start()
        sent.append(c)
        return c

    def arrived(ref, group, at=0):
        pltpu.make_async_remote_copy(
            src_ref=ref,
            dst_ref=ref,
            send_sem=ssem.at[0],
            recv_sem=rsem.at[RECVS[group] + at],
            device_id=twin,
            device_id_type=pl.DeviceIdType.MESH,
        ).wait_recv()

    def pick(whole, which):
        return jnp.where(which == 0, whole[:, :HALF], whole[:, HALF:])

    barrier = pltpu.get_barrier_semaphore()
    friends = [mate, twin, far, dev(zz=oz), xup, xdown, yup, ydown, dev(xx=x2), dev(yy=y2)]
    for friend in friends:
        pl.semaphore_signal(barrier, inc=1, device_id=friend, device_id_type=pl.DeviceIdType.MESH)

    loads[0].wait()

    def norm(i):
        r = rows(i)
        t = s.tf[r, :].astype(F32)
        c = t - rowsum(t) * (1.0 / D)
        rs = lax.rsqrt(rowsum(c * c) * (1.0 / D) + NORM_EPS)
        half = pick(c * rs, m)
        s.nhf[r, :] = half
        s.nhb[r, :] = half.astype(BF)
        s.rs[r, :] = wide(rs)

    each(PAIRS // 16, norm)
    loads[1].wait()
    s.tpart[...] = dot(s.nhb[...], s.th[...], NN)

    def tosend(i):
        s.tsend[rows(i), :] = s.tpart[rows(i, om * STEP), :].astype(BF)

    each(WIN // 16, tosend)
    pl.semaphore_wait(barrier, len(friends))
    for half, where in enumerate(TEXT_PARTS):
        r = pl.ds(*where)
        send(copy(s.tsend.at[r], s.trecv.at[r], "t", half, mate))

    loads[2].wait()
    loads[3].wait()
    s.imh[x, m] = dot(s.imf[...], s.iht[...], NT).astype(BF)

    def image_part(xx, half, cut):
        if cut is None:
            return s.imh.at[xx, half]
        return s.imh.at[xx, half, pl.ds(*IMAGE_PARTS[cut])]

    def send_image(xx, half, to, cut=None):
        ref = image_part(xx, half, cut)
        send(copy(ref, ref, "img", xx * 4 + half * 2 + (cut or 0), to))

    def image_arrived(xx, half, cut=None):
        arrived(image_part(xx, half, cut), "img", xx * 4 + half * 2 + (cut or 0))

    def forward_image(half):
        image_arrived(x1, half)
        send_image(x1, half, xdown, 0)
        image_arrived(x3, half)
        send_image(x3, half, xup, 1)

    for to in (mate, xup, xdown):
        send_image(x, m, to)
    s.u[m] = dot(jnp.ones((8, HALF), BF), s.th[...], NN)
    send(copy(s.u.at[m], s.u.at[m], "u", 0, mate))

    nhb_copy = copy(s.nhb, s.nhbt, "nhbt", 0, twin)
    imf_copy = copy(s.imf, s.imft, "imft", 0, twin)
    pg_copy = copy(s.pg, s.pgt, "pgt", 0, twin)
    tpg_copy = copy(s.tpg, s.tpgt, "tpgt", 0, twin)

    @pl.when(core == 0)
    def _():
        nhb_copy.start()

    @pl.when(core == 1)
    def _():
        imf_copy.start()


    def embed_text(i):
        p = s.tpart[rows(i, m * STEP), :] + s.trecv[rows(i), :].astype(F32)
        sc = lax.rsqrt(rowsum(p * p) + NORM_EPS)
        row = m * STEP + i * 16 + lax.broadcasted_iota(jnp.int32, (16, 1), 0)
        mine = (row >= m * OWN) & (row < m * OWN + OWN)
        s.tproj[rows(i), :] = p
        s.tsc[rows(i), :] = wide(sc)
        s.txt[y, rows(i, core * TC + zh * WIN), :] = jnp.where(mine, p * sc, 0.0).astype(BF)


    def part(yy, zz, cut=None):
        first, count = (0, WIN) if cut is None else TEXT_PARTS[cut]
        return s.txt.at[yy, pl.ds(pl.multiple_of(core * TC + zz * WIN + first, 16), count)]

    def send_text(yy, zz, to, cut=None):
        ref = part(yy, zz, cut)
        send(copy(ref, ref, "txt", yy * 4 + zz * 2 + (cut or 0), to))

    def text_arrived(yy, zz, cut=None):
        arrived(part(yy, zz, cut), "txt", yy * 4 + zz * 2 + (cut or 0))

    def forward_text(zz):
        text_arrived(y1, zz, 0)
        send_text(y1, zz, ydown, 0)
        text_arrived(y3, zz, 0)
        text_arrived(y3, zz, 1)
        send_text(y3, zz, yup, 1)
        send_twin(y3, zz)
        text_arrived(y1, zz, 1)
        send_twin(y1, zz)

    def side_part(yy, cc, zz):
        return s.txt.at[yy, pl.ds(pl.multiple_of(cc * TC + zz * WIN, 16), WIN)]

    def send_twin(yy, zz):
        send(copy(part(yy, zz), part(yy, zz), "txtc", yy * NZ + zz, twin))

    def twin_arrived(yy):
        for zz in range(NZ):
            arrived(side_part(yy, oc, zz), "txtc", yy * NZ + zz)

    for half, (first, count) in enumerate(TEXT_PARTS):
        arrived(s.trecv.at[pl.ds(first, count)], "t", half)
        each(count // 16, lambda i, first=first: embed_text(i + first // 16))
        for to in (far, yup, ydown):
            send_text(y, zh, to, half)
    send_twin(y, zh)

    def zero(i):
        s.gi[rows(i), :] = jnp.zeros((16, D), F32)

    each(IMGS // 16, zero)
    forward_image(m)

    image_arrived(x, om)
    send_image(x, om, xup)
    send_image(x, om, xdown)

    def embed_images(xx, at, own=False):
        def embed(i):
            r = rows(i)
            p = jnp.concatenate([s.imh[xx, 0, r, :].astype(F32), s.imh[xx, 1, r, :].astype(F32)], axis=1)
            sc = lax.rsqrt(rowsum(p * p) + NORM_EPS)
            if own:
                s.isc[r, :] = wide(sc)
            s.img[rows(i, at * PAIRS), :] = (p * sc).astype(BF)

        each(PAIRS // 16, embed)

    embed_images(x, 0, own=True)

    for half in (0, 1):
        text_arrived(y, oz, half)
        send_text(y, oz, yup, half)
        send_text(y, oz, ydown, half)
    send_twin(y, oz)
    forward_text(zh)

    def unit(yy, first, count, own=False):
        r = pl.ds(first, count)
        texts = s.txt[yy]
        scores = dot(s.img[r, :], texts, NT)
        weights = 0.5 + 0.5 * jnp.tanh((0.5 * LOGIT_SCALE) * scores + 0.5 * LOGIT_BIAS)
        if own:
            row = lax.broadcasted_iota(jnp.int32, (count, NC * TC), 0)
            col = lax.broadcasted_iota(jnp.int32, (count, NC * TC), 1)
            at = core * TC + zh * WIN
            match = (row - col == m * STEP - at) & (col >= at) & (col < at + WIN)
            weights = weights - match.astype(F32)
        weights = weights.astype(BF)
        s.w[yy, r, :] = weights
        s.gi[r, :] += dot(weights, texts, NN)

    twin_arrived(y)
    unit(y, 0, PAIRS, own=True)
    forward_image(om)
    embed_images(x1, 1)
    embed_images(x3, 2)
    forward_text(oz)
    unit(y, PAIRS, 2 * PAIRS)
    twin_arrived(y1)
    unit(y1, 0, 3 * PAIRS)
    twin_arrived(y3)
    unit(y3, 0, 3 * PAIRS)
    for zz in (zh, oz):
        for half in (0, 1):
            text_arrived(y2, zz, half)
        send_twin(y2, zz)
    for half in (0, 1):
        for cut in (0, 1):
            image_arrived(x2, half, cut)
    embed_images(x2, 3)
    each(3, lambda i: unit(other(y, i + i // 2, NY), 3 * PAIRS, PAIRS))

    twin_arrived(y2)
    unit(y2, 2 * PAIRS, 2 * PAIRS)

    def cast(at, place, add=None, first=0, count=PAIRS):
        def body(i):
            v = s.gi[rows(i, place * PAIRS + first), :]
            if add is not None:
                v = v + add[rows(i), :].astype(F32)
            s.xsend[at, rows(i, first), :] = v.astype(BF)

        each(count // 16, body)

    for half in (0, 1):
        first, count = IMAGE_PARTS[half]
        cast(0, 3, first=first, count=count)
        to, at = ((xup, s.xa), (xdown, s.xb))[half]
        send(copy(s.xsend.at[0, pl.ds(first, count)], at, ("xa", "xb")[half], 0, to))

    def image_back(at, place, half, to, add=None):
        first, count = IMAGE_PARTS[half]
        cast(at, place, add=add, first=first, count=count)
        r = pl.ds(first, count)
        send(copy(s.xsend.at[at, r], s.xr.at[at - 1, r], "xr", (at - 1) * 2 + half, to))

    image_back(2, 2, 0, xdown)
    unit(y2, 0, 2 * PAIRS)
    image_back(1, 1, 1, xup)

    def text_grad(yy):
        s.gtall[...] = dot(s.w[yy], s.img[...], TN)

        def out(i):
            s.gtcsend[yy, rows(i), :] = s.gtall[rows(i, oc * TC), :].astype(BF)
            s.gt[yy, rows(i), :] = s.gtall[rows(i, core * TC), :]

        each(TC // 16, out)

    def send_back_twin(yy):
        send(copy(s.gtcsend.at[yy], s.gtcrecv.at[yy], "gtc", yy, twin))

    def back_twin_arrived(yy):
        arrived(s.gtcrecv.at[yy], "gtc", yy)

    def columns_of(cc):
        return s.w[y2, :, pl.ds(cc * TC, TC)]

    @pl.when(core == 0)
    def _():
        s.gtcsend[y2] = dot(columns_of(1), s.img[...], TN).astype(BF)

    @pl.when(core == 1)
    def _():
        s.gtcsend[y2] = dot(columns_of(0), s.img[...], TN).astype(BF)

    send_back_twin(y2)

    @pl.when(core == 0)
    def _():
        s.gt[y2] = dot(columns_of(0), s.img[...], TN)

    @pl.when(core == 1)
    def _():
        s.gt[y2] = dot(columns_of(1), s.img[...], TN)

    text_grad(y1)
    send_back_twin(y1)
    arrived(s.xa, "xa")
    image_back(1, 1, 0, xup, add=s.xa)
    arrived(s.xb, "xb")
    image_back(2, 2, 1, xdown, add=s.xb)
    back_twin_arrived(y2)

    def text_back(at, yy, zz, half, dst, group, index, to, add=None):
        first, count = TEXT_PARTS[half]

        def body(i):
            r = rows(i, zz * WIN + first)
            v = s.gt[yy, r, :] + s.gtcrecv[yy, r, :].astype(F32)
            if add is not None:
                v = v + add[zz, rows(i), :].astype(F32)
            s.ysend[at, r, :] = v.astype(BF)

        each(count // 16, body)
        r = pl.ds(pl.multiple_of(zz * WIN + first, 16), count)
        send(copy(s.ysend.at[at, r], dst(r), group, index, to))

    def text_back_to(at, yy, zz, half, to, add=None):
        text_back(at, yy, zz, half, lambda r: s.yr.at[at - 1, r], "yr", (at - 1) * 4 + zz * 2 + half, to, add)

    for zz in (oz, zh):
        text_back(0, y2, zz, 0, lambda r, zz=zz: s.ya.at[zz], "ya", zz, yup)
        text_back(0, y2, zz, 1, lambda r, zz=zz: s.yb.at[zz], "yb", zz, ydown)
    text_grad(y3)
    send_back_twin(y3)
    back_twin_arrived(y1)
    for zz in (oz, zh):
        text_back_to(1, y1, zz, 1, yup)
    back_twin_arrived(y3)
    for zz in (oz, zh):
        text_back_to(2, y3, zz, 0, ydown)
    text_grad(y)
    send_back_twin(y)
    for zz in (oz, zh):
        arrived(s.ya.at[zz], "ya", zz)
        text_back_to(1, y1, zz, 0, yup, add=s.ya)
        arrived(s.yb.at[zz], "yb", zz)
        text_back_to(2, y3, zz, 1, ydown, add=s.yb)
    back_twin_arrived(y)

    for way in (0, 1):
        for half in (0, 1):
            arrived(s.xr.at[way, pl.ds(*IMAGE_PARTS[half])], "xr", way * 2 + half)

    def projection(r):
        return jnp.concatenate([s.imh[x, 0, r, :].astype(F32), s.imh[x, 1, r, :].astype(F32)], axis=1)

    def image_sum(i):
        r = rows(i)
        g = s.gi[rows(i), :] + s.xr[0, r, :].astype(F32) + s.xr[1, r, :].astype(F32)
        g = LOGIT_SCALE * g
        s.dots[m, r, :] = wide(rowsum(g * projection(r)))
        s.ghalf[r, :] = pick(g, m)
        s.izsend[r, :] = pick(g, om).astype(BF)

    each(PAIRS // 16, image_sum)
    send(copy(s.dots.at[m], s.dots.at[m], "dots", 0, mate))
    send(copy(s.izsend, s.izrecv, "iz", 0, mate))

    def back_arrived(zz):
        for way in (0, 1):
            for half in (0, 1):
                first, count = TEXT_PARTS[half]
                r = pl.ds(pl.multiple_of(zz * WIN + first, 16), count)
                arrived(s.yr.at[way, r], "yr", way * 4 + zz * 2 + half)

    def text_sum(r):
        g = s.gt[y, r, :] + s.gtcrecv[y, r, :].astype(F32)
        return g + s.yr[0, r, :].astype(F32) + s.yr[1, r, :].astype(F32)

    def text_far(i):
        s.zsend[rows(i), :] = text_sum(rows(i, oz * WIN)).astype(BF)

    back_arrived(oz)
    for half, (first, count) in enumerate(Z_PARTS):
        each(count // 16, lambda i, first=first: text_far(i + first // 16))
        r = pl.ds(first, count)
        send(copy(s.zsend.at[r], s.zrecv.at[r], "z", half, far))
    back_arrived(zh)

    def text_near(i):
        s.gown[rows(i), :] = text_sum(rows(i, zh * WIN))

    each(WIN // 16, text_near)


    def text_own(i):
        r = rows(i)
        g = LOGIT_SCALE * (s.gown[r, :] + s.zrecv[r, :].astype(F32))
        p = s.tproj[r, :]
        sc = s.tsc[r, :][:, :1]
        v = sc * g - (sc * sc * sc) * p * rowsum(p * g)
        row = m * STEP + i * 16 + lax.broadcasted_iota(jnp.int32, (16, 1), 0)
        mine = (row >= m * OWN) & (row < m * OWN + OWN)
        v = jnp.where(mine, v, 0.0).astype(BF)
        s.tw[m, r, :] = v
        s.sw[m, r, :] = wide(rowsum(v.astype(F32) * p))

    for half, (first, count) in enumerate(Z_PARTS):
        r = pl.ds(first, count)
        arrived(s.zrecv.at[r], "z", half)
        each(count // 16, lambda i, first=first: text_own(i + first // 16))
        send(copy(s.tw.at[m, r], s.tw.at[m, r], "tw", half, mate))
    send(copy(s.sw.at[m], s.sw.at[m], "sw", 0, mate))

    arrived(s.dots.at[om], "dots")
    arrived(s.izrecv, "iz")

    def image_grad(i):
        r = rows(i)
        g = s.ghalf[r, :] + s.izrecv[r, :].astype(F32)
        sc = s.isc[r, :][:, :1]
        total = (s.dots[0, r, :] + s.dots[1, r, :])[:, :1]
        p = s.imh[x, m, r, :].astype(F32)
        s.pg[r, :] = (sc * g - (sc * sc * sc) * p * total).astype(BF)

    each(PAIRS // 16, image_grad)

    @pl.when(core == 1)
    def _():
        pg_copy.start()

    class Sum:
        def __init__(self, load, count, bufs, group, devices, chunks, side):
            self.load, self.count, self.chunks = load, count, chunks
            self.out, self.back = bufs
            self.group, self.side = group, side
            n, cols = self.used, self.cols = pl.ds(0, count * 16), pl.ds(*COLUMNS[side])
            self.copies = [
                copy(self.out.at[at, :, n, cols], self.back.at[at, :, n, cols], group, side * 3 + at, to)
                for at, to in enumerate(devices)
            ]

        def begin(self):
            for at in (1, 0, 2):
                for half in (0, 1):

                    def body(i, at=at, half=half):
                        v = self.load(self.chunks[1 + at], half, i)
                        self.out[at, half, rows(i), self.cols] = v.astype(BF)

                    each(self.count, body)
                self.copies[at].start()

        def finish(self, store):
            for at in range(3):
                arrived(self.back.at[at, :, self.used, self.cols], self.group, self.side * 3 + at)
            for half in (0, 1):

                def total(i, half=half):
                    v = self.load(self.chunks[0], half, i)
                    for at in range(3):
                        v = v + self.back[at, half, rows(i), self.cols].astype(F32)
                    store(half, i, v)

                each(self.count, total)
            for c in self.copies:
                c.wait_send()

    low, high = (pl.ds(*where) for where in COLUMNS)
    bufs1, bufs2 = (s.h1send, s.h1r), (s.h2send, s.h2r)
    along_x, along_y = (xup, dev(xx=x2), xdown), (yup, dev(yy=y2), ydown)
    xs, ys = (x, x1, x2, x3), (y, y1, y2, y3)
    tall, short = ZROWS // 16, XWIN // 16
    x_first = Sum(
        lambda c, half, i: s.h[rows(lax.rem(i, 3), (half * NY + i // 3) * ZROWS + c * 32), low],
        XHALF // 16, bufs1, "h1r", along_x, xs, 0,
    )
    y_second = Sum(
        lambda c, half, i: s.h1[rows(i, (c * NZ + half) * XWIN), low],
        short, bufs2, "h2r", along_y, ys, 0,
    )
    y_first = Sum(
        lambda c, half, i: s.h[rows(i, c * YROWS + half * ZROWS), high],
        tall, bufs1, "h1r", along_y, ys, 1,
    )
    x_second = Sum(
        lambda c, half, i: s.h1[rows(i, half * ZROWS + c * 32), high],
        short, bufs2, "h2r", along_x, xs, 1,
    )

    def store(to, count, cols):
        def at(half, i, v):
            to[rows(i, half * count * 16), cols] = v

        return at

    @pl.when(core == 0)
    def _():
        arrived(s.imft, "imft")
        arrived(s.pgt, "pgt")
        s.h[...] = dot(s.imf[...], s.pg[...], TN) + dot(s.imft[...], s.pgt[...], TN)
        x_first.begin()
        y_first.begin()

    s.gip[...] = dot(s.pg[...], s.iht[...], NN)

    def image_out(i):
        s.gsend[rows(i), :] = pick(s.gip[rows(i), :], om).astype(BF)

    each(PAIRS // 16, image_out)

    for half, where in enumerate(Z_PARTS):
        arrived(s.tw.at[om, pl.ds(*where)], "tw", half)

    send(copy(s.gsend, s.grecv, "g", 0, mate))

    def merge(i):
        lo, hi = jnp.minimum(i, 6), jnp.maximum(i - 6, 0)
        v = jnp.where(i <= 6, s.tw[0, rows(lo), :].astype(F32), 0.0)
        v = v + jnp.where(i >= 6, s.tw[1, rows(hi), :].astype(F32), 0.0)
        s.tpg[rows(i), :] = v.astype(BF)

    each(PAIRS // 16, merge)

    @pl.when(core == 0)
    def _():
        tpg_copy.start()

    @pl.when(core == 1)
    def _():
        arrived(s.nhbt, "nhbt")
        arrived(s.tpgt, "tpgt")
        s.h[...] = dot(s.tpg[...], s.nhb[...], TN) + dot(s.tpgt[...], s.nhbt[...], TN)
        x_first.begin()
        y_first.begin()


    g_txt[...] = dot(s.tpg[...], s.th[...], NT)

    arrived(s.sw.at[om], "sw")
    arrived(s.u.at[om], "u")

    def text_input(i):
        r = rows(i)
        u = (s.u[0] + s.u[1])[:1, :]
        first = rowsum(s.tpg[r, :].astype(F32) * u) * (1.0 / D)
        lo, hi = jnp.minimum(i, 6), jnp.maximum(i - 6, 0)
        second = jnp.where(i <= 6, s.sw[0, rows(lo), :], 0.0) + jnp.where(i >= 6, s.sw[1, rows(hi), :], 0.0)
        second = second[:, :1] * (1.0 / D)
        g_txt[r, :] = s.rs[r, :][:, :1] * (g_txt[r, :] - first - s.nhf[r, :] * second)

    each(PAIRS // 16, text_input)

    x_first.finish(store(s.h1, XHALF // 16, low))
    y_second.begin()
    y_first.finish(store(s.h1, tall, high))
    x_second.begin()
    y_second.finish(store(s.h2, short, low))
    x_second.finish(store(s.h2, short, high))

    @pl.when(core == 0)
    def _():
        nhb_copy.wait_send()
        tpg_copy.wait_send()

    @pl.when(core == 1)
    def _():
        imf_copy.wait_send()
        pg_copy.wait_send()

    def head_far(i):
        s.h3send[rows(i), :] = s.h2[rows(i, oz * XWIN), :].astype(BF)

    each(XWIN // 16, head_far)
    send(copy(s.h3send, s.h3recv, "h3", 0, dev(zz=oz)))

    arrived(s.grecv, "g")

    def image_input(i):
        r = rows(i)
        g_img[r, :] = pick(s.gip[r, :], m) + s.grecv[r, :].astype(F32)

    each(PAIRS // 16, image_input)

    arrived(s.h3recv, "h3")

    def head_near(i):
        s.h4[rows(i), :] = s.h2[rows(i, zh * XWIN), :] + s.h3recv[rows(i), :].astype(F32)

    each(XWIN // 16, head_near)
    theirs = s.h4.at[pl.ds(pl.multiple_of(oc * 16, 16), FIN)]
    send(copy(theirs, s.finr, "fin", 0, twin))
    own = pltpu.roll(s.h4[...], lax.rem(XWIN - 4 * x - LAST * core, XWIN), 0)[:LAST, :]
    arrived(s.finr, "fin")
    got = pltpu.roll(s.finr[...], lax.rem(FIN - 4 * x - 2 * core, FIN), 0)[:LAST, :]
    g_ih[...] = jnp.where(core == 0, own, got)
    g_th[...] = jnp.where(core == 0, got, own)

    for c in sent:
        c.wait_send()


def per_device(img_feat, img_head, txt_feat, txt_head):
    vmem = pl.BlockSpec(memory_space=pltpu.VMEM)
    g_img, g_ih, g_txt, g_th = pl.pallas_call(
        kernel,
        out_shape=(
            jax.ShapeDtypeStruct((PAIRS, HALF), F32),
            jax.ShapeDtypeStruct((LAST, HALF), F32),
            jax.ShapeDtypeStruct((PAIRS, HALF), F32),
            jax.ShapeDtypeStruct((LAST, HALF), F32),
        ),
        in_specs=[pl.BlockSpec(memory_space=pl.ANY)] * 4,
        out_specs=(vmem,) * 4,
        scratch_shapes=[pltpu.VMEM(shape, kind) for shape, kind in SCRATCH.values()]
        + [pltpu.SemaphoreType.DMA((total_sends,)), pltpu.SemaphoreType.DMA((total_recvs,))]
        + [pltpu.SemaphoreType.DMA((4,))],
        compiler_params=pltpu.CompilerParams(
            collective_id=0, has_side_effects=True, vmem_limit_bytes=60 * 1024 * 1024
        ),
        cost_estimate=pl.CostEstimate(flops=14 * 10**9, bytes_accessed=5 * 10**6, transcendentals=0),
    )(img_feat, img_head.T, txt_feat, txt_head)
    return g_img, g_ih, g_txt, g_th.T


def solution(mesh):
    in_specs = (P("dp", None), P(None, "mp"), P("dp", None), P("mp", None))
    out_specs = (P("dp", "mp"), P("dp", "mp"), P("dp", "mp"), P("mp", "dp"))
    return jax.shard_map(
        per_device, mesh=mesh, in_specs=in_specs, out_specs=out_specs, check_vma=False
    )
```

```python
import types

import jax
import jax.numpy as jnp
from jax import lax
from jax.experimental import pallas as pl
from jax.experimental.pallas import tpu as pltpu
from jax.sharding import PartitionSpec as P

LOGIT_SCALE = 10.0
LOGIT_BIAS = -2.5
NORM_EPS = 1e-06

NX = 4
NY = 4
NZ = 2
NC = 2
D = 1152
HALF = D // 2
PAIRS = 208
OWN = PAIRS // 2
WIN = 112
STEP = PAIRS - WIN
TC = NZ * WIN
IMGS = NX * PAIRS
YROWS = D // NY
ZROWS = YROWS // NZ
LAST = ZROWS // (NX * NC)
XWIN = 48
XHALF = NY * NZ * XWIN // 2
FIN = 32
CUT = 64
IMAGE_PARTS = ((0, WIN), (WIN, STEP))
TEXT_PARTS = ((0, CUT), (CUT, WIN - CUT))
Z_PARTS = ((0, 32), (32, 32), (64, 48))

COLUMNS = ((0, 256), (256, HALF - 256))

NN = ((1,), (0,))
NT = ((1,), (1,))
TN = ((0,), (0,))
BF = jnp.bfloat16
F32 = jnp.float32

SCRATCH = {
    "tf": ((PAIRS, D), BF),
    "th": ((HALF, D), BF),
    "imf": ((PAIRS, D), BF),
    "iht": ((HALF, D), BF),
    "nhf": ((PAIRS, HALF), F32),
    "nhb": ((PAIRS, HALF), BF),
    "rs": ((PAIRS, 128), F32),
    "tpart": ((PAIRS, D), F32),
    "tsend": ((WIN, D), BF),
    "trecv": ((WIN, D), BF),
    "u": ((2, 8, D), F32),
    "tproj": ((WIN, D), F32),
    "tsc": ((WIN, 128), F32),
    "imh": ((NX, 2, PAIRS, HALF), BF),
    "isc": ((PAIRS, 128), F32),
    "img": ((IMGS, D), BF),
    "txt": ((NY, NC * TC, D), BF),
    "w": ((NY, IMGS, NC * TC), BF),
    "gi": ((IMGS, D), F32),
    "xsend": ((3, PAIRS, D), BF),
    "xa": ((WIN, D), BF),
    "xb": ((STEP, D), BF),
    "xr": ((2, PAIRS, D), BF),
    "gtcsend": ((NY, TC, D), BF),
    "gtcrecv": ((NY, TC, D), BF),
    "gt": ((NY, TC, D), F32),
    "gtall": ((NC * TC, D), F32),
    "ysend": ((3, TC, D), BF),
    "ya": ((NZ, CUT, D), BF),
    "yb": ((NZ, WIN - CUT, D), BF),
    "yr": ((2, TC, D), BF),
    "zsend": ((WIN, D), BF),
    "zrecv": ((WIN, D), BF),
    "gown": ((WIN, D), F32),
    "tw": ((2, WIN, D), BF),
    "sw": ((2, WIN, 128), F32),
    "tpg": ((PAIRS, D), BF),
    "ghalf": ((PAIRS, HALF), F32),
    "izsend": ((PAIRS, HALF), BF),
    "izrecv": ((PAIRS, HALF), BF),
    "dots": ((2, PAIRS, 128), F32),
    "pg": ((PAIRS, HALF), BF),
    "gip": ((PAIRS, D), F32),
    "gsend": ((PAIRS, HALF), BF),
    "grecv": ((PAIRS, HALF), BF),
    "imft": ((PAIRS, D), BF),
    "nhbt": ((PAIRS, HALF), BF),
    "pgt": ((PAIRS, HALF), BF),
    "tpgt": ((PAIRS, D), BF),
    "h": ((D, HALF), F32),
    "h1send": ((3, 2, XHALF, HALF), BF),
    "h1r": ((3, 2, XHALF, HALF), BF),
    "h1": ((2 * XHALF, HALF), F32),
    "h2send": ((3, 2, XWIN, HALF), BF),
    "h2r": ((3, 2, XWIN, HALF), BF),
    "h2": ((2 * XWIN, HALF), F32),
    "h3send": ((XWIN, HALF), BF),
    "h3recv": ((XWIN, HALF), BF),
    "h4": ((XWIN, HALF), F32),
    "finr": ((FIN, HALF), F32),
}

GROUPS = (
    ("t", 2), ("u", 1), ("img", NX * 4), ("txt", NY * NZ * 2), ("txtc", NY * NZ), ("xa", 1), ("xb", 1), ("xr", 4),
    ("iz", 1), ("dots", 1), ("gtc", NY), ("ya", 2), ("yb", 2), ("yr", 8), ("z", 3), ("tw", 3), ("sw", 1),
    ("g", 1), ("imft", 1), ("nhbt", 1), ("pgt", 1), ("tpgt", 1),
    ("h1r", 6), ("h2r", 6), ("h3", 1), ("fin", 1),
)
RECVS = {}
total_recvs = 0
for group, many in GROUPS:
    RECVS[group] = total_recvs
    total_recvs += many
total_sends = 160


def dot(a, b, dims):
    return lax.dot_general(a, b, (dims, ((), ())), preferred_element_type=F32)


def rows(i, first=0):
    return pl.ds(pl.multiple_of(first + i * 16, 16), 16)


def rowsum(v):
    return jnp.sum(v, -1, keepdims=True)


def wide(v):
    return jnp.broadcast_to(v, (v.shape[0], 128))


def each(count, body):
    lax.fori_loop(0, count, lambda i, c: (body(i), c)[1], 0)


def kernel(img_feat, img_head_t, txt_feat, txt_head, g_img, g_ih, g_txt, g_th, *scratch):
    s = types.SimpleNamespace(**dict(zip(SCRATCH, scratch)))
    ssem, rsem, lsem = scratch[len(SCRATCH) :]
    dp, m = lax.axis_index("dp"), lax.axis_index("mp")
    core = lax.rem(dp, NC)
    x = lax.rem(dp // NC, NX)
    zh = lax.rem(dp // (NC * NX), NZ)
    y = dp // (NC * NX * NZ)
    om, oc, oz = 1 - m, 1 - core, 1 - zh

    loads = [
        pltpu.make_async_copy(src, dst, lsem.at[at])
        for at, (src, dst) in enumerate(
            ((txt_feat, s.tf), (txt_head, s.th), (img_feat, s.imf), (img_head_t, s.iht))
        )
    ]
    for load in loads:
        load.start()

    def dev(yy=None, zz=None, xx=None, cc=None, mm=None):
        yy = y if yy is None else yy
        zz = zh if zz is None else zz
        xx = x if xx is None else xx
        cc = core if cc is None else cc
        mm = m if mm is None else mm
        return (((yy * NZ + zz) * NX + xx) * NC + cc, mm)

    def other(base, by, size):
        return lax.rem(base + by, size)

    x1, x2, x3 = (other(x, d, NX) for d in (1, 2, 3))
    y1, y2, y3 = (other(y, d, NY) for d in (1, 2, 3))
    mate, twin, far = dev(mm=om), dev(cc=oc), dev(zz=oz, mm=om)
    xup, xdown, yup, ydown = dev(xx=x1), dev(xx=x3), dev(yy=y1), dev(yy=y3)

    used = [0]
    sent = []

    def copy(src, dst, group, at, to):
        used[0] += 1
        return pltpu.make_async_remote_copy(
            src_ref=src,
            dst_ref=dst,
            send_sem=ssem.at[used[0] - 1],
            recv_sem=rsem.at[RECVS[group] + at],
            device_id=to,
            device_id_type=pl.DeviceIdType.MESH,
        )

    def send(c):
        c.start()
        sent.append(c)
        return c

    def arrived(ref, group, at=0):
        pltpu.make_async_remote_copy(
            src_ref=ref,
            dst_ref=ref,
            send_sem=ssem.at[0],
            recv_sem=rsem.at[RECVS[group] + at],
            device_id=twin,
            device_id_type=pl.DeviceIdType.MESH,
        ).wait_recv()

    def pick(whole, which):
        return jnp.where(which == 0, whole[:, :HALF], whole[:, HALF:])

    barrier = pltpu.get_barrier_semaphore()
    friends = [mate, twin, far, dev(zz=oz), xup, xdown, yup, ydown, dev(xx=x2), dev(yy=y2)]
    for friend in friends:
        pl.semaphore_signal(barrier, inc=1, device_id=friend, device_id_type=pl.DeviceIdType.MESH)

    loads[0].wait()

    t = s.tf[...].astype(F32)
    t = t - rowsum(t) * (1.0 / D)
    rs = lax.rsqrt(rowsum(t * t) * (1.0 / D) + NORM_EPS)
    half = pick(t * rs, m)
    s.nhf[...] = half
    s.nhb[...] = half.astype(BF)
    s.rs[...] = wide(rs)
    loads[1].wait()
    s.tpart[...] = dot(s.nhb[...], s.th[...], NN)

    def tosend(i):
        s.tsend[rows(i), :] = s.tpart[rows(i, om * STEP), :].astype(BF)

    each(WIN // 16, tosend)
    pl.semaphore_wait(barrier, len(friends))
    for half, where in enumerate(TEXT_PARTS):
        r = pl.ds(*where)
        send(copy(s.tsend.at[r], s.trecv.at[r], "t", half, mate))

    loads[2].wait()
    loads[3].wait()
    s.imh[x, m] = dot(s.imf[...], s.iht[...], NT).astype(BF)

    def image_part(xx, half, cut):
        if cut is None:
            return s.imh.at[xx, half]
        return s.imh.at[xx, half, pl.ds(*IMAGE_PARTS[cut])]

    def send_image(xx, half, to, cut=None):
        ref = image_part(xx, half, cut)
        send(copy(ref, ref, "img", xx * 4 + half * 2 + (cut or 0), to))

    def image_arrived(xx, half, cut=None):
        arrived(image_part(xx, half, cut), "img", xx * 4 + half * 2 + (cut or 0))

    def forward_image(half):
        image_arrived(x1, half)
        send_image(x1, half, xdown, 0)
        image_arrived(x3, half)
        send_image(x3, half, xup, 1)

    for to in (mate, xup, xdown):
        send_image(x, m, to)
    s.u[m] = dot(jnp.ones((8, HALF), BF), s.th[...], NN)
    send(copy(s.u.at[m], s.u.at[m], "u", 0, mate))

    nhb_copy = copy(s.nhb, s.nhbt, "nhbt", 0, twin)
    imf_copy = copy(s.imf, s.imft, "imft", 0, twin)
    pg_copy = copy(s.pg, s.pgt, "pgt", 0, twin)
    tpg_copy = copy(s.tpg, s.tpgt, "tpgt", 0, twin)

    @pl.when(core == 0)
    def _():
        nhb_copy.start()

    @pl.when(core == 1)
    def _():
        imf_copy.start()


    def own_rows(first, count):
        row = m * STEP + first + lax.broadcasted_iota(jnp.int32, (count, 1), 0)
        return (row >= m * OWN) & (row < m * OWN + OWN)

    def at16(first, count):
        return pl.ds(pl.multiple_of(first, 16), count)

    def embed_text(first, count):
        r = pl.ds(first, count)
        p = s.tpart[at16(m * STEP + first, count), :] + s.trecv[r, :].astype(F32)
        sc = lax.rsqrt(rowsum(p * p) + NORM_EPS)
        s.tproj[r, :] = p
        s.tsc[r, :] = wide(sc)
        emb = jnp.where(own_rows(first, count), p * sc, 0.0).astype(BF)
        s.txt[y, at16(core * TC + zh * WIN + first, count), :] = emb

    def part(yy, zz, cut=None):
        first, count = (0, WIN) if cut is None else TEXT_PARTS[cut]
        return s.txt.at[yy, pl.ds(pl.multiple_of(core * TC + zz * WIN + first, 16), count)]

    def send_text(yy, zz, to, cut=None):
        ref = part(yy, zz, cut)
        send(copy(ref, ref, "txt", yy * 4 + zz * 2 + (cut or 0), to))

    def text_arrived(yy, zz, cut=None):
        arrived(part(yy, zz, cut), "txt", yy * 4 + zz * 2 + (cut or 0))

    def forward_text(zz):
        text_arrived(y1, zz, 0)
        send_text(y1, zz, ydown, 0)
        text_arrived(y3, zz, 0)
        text_arrived(y3, zz, 1)
        send_text(y3, zz, yup, 1)
        send_twin(y3, zz)
        text_arrived(y1, zz, 1)
        send_twin(y1, zz)

    def side_part(yy, cc, zz):
        return s.txt.at[yy, pl.ds(pl.multiple_of(cc * TC + zz * WIN, 16), WIN)]

    def send_twin(yy, zz):
        send(copy(part(yy, zz), part(yy, zz), "txtc", yy * NZ + zz, twin))

    def twin_arrived(yy):
        for zz in range(NZ):
            arrived(side_part(yy, oc, zz), "txtc", yy * NZ + zz)

    for half, (first, count) in enumerate(TEXT_PARTS):
        arrived(s.trecv.at[pl.ds(first, count)], "t", half)
        embed_text(first, count)
        for to in (far, yup, ydown):
            send_text(y, zh, to, half)
    send_twin(y, zh)

    def zero(i):
        s.gi[rows(i), :] = jnp.zeros((16, D), F32)

    each(IMGS // 16, zero)
    forward_image(m)

    image_arrived(x, om)
    send_image(x, om, xup)
    send_image(x, om, xdown)

    def embed_images(xx, at, own=False):
        p = jnp.concatenate([s.imh[xx, 0].astype(F32), s.imh[xx, 1].astype(F32)], axis=1)
        sc = lax.rsqrt(rowsum(p * p) + NORM_EPS)
        if own:
            s.isc[...] = wide(sc)
        s.img[pl.ds(at * PAIRS, PAIRS), :] = (p * sc).astype(BF)

    embed_images(x, 0, own=True)

    for half in (0, 1):
        text_arrived(y, oz, half)
        send_text(y, oz, yup, half)
        send_text(y, oz, ydown, half)
    send_twin(y, oz)
    forward_text(zh)

    def unit(yy, first, count, own=False):
        r = pl.ds(first, count)
        texts = s.txt[yy]
        scores = dot(s.img[r, :], texts, NT)
        weights = 0.5 + 0.5 * jnp.tanh((0.5 * LOGIT_SCALE) * scores + 0.5 * LOGIT_BIAS)
        if own:
            row = lax.broadcasted_iota(jnp.int32, (count, NC * TC), 0)
            col = lax.broadcasted_iota(jnp.int32, (count, NC * TC), 1)
            at = core * TC + zh * WIN
            match = (row - col == m * STEP - at) & (col >= at) & (col < at + WIN)
            weights = weights - match.astype(F32)
        weights = weights.astype(BF)
        s.w[yy, r, :] = weights
        s.gi[r, :] += dot(weights, texts, NN)

    forward_image(om)
    forward_text(oz)
    embed_images(x1, 1)
    embed_images(x3, 2)
    twin_arrived(y)
    unit(y, 0, 3 * PAIRS, own=True)
    twin_arrived(y1)
    unit(y1, 0, 3 * PAIRS)
    twin_arrived(y3)
    unit(y3, 0, 3 * PAIRS)
    for zz in (zh, oz):
        for half in (0, 1):
            text_arrived(y2, zz, half)
        send_twin(y2, zz)
    for half in (0, 1):
        for cut in (0, 1):
            image_arrived(x2, half, cut)
    embed_images(x2, 3)
    each(3, lambda i: unit(other(y, i + i // 2, NY), 3 * PAIRS, PAIRS))

    twin_arrived(y2)
    unit(y2, 2 * PAIRS, 2 * PAIRS)

    def cast(at, place, add=None, first=0, count=PAIRS):
        def body(i):
            v = s.gi[rows(i, place * PAIRS + first), :]
            if add is not None:
                v = v + add[rows(i), :].astype(F32)
            s.xsend[at, rows(i, first), :] = v.astype(BF)

        each(count // 16, body)

    for half in (0, 1):
        first, count = IMAGE_PARTS[half]
        cast(0, 3, first=first, count=count)
        to, at = ((xup, s.xa), (xdown, s.xb))[half]
        send(copy(s.xsend.at[0, pl.ds(first, count)], at, ("xa", "xb")[half], 0, to))

    def image_back(at, place, half, to, add=None):
        first, count = IMAGE_PARTS[half]
        cast(at, place, add=add, first=first, count=count)
        r = pl.ds(first, count)
        send(copy(s.xsend.at[at, r], s.xr.at[at - 1, r], "xr", (at - 1) * 2 + half, to))

    image_back(2, 2, 0, xdown)
    unit(y2, 0, 2 * PAIRS)
    image_back(1, 1, 1, xup)

    def text_grad(yy):
        s.gtall[...] = dot(s.w[yy], s.img[...], TN)

        def out(i):
            s.gtcsend[yy, rows(i), :] = s.gtall[rows(i, oc * TC), :].astype(BF)
            s.gt[yy, rows(i), :] = s.gtall[rows(i, core * TC), :]

        each(TC // 16, out)

    def send_back_twin(yy):
        send(copy(s.gtcsend.at[yy], s.gtcrecv.at[yy], "gtc", yy, twin))

    def back_twin_arrived(yy):
        arrived(s.gtcrecv.at[yy], "gtc", yy)

    def columns_of(cc):
        return s.w[y2, :, pl.ds(cc * TC, TC)]

    @pl.when(core == 0)
    def _():
        s.gtcsend[y2] = dot(columns_of(1), s.img[...], TN).astype(BF)

    @pl.when(core == 1)
    def _():
        s.gtcsend[y2] = dot(columns_of(0), s.img[...], TN).astype(BF)

    send_back_twin(y2)

    @pl.when(core == 0)
    def _():
        s.gt[y2] = dot(columns_of(0), s.img[...], TN)

    @pl.when(core == 1)
    def _():
        s.gt[y2] = dot(columns_of(1), s.img[...], TN)

    text_grad(y1)
    send_back_twin(y1)
    back_twin_arrived(y2)

    def text_back(at, yy, zz, half, dst, group, index, to, add=None):
        first, count = TEXT_PARTS[half]

        def body(i):
            r = rows(i, zz * WIN + first)
            v = s.gt[yy, r, :] + s.gtcrecv[yy, r, :].astype(F32)
            if add is not None:
                v = v + add[zz, rows(i), :].astype(F32)
            s.ysend[at, r, :] = v.astype(BF)

        each(count // 16, body)
        r = pl.ds(pl.multiple_of(zz * WIN + first, 16), count)
        send(copy(s.ysend.at[at, r], dst(r), group, index, to))

    def text_back_to(at, yy, zz, half, to, add=None):
        text_back(at, yy, zz, half, lambda r: s.yr.at[at - 1, r], "yr", (at - 1) * 4 + zz * 2 + half, to, add)

    for zz in (oz, zh):
        text_back(0, y2, zz, 0, lambda r, zz=zz: s.ya.at[zz], "ya", zz, yup)
        text_back(0, y2, zz, 1, lambda r, zz=zz: s.yb.at[zz], "yb", zz, ydown)
    text_grad(y3)
    send_back_twin(y3)
    back_twin_arrived(y1)
    for zz in (oz, zh):
        text_back_to(1, y1, zz, 1, yup)
    back_twin_arrived(y3)
    for zz in (oz, zh):
        text_back_to(2, y3, zz, 0, ydown)
    arrived(s.xa, "xa")
    image_back(1, 1, 0, xup, add=s.xa)
    arrived(s.xb, "xb")
    image_back(2, 2, 1, xdown, add=s.xb)
    text_grad(y)
    send_back_twin(y)
    for zz in (oz, zh):
        arrived(s.ya.at[zz], "ya", zz)
        text_back_to(1, y1, zz, 0, yup, add=s.ya)
        arrived(s.yb.at[zz], "yb", zz)
        text_back_to(2, y3, zz, 1, ydown, add=s.yb)
    back_twin_arrived(y)

    for way in (0, 1):
        for half in (0, 1):
            arrived(s.xr.at[way, pl.ds(*IMAGE_PARTS[half])], "xr", way * 2 + half)

    g = s.gi[pl.ds(0, PAIRS), :] + s.xr[0].astype(F32) + s.xr[1].astype(F32)
    g = LOGIT_SCALE * g
    p = jnp.concatenate([s.imh[x, 0].astype(F32), s.imh[x, 1].astype(F32)], axis=1)
    s.dots[m] = wide(rowsum(g * p))
    s.ghalf[...] = pick(g, m)
    s.izsend[...] = pick(g, om).astype(BF)
    send(copy(s.dots.at[m], s.dots.at[m], "dots", 0, mate))
    send(copy(s.izsend, s.izrecv, "iz", 0, mate))

    def back_arrived(zz):
        for way in (0, 1):
            for half in (0, 1):
                first, count = TEXT_PARTS[half]
                r = pl.ds(pl.multiple_of(zz * WIN + first, 16), count)
                arrived(s.yr.at[way, r], "yr", way * 4 + zz * 2 + half)

    def text_sum(r):
        g = s.gt[y, r, :] + s.gtcrecv[y, r, :].astype(F32)
        return g + s.yr[0, r, :].astype(F32) + s.yr[1, r, :].astype(F32)

    def text_far(i):
        s.zsend[rows(i), :] = text_sum(rows(i, oz * WIN)).astype(BF)

    back_arrived(oz)
    for half, (first, count) in enumerate(Z_PARTS):
        each(count // 16, lambda i, first=first: text_far(i + first // 16))
        r = pl.ds(first, count)
        send(copy(s.zsend.at[r], s.zrecv.at[r], "z", half, far))
    back_arrived(zh)

    def text_near(i):
        s.gown[rows(i), :] = text_sum(rows(i, zh * WIN))

    each(WIN // 16, text_near)


    def text_own(first, count):
        r = pl.ds(first, count)
        g = LOGIT_SCALE * (s.gown[r, :] + s.zrecv[r, :].astype(F32))
        p = s.tproj[r, :]
        sc = s.tsc[r, :][:, :1]
        v = sc * g - (sc * sc * sc) * p * rowsum(p * g)
        v = jnp.where(own_rows(first, count), v, 0.0).astype(BF)
        s.tw[m, r, :] = v
        s.sw[m, r, :] = wide(rowsum(v.astype(F32) * p))

    for half, (first, count) in enumerate(Z_PARTS):
        r = pl.ds(first, count)
        arrived(s.zrecv.at[r], "z", half)
        text_own(first, count)
        send(copy(s.tw.at[m, r], s.tw.at[m, r], "tw", half, mate))
    send(copy(s.sw.at[m], s.sw.at[m], "sw", 0, mate))

    arrived(s.dots.at[om], "dots")
    arrived(s.izrecv, "iz")

    g = s.ghalf[...] + s.izrecv[...].astype(F32)
    sc = s.isc[...][:, :1]
    total = (s.dots[0] + s.dots[1])[:, :1]
    p = s.imh[x, m].astype(F32)
    s.pg[...] = (sc * g - (sc * sc * sc) * p * total).astype(BF)

    @pl.when(core == 1)
    def _():
        pg_copy.start()

    class Sum:
        def __init__(self, load, count, bufs, group, devices, chunks, side):
            self.load, self.count, self.chunks = load, count, chunks
            self.out, self.back = bufs
            self.group, self.side = group, side
            n, cols = self.used, self.cols = pl.ds(0, count * 16), pl.ds(*COLUMNS[side])
            self.copies = [
                copy(self.out.at[at, :, n, cols], self.back.at[at, :, n, cols], group, side * 3 + at, to)
                for at, to in enumerate(devices)
            ]

        def begin(self):
            for at in (1, 0, 2):
                for half in (0, 1):

                    def body(i, at=at, half=half):
                        v = self.load(self.chunks[1 + at], half, i)
                        self.out[at, half, rows(i), self.cols] = v.astype(BF)

                    each(self.count, body)
                self.copies[at].start()

        def finish(self, store):
            for at in range(3):
                arrived(self.back.at[at, :, self.used, self.cols], self.group, self.side * 3 + at)
            for half in (0, 1):

                def total(i, half=half):
                    v = self.load(self.chunks[0], half, i)
                    for at in range(3):
                        v = v + self.back[at, half, rows(i), self.cols].astype(F32)
                    store(half, i, v)

                each(self.count, total)
            for c in self.copies:
                c.wait_send()

    low, high = (pl.ds(*where) for where in COLUMNS)
    bufs1, bufs2 = (s.h1send, s.h1r), (s.h2send, s.h2r)
    along_x, along_y = (xup, dev(xx=x2), xdown), (yup, dev(yy=y2), ydown)
    xs, ys = (x, x1, x2, x3), (y, y1, y2, y3)
    tall, short = ZROWS // 16, XWIN // 16
    x_first = Sum(
        lambda c, half, i: s.h[rows(lax.rem(i, 3), (half * NY + i // 3) * ZROWS + c * 32), low],
        XHALF // 16, bufs1, "h1r", along_x, xs, 0,
    )
    y_second = Sum(
        lambda c, half, i: s.h1[rows(i, (c * NZ + half) * XWIN), low],
        short, bufs2, "h2r", along_y, ys, 0,
    )
    y_first = Sum(
        lambda c, half, i: s.h[rows(i, c * YROWS + half * ZROWS), high],
        tall, bufs1, "h1r", along_y, ys, 1,
    )
    x_second = Sum(
        lambda c, half, i: s.h1[rows(i, half * ZROWS + c * 32), high],
        short, bufs2, "h2r", along_x, xs, 1,
    )

    def store(to, count, cols):
        def at(half, i, v):
            to[rows(i, half * count * 16), cols] = v

        return at

    @pl.when(core == 0)
    def _():
        arrived(s.imft, "imft")
        arrived(s.pgt, "pgt")
        s.h[...] = dot(s.imf[...], s.pg[...], TN) + dot(s.imft[...], s.pgt[...], TN)
        x_first.begin()
        y_first.begin()

    s.gip[...] = dot(s.pg[...], s.iht[...], NN)

    def image_out(i):
        s.gsend[rows(i), :] = pick(s.gip[rows(i), :], om).astype(BF)

    each(PAIRS // 16, image_out)

    for half, where in enumerate(Z_PARTS):
        arrived(s.tw.at[om, pl.ds(*where)], "tw", half)

    send(copy(s.gsend, s.grecv, "g", 0, mate))

    def merged(a, b):
        a, b = a.astype(F32), b.astype(F32)
        both = a[STEP:, :] + b[: WIN - STEP, :]
        return jnp.concatenate([a[:STEP, :], both, b[WIN - STEP :, :]], axis=0)

    s.tpg[...] = merged(s.tw[0], s.tw[1]).astype(BF)

    @pl.when(core == 0)
    def _():
        tpg_copy.start()

    @pl.when(core == 1)
    def _():
        arrived(s.nhbt, "nhbt")
        arrived(s.tpgt, "tpgt")
        s.h[...] = dot(s.tpg[...], s.nhb[...], TN) + dot(s.tpgt[...], s.nhbt[...], TN)
        x_first.begin()
        y_first.begin()


    g_txt[...] = dot(s.tpg[...], s.th[...], NT)

    arrived(s.sw.at[om], "sw")
    arrived(s.u.at[om], "u")

    u = (s.u[0] + s.u[1])[:1, :]
    mean = rowsum(s.tpg[...].astype(F32) * u) * (1.0 / D)
    product = merged(s.sw[0], s.sw[1])[:, :1] * (1.0 / D)
    g_txt[...] = s.rs[...][:, :1] * (g_txt[...] - mean - s.nhf[...] * product)

    x_first.finish(store(s.h1, XHALF // 16, low))
    y_second.begin()
    y_first.finish(store(s.h1, tall, high))
    x_second.begin()
    y_second.finish(store(s.h2, short, low))
    x_second.finish(store(s.h2, short, high))

    @pl.when(core == 0)
    def _():
        nhb_copy.wait_send()
        tpg_copy.wait_send()

    @pl.when(core == 1)
    def _():
        imf_copy.wait_send()
        pg_copy.wait_send()

    def head_far(i):
        s.h3send[rows(i), :] = s.h2[rows(i, oz * XWIN), :].astype(BF)

    each(XWIN // 16, head_far)
    send(copy(s.h3send, s.h3recv, "h3", 0, dev(zz=oz)))

    arrived(s.grecv, "g")

    def image_input(i):
        r = rows(i)
        g_img[r, :] = pick(s.gip[r, :], m) + s.grecv[r, :].astype(F32)

    each(PAIRS // 16, image_input)

    arrived(s.h3recv, "h3")

    def head_near(i):
        s.h4[rows(i), :] = s.h2[rows(i, zh * XWIN), :] + s.h3recv[rows(i), :].astype(F32)

    each(XWIN // 16, head_near)
    theirs = s.h4.at[pl.ds(pl.multiple_of(oc * 16, 16), FIN)]
    send(copy(theirs, s.finr, "fin", 0, twin))
    own = pltpu.roll(s.h4[...], lax.rem(XWIN - 4 * x - LAST * core, XWIN), 0)[:LAST, :]
    arrived(s.finr, "fin")
    got = pltpu.roll(s.finr[...], lax.rem(FIN - 4 * x - 2 * core, FIN), 0)[:LAST, :]
    g_ih[...] = jnp.where(core == 0, own, got)
    g_th[...] = jnp.where(core == 0, got, own)

    for c in sent:
        c.wait_send()


def per_device(img_feat, img_head, txt_feat, txt_head):
    vmem = pl.BlockSpec(memory_space=pltpu.VMEM)
    g_img, g_ih, g_txt, g_th = pl.pallas_call(
        kernel,
        out_shape=(
            jax.ShapeDtypeStruct((PAIRS, HALF), F32),
            jax.ShapeDtypeStruct((LAST, HALF), F32),
            jax.ShapeDtypeStruct((PAIRS, HALF), F32),
            jax.ShapeDtypeStruct((LAST, HALF), F32),
        ),
        in_specs=[pl.BlockSpec(memory_space=pl.ANY)] * 4,
        out_specs=(vmem,) * 4,
        scratch_shapes=[pltpu.VMEM(shape, kind) for shape, kind in SCRATCH.values()]
        + [pltpu.SemaphoreType.DMA((total_sends,)), pltpu.SemaphoreType.DMA((total_recvs,))]
        + [pltpu.SemaphoreType.DMA((4,))],
        compiler_params=pltpu.CompilerParams(
            collective_id=0, has_side_effects=True, vmem_limit_bytes=60 * 1024 * 1024
        ),
        cost_estimate=pl.CostEstimate(flops=14 * 10**9, bytes_accessed=5 * 10**6, transcendentals=0),
    )(img_feat, img_head.T, txt_feat, txt_head)
    return g_img, g_ih, g_txt, g_th.T


def solution(mesh):
    in_specs = (P("dp", None), P(None, "mp"), P("dp", None), P("mp", None))
    out_specs = (P("dp", "mp"), P("dp", "mp"), P("dp", "mp"), P("mp", "dp"))
    return jax.shard_map(
        per_device, mesh=mesh, in_specs=in_specs, out_specs=out_specs, check_vma=False
    )
```

```python
import types

import jax
import jax.numpy as jnp
from jax import lax
from jax.experimental import pallas as pl
from jax.experimental.pallas import tpu as pltpu
from jax.sharding import PartitionSpec as P

LOGIT_SCALE = 10.0
LOGIT_BIAS = -2.5
NORM_EPS = 1e-06

NX = 4
NY = 4
NZ = 2
NC = 2
D = 1152
HALF = D // 2
PAIRS = 208
OWN = PAIRS // 2
WIN = 112
STEP = PAIRS - WIN
TC = NZ * WIN
IMGS = NX * PAIRS
YROWS = D // NY
ZROWS = YROWS // NZ
LAST = ZROWS // (NX * NC)
XWIN = 48
XHALF = NY * NZ * XWIN // 2
FIN = 32
CUT = 64
IMAGE_PARTS = ((0, WIN), (WIN, STEP))
TEXT_PARTS = ((0, CUT), (CUT, WIN - CUT))
Z_PARTS = ((0, 32), (32, 32), (64, 48))

COLUMNS = ((0, 256), (256, HALF - 256))

NN = ((1,), (0,))
NT = ((1,), (1,))
TN = ((0,), (0,))
BF = jnp.bfloat16
F32 = jnp.float32

SCRATCH = {
    "tf": ((PAIRS, D), BF),
    "th": ((HALF, D), BF),
    "imf": ((PAIRS, D), BF),
    "iht": ((HALF, D), BF),
    "nhf": ((PAIRS, HALF), F32),
    "nhb": ((PAIRS, HALF), BF),
    "rs": ((PAIRS, 128), F32),
    "tpart": ((PAIRS, D), F32),
    "tsend": ((WIN, D), BF),
    "trecv": ((WIN, D), BF),
    "u": ((2, 8, D), F32),
    "tproj": ((WIN, D), F32),
    "tsc": ((WIN, 128), F32),
    "imh": ((NX, 2, PAIRS, HALF), BF),
    "isc": ((PAIRS, 128), F32),
    "img": ((IMGS, D), BF),
    "txt": ((NY, NC * TC, D), BF),
    "w": ((NY, IMGS, NC * TC), BF),
    "gi": ((IMGS, D), F32),
    "xsend": ((3, PAIRS, D), BF),
    "xa": ((WIN, D), BF),
    "xb": ((STEP, D), BF),
    "xr": ((2, PAIRS, D), BF),
    "gtcsend": ((NY, TC, D), BF),
    "gtcrecv": ((NY, TC, D), BF),
    "gt": ((NY, TC, D), F32),
    "gtall": ((NC * TC, D), F32),
    "ysend": ((3, TC, D), BF),
    "ya": ((NZ, CUT, D), BF),
    "yb": ((NZ, WIN - CUT, D), BF),
    "yr": ((2, TC, D), BF),
    "zsend": ((WIN, D), BF),
    "zrecv": ((WIN, D), BF),
    "gown": ((WIN, D), F32),
    "tw": ((2, WIN, D), BF),
    "sw": ((2, WIN, 128), F32),
    "tpg": ((PAIRS, D), BF),
    "ghalf": ((PAIRS, HALF), F32),
    "izsend": ((PAIRS, HALF), BF),
    "izrecv": ((PAIRS, HALF), BF),
    "dots": ((2, PAIRS, 128), F32),
    "pg": ((PAIRS, HALF), BF),
    "gip": ((PAIRS, D), F32),
    "gsend": ((PAIRS, HALF), BF),
    "grecv": ((PAIRS, HALF), BF),
    "imft": ((PAIRS, D), BF),
    "nhbt": ((PAIRS, HALF), BF),
    "pgt": ((PAIRS, HALF), BF),
    "tpgt": ((PAIRS, D), BF),
    "h": ((NY * NZ, ZROWS, HALF), F32),
    "h1send": ((3, 2, XHALF, HALF), BF),
    "h1r": ((3, 2, XHALF, HALF), BF),
    "h1": ((2 * XHALF, HALF), F32),
    "h2send": ((3, 2, XWIN, HALF), BF),
    "h2r": ((3, 2, XWIN, HALF), BF),
    "h2": ((2 * XWIN, HALF), F32),
    "h3send": ((XWIN, HALF), BF),
    "h3recv": ((XWIN, HALF), BF),
    "h4": ((XWIN, HALF), F32),
    "finr": ((FIN, HALF), F32),
}

GROUPS = (
    ("t", 2), ("u", 1), ("img", NX * 4), ("txt", NY * NZ * 2), ("txtc", NY * NZ), ("xa", 1), ("xb", 1), ("xr", 4),
    ("iz", 1), ("dots", 1), ("gtc", NY), ("ya", 2), ("yb", 2), ("yr", 8), ("z", 3), ("tw", 3), ("sw", 1),
    ("g", 1), ("imft", 1), ("nhbt", 1), ("pgt", 1), ("tpgt", 1),
    ("h1r", 6), ("h2r", 6), ("h3", 1), ("fin", 1),
)
RECVS = {}
total_recvs = 0
for group, many in GROUPS:
    RECVS[group] = total_recvs
    total_recvs += many
total_sends = 160


def dot(a, b, dims):
    return lax.dot_general(a, b, (dims, ((), ())), preferred_element_type=F32)


def rows(i, first=0):
    return pl.ds(pl.multiple_of(first + i * 16, 16), 16)


def rowsum(v):
    return jnp.sum(v, -1, keepdims=True)


def wide(v):
    return jnp.broadcast_to(v, (v.shape[0], 128))


def each(count, body):
    lax.fori_loop(0, count, lambda i, c: (body(i), c)[1], 0)


def kernel(img_feat, img_head_t, txt_feat, txt_head, g_img, g_ih, g_txt, g_th, *scratch):
    s = types.SimpleNamespace(**dict(zip(SCRATCH, scratch)))
    ssem, rsem, lsem = scratch[len(SCRATCH) :]
    dp, m = lax.axis_index("dp"), lax.axis_index("mp")
    core = lax.rem(dp, NC)
    x = lax.rem(dp // NC, NX)
    zh = lax.rem(dp // (NC * NX), NZ)
    y = dp // (NC * NX * NZ)
    om, oc, oz = 1 - m, 1 - core, 1 - zh

    loads = [
        pltpu.make_async_copy(src, dst, lsem.at[at])
        for at, (src, dst) in enumerate(
            ((txt_feat, s.tf), (txt_head, s.th), (img_feat, s.imf), (img_head_t, s.iht))
        )
    ]
    for load in loads:
        load.start()

    def dev(yy=None, zz=None, xx=None, cc=None, mm=None):
        yy = y if yy is None else yy
        zz = zh if zz is None else zz
        xx = x if xx is None else xx
        cc = core if cc is None else cc
        mm = m if mm is None else mm
        return (((yy * NZ + zz) * NX + xx) * NC + cc, mm)

    def other(base, by, size):
        return lax.rem(base + by, size)

    x1, x2, x3 = (other(x, d, NX) for d in (1, 2, 3))
    y1, y2, y3 = (other(y, d, NY) for d in (1, 2, 3))
    mate, twin, far = dev(mm=om), dev(cc=oc), dev(zz=oz, mm=om)
    xup, xdown, yup, ydown = dev(xx=x1), dev(xx=x3), dev(yy=y1), dev(yy=y3)

    used = [0]
    sent = []

    def copy(src, dst, group, at, to):
        used[0] += 1
        return pltpu.make_async_remote_copy(
            src_ref=src,
            dst_ref=dst,
            send_sem=ssem.at[used[0] - 1],
            recv_sem=rsem.at[RECVS[group] + at],
            device_id=to,
            device_id_type=pl.DeviceIdType.MESH,
        )

    def send(c):
        c.start()
        sent.append(c)
        return c

    def arrived(ref, group, at=0):
        pltpu.make_async_remote_copy(
            src_ref=ref,
            dst_ref=ref,
            send_sem=ssem.at[0],
            recv_sem=rsem.at[RECVS[group] + at],
            device_id=twin,
            device_id_type=pl.DeviceIdType.MESH,
        ).wait_recv()

    def pick(whole, which):
        return jnp.where(which == 0, whole[:, :HALF], whole[:, HALF:])

    barrier = pltpu.get_barrier_semaphore()
    friends = [mate, twin, far, dev(zz=oz), xup, xdown, yup, ydown, dev(xx=x2), dev(yy=y2)]
    for friend in friends:
        pl.semaphore_signal(barrier, inc=1, device_id=friend, device_id_type=pl.DeviceIdType.MESH)

    loads[0].wait()

    t = s.tf[...].astype(F32)
    t = t - rowsum(t) * (1.0 / D)
    rs = lax.rsqrt(rowsum(t * t) * (1.0 / D) + NORM_EPS)
    half = pick(t * rs, m)
    s.nhf[...] = half
    s.nhb[...] = half.astype(BF)
    s.rs[...] = wide(rs)
    loads[1].wait()
    s.tpart[...] = dot(s.nhb[...], s.th[...], NN)

    def tosend(i):
        s.tsend[rows(i), :] = s.tpart[rows(i, om * STEP), :].astype(BF)

    each(WIN // 16, tosend)
    pl.semaphore_wait(barrier, len(friends))
    for half, where in enumerate(TEXT_PARTS):
        r = pl.ds(*where)
        send(copy(s.tsend.at[r], s.trecv.at[r], "t", half, mate))

    loads[2].wait()
    loads[3].wait()
    s.imh[x, m] = dot(s.imf[...], s.iht[...], NT).astype(BF)

    def image_part(xx, half, cut):
        if cut is None:
            return s.imh.at[xx, half]
        return s.imh.at[xx, half, pl.ds(*IMAGE_PARTS[cut])]

    def send_image(xx, half, to, cut=None):
        ref = image_part(xx, half, cut)
        send(copy(ref, ref, "img", xx * 4 + half * 2 + (cut or 0), to))

    def image_arrived(xx, half, cut=None):
        arrived(image_part(xx, half, cut), "img", xx * 4 + half * 2 + (cut or 0))

    def forward_image(half):
        image_arrived(x1, half)
        send_image(x1, half, xdown, 0)
        image_arrived(x3, half)
        send_image(x3, half, xup, 1)

    for to in (mate, xup, xdown):
        send_image(x, m, to)
    s.u[m] = dot(jnp.ones((8, HALF), BF), s.th[...], NN)
    send(copy(s.u.at[m], s.u.at[m], "u", 0, mate))

    nhb_copy = copy(s.nhb, s.nhbt, "nhbt", 0, twin)
    imf_copy = copy(s.imf, s.imft, "imft", 0, twin)
    pg_copy = copy(s.pg, s.pgt, "pgt", 0, twin)
    tpg_copy = copy(s.tpg, s.tpgt, "tpgt", 0, twin)

    @pl.when(core == 0)
    def _():
        nhb_copy.start()

    @pl.when(core == 1)
    def _():
        imf_copy.start()


    def own_rows(first, count):
        row = m * STEP + first + lax.broadcasted_iota(jnp.int32, (count, 1), 0)
        return (row >= m * OWN) & (row < m * OWN + OWN)

    def at16(first, count):
        return pl.ds(pl.multiple_of(first, 16), count)

    def embed_text(first, count):
        r = pl.ds(first, count)
        p = s.tpart[at16(m * STEP + first, count), :] + s.trecv[r, :].astype(F32)
        sc = lax.rsqrt(rowsum(p * p) + NORM_EPS)
        s.tproj[r, :] = p
        s.tsc[r, :] = wide(sc)
        emb = jnp.where(own_rows(first, count), p * sc, 0.0).astype(BF)
        s.txt[y, at16(core * TC + zh * WIN + first, count), :] = emb

    def part(yy, zz, cut=None):
        first, count = (0, WIN) if cut is None else TEXT_PARTS[cut]
        return s.txt.at[yy, pl.ds(pl.multiple_of(core * TC + zz * WIN + first, 16), count)]

    def send_text(yy, zz, to, cut=None):
        ref = part(yy, zz, cut)
        send(copy(ref, ref, "txt", yy * 4 + zz * 2 + (cut or 0), to))

    def text_arrived(yy, zz, cut=None):
        arrived(part(yy, zz, cut), "txt", yy * 4 + zz * 2 + (cut or 0))

    def forward_text(zz):
        text_arrived(y1, zz, 0)
        send_text(y1, zz, ydown, 0)
        text_arrived(y3, zz, 0)
        text_arrived(y3, zz, 1)
        send_text(y3, zz, yup, 1)
        send_twin(y3, zz)
        text_arrived(y1, zz, 1)
        send_twin(y1, zz)

    def side_part(yy, cc, zz):
        return s.txt.at[yy, pl.ds(pl.multiple_of(cc * TC + zz * WIN, 16), WIN)]

    def send_twin(yy, zz):
        send(copy(part(yy, zz), part(yy, zz), "txtc", yy * NZ + zz, twin))

    def twin_arrived(yy):
        for zz in range(NZ):
            arrived(side_part(yy, oc, zz), "txtc", yy * NZ + zz)

    for half, (first, count) in enumerate(TEXT_PARTS):
        arrived(s.trecv.at[pl.ds(first, count)], "t", half)
        embed_text(first, count)
        for to in (far, yup, ydown):
            send_text(y, zh, to, half)
    send_twin(y, zh)

    def zero(i):
        s.gi[rows(i), :] = jnp.zeros((16, D), F32)

    each(IMGS // 16, zero)
    forward_image(m)

    image_arrived(x, om)
    send_image(x, om, xup)
    send_image(x, om, xdown)

    def embed_images(xx, at, own=False):
        p = jnp.concatenate([s.imh[xx, 0].astype(F32), s.imh[xx, 1].astype(F32)], axis=1)
        sc = lax.rsqrt(rowsum(p * p) + NORM_EPS)
        if own:
            s.isc[...] = wide(sc)
        s.img[pl.ds(at * PAIRS, PAIRS), :] = (p * sc).astype(BF)

    embed_images(x, 0, own=True)

    for half in (0, 1):
        text_arrived(y, oz, half)
        send_text(y, oz, yup, half)
        send_text(y, oz, ydown, half)
    send_twin(y, oz)
    forward_text(zh)

    def unit(yy, first, count, own=False):
        r = pl.ds(first, count)
        texts = s.txt[yy]
        scores = dot(s.img[r, :], texts, NT)
        weights = 0.5 + 0.5 * jnp.tanh((0.5 * LOGIT_SCALE) * scores + 0.5 * LOGIT_BIAS)
        if own:
            row = lax.broadcasted_iota(jnp.int32, (count, NC * TC), 0)
            col = lax.broadcasted_iota(jnp.int32, (count, NC * TC), 1)
            at = core * TC + zh * WIN
            match = (row - col == m * STEP - at) & (col >= at) & (col < at + WIN)
            weights = weights - match.astype(F32)
        weights = weights.astype(BF)
        s.w[yy, r, :] = weights
        s.gi[r, :] += dot(weights, texts, NN)

    forward_image(om)
    forward_text(oz)
    embed_images(x1, 1)
    embed_images(x3, 2)
    twin_arrived(y)
    unit(y, 0, 3 * PAIRS, own=True)
    twin_arrived(y1)
    unit(y1, 0, 3 * PAIRS)
    twin_arrived(y3)
    unit(y3, 0, 3 * PAIRS)
    for zz in (zh, oz):
        for half in (0, 1):
            text_arrived(y2, zz, half)
        send_twin(y2, zz)
    for half in (0, 1):
        for cut in (0, 1):
            image_arrived(x2, half, cut)
    embed_images(x2, 3)
    each(3, lambda i: unit(other(y, i + i // 2, NY), 3 * PAIRS, PAIRS))

    twin_arrived(y2)
    unit(y2, 2 * PAIRS, 2 * PAIRS)

    def cast(at, place, add=None, first=0, count=PAIRS):
        v = s.gi[pl.ds(place * PAIRS + first, count), :]
        if add is not None:
            v = v + add[...].astype(F32)
        s.xsend[at, pl.ds(first, count), :] = v.astype(BF)

    for half in (0, 1):
        first, count = IMAGE_PARTS[half]
        cast(0, 3, first=first, count=count)
        to, at = ((xup, s.xa), (xdown, s.xb))[half]
        send(copy(s.xsend.at[0, pl.ds(first, count)], at, ("xa", "xb")[half], 0, to))

    def image_back(at, place, half, to, add=None):
        first, count = IMAGE_PARTS[half]
        cast(at, place, add=add, first=first, count=count)
        r = pl.ds(first, count)
        send(copy(s.xsend.at[at, r], s.xr.at[at - 1, r], "xr", (at - 1) * 2 + half, to))

    image_back(2, 2, 0, xdown)
    unit(y2, 0, 2 * PAIRS)
    image_back(1, 1, 1, xup)

    def text_grad(yy):
        s.gtall[...] = dot(s.w[yy], s.img[...], TN)

        def out(i):
            s.gtcsend[yy, rows(i), :] = s.gtall[rows(i, oc * TC), :].astype(BF)
            s.gt[yy, rows(i), :] = s.gtall[rows(i, core * TC), :]

        each(TC // 16, out)

    def send_back_twin(yy):
        send(copy(s.gtcsend.at[yy], s.gtcrecv.at[yy], "gtc", yy, twin))

    def back_twin_arrived(yy):
        arrived(s.gtcrecv.at[yy], "gtc", yy)

    def columns_of(cc):
        return s.w[y2, :, pl.ds(cc * TC, TC)]

    @pl.when(core == 0)
    def _():
        s.gtcsend[y2] = dot(columns_of(1), s.img[...], TN).astype(BF)

    @pl.when(core == 1)
    def _():
        s.gtcsend[y2] = dot(columns_of(0), s.img[...], TN).astype(BF)

    send_back_twin(y2)

    @pl.when(core == 0)
    def _():
        s.gt[y2] = dot(columns_of(0), s.img[...], TN)

    @pl.when(core == 1)
    def _():
        s.gt[y2] = dot(columns_of(1), s.img[...], TN)

    text_grad(y1)
    send_back_twin(y1)
    back_twin_arrived(y2)

    def text_back(at, yy, zz, half, dst, group, index, to, add=None):
        first, count = TEXT_PARTS[half]

        r = at16(zz * WIN + first, count)
        v = s.gt[yy, r, :] + s.gtcrecv[yy, r, :].astype(F32)
        if add is not None:
            v = v + add[zz].astype(F32)
        s.ysend[at, r, :] = v.astype(BF)
        send(copy(s.ysend.at[at, r], dst(r), group, index, to))

    def text_back_to(at, yy, zz, half, to, add=None):
        text_back(at, yy, zz, half, lambda r: s.yr.at[at - 1, r], "yr", (at - 1) * 4 + zz * 2 + half, to, add)

    for zz in (oz, zh):
        text_back(0, y2, zz, 0, lambda r, zz=zz: s.ya.at[zz], "ya", zz, yup)
        text_back(0, y2, zz, 1, lambda r, zz=zz: s.yb.at[zz], "yb", zz, ydown)
    text_grad(y3)
    send_back_twin(y3)
    back_twin_arrived(y1)
    for zz in (oz, zh):
        text_back_to(1, y1, zz, 1, yup)
    back_twin_arrived(y3)
    for zz in (oz, zh):
        text_back_to(2, y3, zz, 0, ydown)
    arrived(s.xa, "xa")
    image_back(1, 1, 0, xup, add=s.xa)
    arrived(s.xb, "xb")
    image_back(2, 2, 1, xdown, add=s.xb)
    text_grad(y)
    send_back_twin(y)
    for zz in (oz, zh):
        arrived(s.ya.at[zz], "ya", zz)
        text_back_to(1, y1, zz, 0, yup, add=s.ya)
        arrived(s.yb.at[zz], "yb", zz)
        text_back_to(2, y3, zz, 1, ydown, add=s.yb)
    back_twin_arrived(y)

    for way in (0, 1):
        for half in (0, 1):
            arrived(s.xr.at[way, pl.ds(*IMAGE_PARTS[half])], "xr", way * 2 + half)

    g = s.gi[pl.ds(0, PAIRS), :] + s.xr[0].astype(F32) + s.xr[1].astype(F32)
    g = LOGIT_SCALE * g
    p = jnp.concatenate([s.imh[x, 0].astype(F32), s.imh[x, 1].astype(F32)], axis=1)
    s.dots[m] = wide(rowsum(g * p))
    s.ghalf[...] = pick(g, m)
    s.izsend[...] = pick(g, om).astype(BF)
    send(copy(s.dots.at[m], s.dots.at[m], "dots", 0, mate))
    send(copy(s.izsend, s.izrecv, "iz", 0, mate))

    def back_arrived(zz):
        for way in (0, 1):
            for half in (0, 1):
                first, count = TEXT_PARTS[half]
                r = pl.ds(pl.multiple_of(zz * WIN + first, 16), count)
                arrived(s.yr.at[way, r], "yr", way * 4 + zz * 2 + half)

    def text_sum(r):
        g = s.gt[y, r, :] + s.gtcrecv[y, r, :].astype(F32)
        return g + s.yr[0, r, :].astype(F32) + s.yr[1, r, :].astype(F32)

    back_arrived(oz)
    for half, (first, count) in enumerate(Z_PARTS):
        r = pl.ds(first, count)
        s.zsend[r, :] = text_sum(at16(oz * WIN + first, count)).astype(BF)
        send(copy(s.zsend.at[r], s.zrecv.at[r], "z", half, far))
    back_arrived(zh)

    s.gown[...] = text_sum(at16(zh * WIN, WIN))


    def text_own(first, count):
        r = pl.ds(first, count)
        g = LOGIT_SCALE * (s.gown[r, :] + s.zrecv[r, :].astype(F32))
        p = s.tproj[r, :]
        sc = s.tsc[r, :][:, :1]
        v = sc * g - (sc * sc * sc) * p * rowsum(p * g)
        v = jnp.where(own_rows(first, count), v, 0.0).astype(BF)
        s.tw[m, r, :] = v
        s.sw[m, r, :] = wide(rowsum(v.astype(F32) * p))

    for half, (first, count) in enumerate(Z_PARTS):
        r = pl.ds(first, count)
        arrived(s.zrecv.at[r], "z", half)
        text_own(first, count)
        send(copy(s.tw.at[m, r], s.tw.at[m, r], "tw", half, mate))
    send(copy(s.sw.at[m], s.sw.at[m], "sw", 0, mate))

    arrived(s.dots.at[om], "dots")
    arrived(s.izrecv, "iz")

    g = s.ghalf[...] + s.izrecv[...].astype(F32)
    sc = s.isc[...][:, :1]
    total = (s.dots[0] + s.dots[1])[:, :1]
    p = s.imh[x, m].astype(F32)
    s.pg[...] = (sc * g - (sc * sc * sc) * p * total).astype(BF)

    @pl.when(core == 1)
    def _():
        pg_copy.start()

    class Sum:
        def __init__(self, load, count, bufs, group, devices, chunks, side):
            self.load, self.chunks = load, chunks
            self.out, self.back = bufs
            self.group, self.side = group, side
            n, cols = self.used, self.cols = pl.ds(0, count), pl.ds(*COLUMNS[side])
            self.copies = [
                copy(self.out.at[at, :, n, cols], self.back.at[at, :, n, cols], group, side * 3 + at, to)
                for at, to in enumerate(devices)
            ]

        def begin(self):
            for at in (1, 0, 2):
                for half in (0, 1):
                    self.out[at, half, self.used, self.cols] = self.load(self.chunks[1 + at], half).astype(BF)
                self.copies[at].start()

        def finish(self, store):
            for at in range(3):
                arrived(self.back.at[at, :, self.used, self.cols], self.group, self.side * 3 + at)
            for half in (0, 1):
                v = self.load(self.chunks[0], half)
                for at in range(3):
                    v = v + self.back[at, half, self.used, self.cols].astype(F32)
                store(half, v)
            for c in self.copies:
                c.wait_send()

    low, high = (pl.ds(*where) for where in COLUMNS)
    bufs1, bufs2 = (s.h1send, s.h1r), (s.h2send, s.h2r)
    along_x, along_y = (xup, dev(xx=x2), xdown), (yup, dev(yy=y2), ydown)
    xs, ys = (x, x1, x2, x3), (y, y1, y2, y3)
    x_first = Sum(
        lambda c, half: s.h[pl.ds(half * NY, NY), at16(c * 32, XWIN), low].reshape(XHALF, COLUMNS[0][1]),
        XHALF, bufs1, "h1r", along_x, xs, 0,
    )
    y_second = Sum(
        lambda c, half: s.h1[at16((c * NZ + half) * XWIN, XWIN), low],
        XWIN, bufs2, "h2r", along_y, ys, 0,
    )
    y_first = Sum(lambda c, half: s.h[c * NZ + half, :, high], ZROWS, bufs1, "h1r", along_y, ys, 1)
    x_second = Sum(
        lambda c, half: s.h1[at16(half * ZROWS + c * 32, XWIN), high],
        XWIN, bufs2, "h2r", along_x, xs, 1,
    )

    def store(to, count, cols):
        def at(half, v):
            to[pl.ds(half * count, count), cols] = v

        return at

    @pl.when(core == 0)
    def _():
        arrived(s.imft, "imft")
        arrived(s.pgt, "pgt")
        h = dot(s.imf[...], s.pg[...], TN) + dot(s.imft[...], s.pgt[...], TN)
        s.h[...] = h.reshape(s.h.shape)
        x_first.begin()
        y_first.begin()

    s.gip[...] = dot(s.pg[...], s.iht[...], NN)

    def image_out(i):
        s.gsend[rows(i), :] = pick(s.gip[rows(i), :], om).astype(BF)

    each(PAIRS // 16, image_out)

    for half, where in enumerate(Z_PARTS):
        arrived(s.tw.at[om, pl.ds(*where)], "tw", half)

    send(copy(s.gsend, s.grecv, "g", 0, mate))

    def merged(a, b):
        a, b = a.astype(F32), b.astype(F32)
        both = a[STEP:, :] + b[: WIN - STEP, :]
        return jnp.concatenate([a[:STEP, :], both, b[WIN - STEP :, :]], axis=0)

    s.tpg[...] = merged(s.tw[0], s.tw[1]).astype(BF)

    @pl.when(core == 0)
    def _():
        tpg_copy.start()

    @pl.when(core == 1)
    def _():
        arrived(s.nhbt, "nhbt")
        arrived(s.tpgt, "tpgt")
        h = dot(s.tpg[...], s.nhb[...], TN) + dot(s.tpgt[...], s.nhbt[...], TN)
        s.h[...] = h.reshape(s.h.shape)
        x_first.begin()
        y_first.begin()


    g_txt[...] = dot(s.tpg[...], s.th[...], NT)

    arrived(s.sw.at[om], "sw")
    arrived(s.u.at[om], "u")

    u = (s.u[0] + s.u[1])[:1, :]
    mean = rowsum(s.tpg[...].astype(F32) * u) * (1.0 / D)
    product = merged(s.sw[0], s.sw[1])[:, :1] * (1.0 / D)
    g_txt[...] = s.rs[...][:, :1] * (g_txt[...] - mean - s.nhf[...] * product)

    x_first.finish(store(s.h1, XHALF, low))
    y_second.begin()
    y_first.finish(store(s.h1, ZROWS, high))
    x_second.begin()
    y_second.finish(store(s.h2, XWIN, low))
    x_second.finish(store(s.h2, XWIN, high))

    @pl.when(core == 0)
    def _():
        nhb_copy.wait_send()
        tpg_copy.wait_send()

    @pl.when(core == 1)
    def _():
        imf_copy.wait_send()
        pg_copy.wait_send()

    def head_far(i):
        s.h3send[rows(i), :] = s.h2[rows(i, oz * XWIN), :].astype(BF)

    each(XWIN // 16, head_far)
    send(copy(s.h3send, s.h3recv, "h3", 0, dev(zz=oz)))

    arrived(s.grecv, "g")

    def image_input(i):
        r = rows(i)
        g_img[r, :] = pick(s.gip[r, :], m) + s.grecv[r, :].astype(F32)

    each(PAIRS // 16, image_input)

    arrived(s.h3recv, "h3")

    def head_near(i):
        s.h4[rows(i), :] = s.h2[rows(i, zh * XWIN), :] + s.h3recv[rows(i), :].astype(F32)

    each(XWIN // 16, head_near)
    theirs = s.h4.at[pl.ds(pl.multiple_of(oc * 16, 16), FIN)]
    send(copy(theirs, s.finr, "fin", 0, twin))
    own = pltpu.roll(s.h4[...], lax.rem(XWIN - 4 * x - LAST * core, XWIN), 0)[:LAST, :]
    arrived(s.finr, "fin")
    got = pltpu.roll(s.finr[...], lax.rem(FIN - 4 * x - 2 * core, FIN), 0)[:LAST, :]
    g_ih[...] = jnp.where(core == 0, own, got)
    g_th[...] = jnp.where(core == 0, got, own)

    for c in sent:
        c.wait_send()


def per_device(img_feat, img_head, txt_feat, txt_head):
    vmem = pl.BlockSpec(memory_space=pltpu.VMEM)
    g_img, g_ih, g_txt, g_th = pl.pallas_call(
        kernel,
        out_shape=(
            jax.ShapeDtypeStruct((PAIRS, HALF), F32),
            jax.ShapeDtypeStruct((LAST, HALF), F32),
            jax.ShapeDtypeStruct((PAIRS, HALF), F32),
            jax.ShapeDtypeStruct((LAST, HALF), F32),
        ),
        in_specs=[pl.BlockSpec(memory_space=pl.ANY)] * 4,
        out_specs=(vmem,) * 4,
        scratch_shapes=[pltpu.VMEM(shape, kind) for shape, kind in SCRATCH.values()]
        + [pltpu.SemaphoreType.DMA((total_sends,)), pltpu.SemaphoreType.DMA((total_recvs,))]
        + [pltpu.SemaphoreType.DMA((4,))],
        compiler_params=pltpu.CompilerParams(
            collective_id=0, has_side_effects=True, vmem_limit_bytes=60 * 1024 * 1024
        ),
        cost_estimate=pl.CostEstimate(flops=14 * 10**9, bytes_accessed=5 * 10**6, transcendentals=0),
    )(img_feat, img_head.T, txt_feat, txt_head)
    return g_img, g_ih, g_txt, g_th.T


def solution(mesh):
    in_specs = (P("dp", None), P(None, "mp"), P("dp", None), P("mp", None))
    out_specs = (P("dp", "mp"), P("dp", "mp"), P("dp", "mp"), P("mp", "dp"))
    return jax.shard_map(
        per_device, mesh=mesh, in_specs=in_specs, out_specs=out_specs, check_vma=False
    )
```

```python
import types

import jax
import jax.numpy as jnp
from jax import lax
from jax.experimental import pallas as pl
from jax.experimental.pallas import tpu as pltpu
from jax.sharding import PartitionSpec as P

LOGIT_SCALE = 10.0
LOGIT_BIAS = -2.5
NORM_EPS = 1e-06

NX = 4
NY = 4
NZ = 2
NC = 2
D = 1152
HALF = D // 2
PAIRS = 208
OWN = PAIRS // 2
WIN = 112
STEP = PAIRS - WIN
TC = NZ * WIN
IMGS = NX * PAIRS
YROWS = D // NY
ZROWS = YROWS // NZ
LAST = ZROWS // (NX * NC)
XWIN = 48
XHALF = NY * NZ * XWIN // 2
FIN = 32
CUT = 64
IMAGE_PARTS = ((0, WIN), (WIN, STEP))
TEXT_PARTS = ((0, CUT), (CUT, WIN - CUT))
Z_PARTS = ((0, 32), (32, 32), (64, 48))

COLUMNS = ((0, 256), (256, HALF - 256))

NN = ((1,), (0,))
NT = ((1,), (1,))
TN = ((0,), (0,))
BF = jnp.bfloat16
F32 = jnp.float32

SCRATCH = {
    "tf": ((PAIRS, D), BF),
    "th": ((HALF, D), BF),
    "imf": ((PAIRS, D), BF),
    "iht": ((HALF, D), BF),
    "nhf": ((PAIRS, HALF), F32),
    "nhb": ((PAIRS, HALF), BF),
    "rs": ((PAIRS, 128), F32),
    "tpart": ((PAIRS, D), F32),
    "tsend": ((WIN, D), BF),
    "trecv": ((WIN, D), BF),
    "u": ((2, 8, D), F32),
    "tproj": ((WIN, D), F32),
    "tsc": ((WIN, 128), F32),
    "imh": ((NX, 2, PAIRS, HALF), BF),
    "isc": ((PAIRS, 128), F32),
    "img": ((IMGS, D), BF),
    "txt": ((NY, NC * TC, D), BF),
    "w": ((NY, IMGS, NC * TC), BF),
    "gi": ((IMGS, D), F32),
    "xsend": ((3, PAIRS, D), BF),
    "xa": ((WIN, D), BF),
    "xb": ((STEP, D), BF),
    "xr": ((2, PAIRS, D), BF),
    "gtcsend": ((NY, TC, D), BF),
    "gtcrecv": ((NY, TC, D), BF),
    "gt": ((NY, TC, D), F32),
    "gtall": ((NC * TC, D), F32),
    "ysend": ((3, TC, D), BF),
    "ya": ((NZ, CUT, D), BF),
    "yb": ((NZ, WIN - CUT, D), BF),
    "yr": ((2, TC, D), BF),
    "zsend": ((WIN, D), BF),
    "zrecv": ((WIN, D), BF),
    "gown": ((WIN, D), F32),
    "tw": ((2, WIN, D), BF),
    "sw": ((2, WIN, 128), F32),
    "tpg": ((PAIRS, D), BF),
    "ghalf": ((PAIRS, HALF), F32),
    "izsend": ((PAIRS, HALF), BF),
    "izrecv": ((PAIRS, HALF), BF),
    "dots": ((2, PAIRS, 128), F32),
    "pg": ((PAIRS, HALF), BF),
    "gip": ((PAIRS, D), F32),
    "gsend": ((PAIRS, HALF), BF),
    "grecv": ((PAIRS, HALF), BF),
    "imft": ((PAIRS, D), BF),
    "nhbt": ((PAIRS, HALF), BF),
    "pgt": ((PAIRS, HALF), BF),
    "tpgt": ((PAIRS, D), BF),
    "h": ((NY * NZ, ZROWS, HALF), F32),
    "h1send": ((3, 2, XHALF, HALF), BF),
    "h1r": ((3, 2, XHALF, HALF), BF),
    "h1": ((2 * XHALF, HALF), F32),
    "h2send": ((3, 2, XWIN, HALF), BF),
    "h2r": ((3, 2, XWIN, HALF), BF),
    "h2": ((2 * XWIN, HALF), F32),
    "h3send": ((XWIN, HALF), BF),
    "h3recv": ((XWIN, HALF), BF),
    "h4": ((XWIN, HALF), F32),
    "finr": ((FIN, HALF), F32),
}

GROUPS = (
    ("t", 2), ("u", 1), ("img", NX * 4), ("txt", NY * NZ * 2), ("txtc", NY * NZ), ("xa", 1), ("xb", 1), ("xr", 4),
    ("iz", 1), ("dots", 1), ("gtc", NY), ("ya", 2), ("yb", 2), ("yr", 8), ("z", 3), ("tw", 3), ("sw", 1),
    ("g", 1), ("imft", 1), ("nhbt", 1), ("pgt", 1), ("tpgt", 1),
    ("h1r", 6), ("h2r", 6), ("h3", 1), ("fin", 1),
)
RECVS = {}
total_recvs = 0
for group, many in GROUPS:
    RECVS[group] = total_recvs
    total_recvs += many
total_sends = 160


def dot(a, b, dims):
    return lax.dot_general(a, b, (dims, ((), ())), preferred_element_type=F32)


def rows(i, first=0):
    return pl.ds(pl.multiple_of(first + i * 16, 16), 16)


def rowsum(v):
    return jnp.sum(v, -1, keepdims=True)


def wide(v):
    return jnp.broadcast_to(v, (v.shape[0], 128))


def each(count, body):
    lax.fori_loop(0, count, lambda i, c: (body(i), c)[1], 0)


def kernel(img_feat, img_head_t, txt_feat, txt_head, g_img, g_ih, g_txt, g_th, *scratch):
    s = types.SimpleNamespace(**dict(zip(SCRATCH, scratch)))
    ssem, rsem, lsem = scratch[len(SCRATCH) :]
    dp, m = lax.axis_index("dp"), lax.axis_index("mp")
    core = lax.rem(dp, NC)
    x = lax.rem(dp // NC, NX)
    zh = lax.rem(dp // (NC * NX), NZ)
    y = dp // (NC * NX * NZ)
    om, oc, oz = 1 - m, 1 - core, 1 - zh

    loads = [
        pltpu.make_async_copy(src, dst, lsem.at[at])
        for at, (src, dst) in enumerate(
            ((txt_feat, s.tf), (txt_head, s.th), (img_feat, s.imf), (img_head_t, s.iht))
        )
    ]
    for load in loads:
        load.start()

    def dev(yy=None, zz=None, xx=None, cc=None, mm=None):
        yy = y if yy is None else yy
        zz = zh if zz is None else zz
        xx = x if xx is None else xx
        cc = core if cc is None else cc
        mm = m if mm is None else mm
        return (((yy * NZ + zz) * NX + xx) * NC + cc, mm)

    def other(base, by, size):
        return lax.rem(base + by, size)

    x1, x2, x3 = (other(x, d, NX) for d in (1, 2, 3))
    y1, y2, y3 = (other(y, d, NY) for d in (1, 2, 3))
    mate, twin, far = dev(mm=om), dev(cc=oc), dev(zz=oz, mm=om)
    xup, xdown, yup, ydown = dev(xx=x1), dev(xx=x3), dev(yy=y1), dev(yy=y3)

    used = [0]
    sent = []

    def copy(src, dst, group, at, to):
        used[0] += 1
        return pltpu.make_async_remote_copy(
            src_ref=src,
            dst_ref=dst,
            send_sem=ssem.at[used[0] - 1],
            recv_sem=rsem.at[RECVS[group] + at],
            device_id=to,
            device_id_type=pl.DeviceIdType.MESH,
        )

    def send(c):
        c.start()
        sent.append(c)
        return c

    def arrived(ref, group, at=0):
        pltpu.make_async_remote_copy(
            src_ref=ref,
            dst_ref=ref,
            send_sem=ssem.at[0],
            recv_sem=rsem.at[RECVS[group] + at],
            device_id=twin,
            device_id_type=pl.DeviceIdType.MESH,
        ).wait_recv()

    def pick(whole, which):
        return jnp.where(which == 0, whole[:, :HALF], whole[:, HALF:])

    barrier = pltpu.get_barrier_semaphore()
    friends = [mate, twin, far, dev(zz=oz), xup, xdown, yup, ydown, dev(xx=x2), dev(yy=y2)]
    for friend in friends:
        pl.semaphore_signal(barrier, inc=1, device_id=friend, device_id_type=pl.DeviceIdType.MESH)

    loads[0].wait()

    t = s.tf[...].astype(F32)
    t = t - rowsum(t) * (1.0 / D)
    rs = lax.rsqrt(rowsum(t * t) * (1.0 / D) + NORM_EPS)
    half = pick(t * rs, m)
    s.nhf[...] = half
    s.nhb[...] = half.astype(BF)
    s.rs[...] = wide(rs)
    loads[1].wait()
    s.tpart[...] = dot(s.nhb[...], s.th[...], NN)

    s.tsend[...] = s.tpart[pl.ds(pl.multiple_of(om * STEP, 16), WIN), :].astype(BF)
    pl.semaphore_wait(barrier, len(friends))
    for half, where in enumerate(TEXT_PARTS):
        r = pl.ds(*where)
        send(copy(s.tsend.at[r], s.trecv.at[r], "t", half, mate))

    loads[2].wait()
    loads[3].wait()
    s.imh[x, m] = dot(s.imf[...], s.iht[...], NT).astype(BF)

    def image_part(xx, half, cut):
        if cut is None:
            return s.imh.at[xx, half]
        return s.imh.at[xx, half, pl.ds(*IMAGE_PARTS[cut])]

    def send_image(xx, half, to, cut=None):
        ref = image_part(xx, half, cut)
        send(copy(ref, ref, "img", xx * 4 + half * 2 + (cut or 0), to))

    def image_arrived(xx, half, cut=None):
        arrived(image_part(xx, half, cut), "img", xx * 4 + half * 2 + (cut or 0))

    def forward_image(half):
        image_arrived(x1, half)
        send_image(x1, half, xdown, 0)
        image_arrived(x3, half)
        send_image(x3, half, xup, 1)

    for to in (mate, xup, xdown):
        send_image(x, m, to)
    s.u[m] = dot(jnp.ones((8, HALF), BF), s.th[...], NN)
    send(copy(s.u.at[m], s.u.at[m], "u", 0, mate))

    nhb_copy = copy(s.nhb, s.nhbt, "nhbt", 0, twin)
    imf_copy = copy(s.imf, s.imft, "imft", 0, twin)
    pg_copy = copy(s.pg, s.pgt, "pgt", 0, twin)
    tpg_copy = copy(s.tpg, s.tpgt, "tpgt", 0, twin)

    @pl.when(core == 0)
    def _():
        nhb_copy.start()

    @pl.when(core == 1)
    def _():
        imf_copy.start()


    def own_rows(first, count):
        row = m * STEP + first + lax.broadcasted_iota(jnp.int32, (count, 1), 0)
        return (row >= m * OWN) & (row < m * OWN + OWN)

    def at16(first, count):
        return pl.ds(pl.multiple_of(first, 16), count)

    def embed_text(first, count):
        r = pl.ds(first, count)
        p = s.tpart[at16(m * STEP + first, count), :] + s.trecv[r, :].astype(F32)
        sc = lax.rsqrt(rowsum(p * p) + NORM_EPS)
        s.tproj[r, :] = p
        s.tsc[r, :] = wide(sc)
        emb = jnp.where(own_rows(first, count), p * sc, 0.0).astype(BF)
        s.txt[y, at16(core * TC + zh * WIN + first, count), :] = emb

    def part(yy, zz, cut=None):
        first, count = (0, WIN) if cut is None else TEXT_PARTS[cut]
        return s.txt.at[yy, pl.ds(pl.multiple_of(core * TC + zz * WIN + first, 16), count)]

    def send_text(yy, zz, to, cut=None):
        ref = part(yy, zz, cut)
        send(copy(ref, ref, "txt", yy * 4 + zz * 2 + (cut or 0), to))

    def text_arrived(yy, zz, cut=None):
        arrived(part(yy, zz, cut), "txt", yy * 4 + zz * 2 + (cut or 0))

    def forward_text(zz):
        text_arrived(y1, zz, 0)
        send_text(y1, zz, ydown, 0)
        text_arrived(y3, zz, 0)
        text_arrived(y3, zz, 1)
        send_text(y3, zz, yup, 1)
        send_twin(y3, zz)
        text_arrived(y1, zz, 1)
        send_twin(y1, zz)

    def side_part(yy, cc, zz):
        return s.txt.at[yy, pl.ds(pl.multiple_of(cc * TC + zz * WIN, 16), WIN)]

    def send_twin(yy, zz):
        send(copy(part(yy, zz), part(yy, zz), "txtc", yy * NZ + zz, twin))

    def twin_arrived(yy):
        for zz in range(NZ):
            arrived(side_part(yy, oc, zz), "txtc", yy * NZ + zz)

    for half, (first, count) in enumerate(TEXT_PARTS):
        arrived(s.trecv.at[pl.ds(first, count)], "t", half)
        embed_text(first, count)
        for to in (far, yup, ydown):
            send_text(y, zh, to, half)
    send_twin(y, zh)

    def zero(i):
        s.gi[rows(i), :] = jnp.zeros((16, D), F32)

    each(IMGS // 16, zero)
    forward_image(m)

    image_arrived(x, om)
    send_image(x, om, xup)
    send_image(x, om, xdown)

    def embed_images(xx, at, own=False):
        p = jnp.concatenate([s.imh[xx, 0].astype(F32), s.imh[xx, 1].astype(F32)], axis=1)
        sc = lax.rsqrt(rowsum(p * p) + NORM_EPS)
        if own:
            s.isc[...] = wide(sc)
        s.img[pl.ds(at * PAIRS, PAIRS), :] = (p * sc).astype(BF)

    embed_images(x, 0, own=True)

    for half in (0, 1):
        text_arrived(y, oz, half)
        send_text(y, oz, yup, half)
        send_text(y, oz, ydown, half)
    send_twin(y, oz)
    forward_text(zh)

    def unit(yy, first, count, own=False):
        r = pl.ds(first, count)
        texts = s.txt[yy]
        scores = dot(s.img[r, :], texts, NT)
        weights = 0.5 + 0.5 * jnp.tanh((0.5 * LOGIT_SCALE) * scores + 0.5 * LOGIT_BIAS)
        if own:
            row = lax.broadcasted_iota(jnp.int32, (count, NC * TC), 0)
            col = lax.broadcasted_iota(jnp.int32, (count, NC * TC), 1)
            at = core * TC + zh * WIN
            match = (row - col == m * STEP - at) & (col >= at) & (col < at + WIN)
            weights = weights - match.astype(F32)
        weights = weights.astype(BF)
        s.w[yy, r, :] = weights
        s.gi[r, :] += dot(weights, texts, NN)

    forward_image(om)
    forward_text(oz)
    embed_images(x1, 1)
    embed_images(x3, 2)
    twin_arrived(y)
    unit(y, 0, 3 * PAIRS, own=True)
    twin_arrived(y1)
    unit(y1, 0, 3 * PAIRS)
    twin_arrived(y3)
    unit(y3, 0, 3 * PAIRS)
    for zz in (zh, oz):
        for half in (0, 1):
            text_arrived(y2, zz, half)
        send_twin(y2, zz)
    for half in (0, 1):
        for cut in (0, 1):
            image_arrived(x2, half, cut)
    embed_images(x2, 3)
    each(3, lambda i: unit(other(y, i + i // 2, NY), 3 * PAIRS, PAIRS))

    twin_arrived(y2)
    unit(y2, 2 * PAIRS, 2 * PAIRS)

    def cast(at, place, add=None, first=0, count=PAIRS):
        v = s.gi[pl.ds(place * PAIRS + first, count), :]
        if add is not None:
            v = v + add[...].astype(F32)
        s.xsend[at, pl.ds(first, count), :] = v.astype(BF)

    for half in (0, 1):
        first, count = IMAGE_PARTS[half]
        cast(0, 3, first=first, count=count)
        to, at = ((xup, s.xa), (xdown, s.xb))[half]
        send(copy(s.xsend.at[0, pl.ds(first, count)], at, ("xa", "xb")[half], 0, to))

    def image_back(at, place, half, to, add=None):
        first, count = IMAGE_PARTS[half]
        cast(at, place, add=add, first=first, count=count)
        r = pl.ds(first, count)
        send(copy(s.xsend.at[at, r], s.xr.at[at - 1, r], "xr", (at - 1) * 2 + half, to))

    image_back(2, 2, 0, xdown)
    unit(y2, 0, 2 * PAIRS)
    image_back(1, 1, 1, xup)

    def text_grad(yy):
        s.gtall[...] = dot(s.w[yy], s.img[...], TN)

        s.gtcsend[yy] = s.gtall[at16(oc * TC, TC), :].astype(BF)
        s.gt[yy] = s.gtall[at16(core * TC, TC), :]

    def send_back_twin(yy):
        send(copy(s.gtcsend.at[yy], s.gtcrecv.at[yy], "gtc", yy, twin))

    def back_twin_arrived(yy):
        arrived(s.gtcrecv.at[yy], "gtc", yy)

    def columns_of(cc):
        return s.w[y2, :, pl.ds(cc * TC, TC)]

    @pl.when(core == 0)
    def _():
        s.gtcsend[y2] = dot(columns_of(1), s.img[...], TN).astype(BF)

    @pl.when(core == 1)
    def _():
        s.gtcsend[y2] = dot(columns_of(0), s.img[...], TN).astype(BF)

    send_back_twin(y2)

    @pl.when(core == 0)
    def _():
        s.gt[y2] = dot(columns_of(0), s.img[...], TN)

    @pl.when(core == 1)
    def _():
        s.gt[y2] = dot(columns_of(1), s.img[...], TN)

    text_grad(y1)
    send_back_twin(y1)
    back_twin_arrived(y2)

    def text_back(at, yy, zz, half, dst, group, index, to, add=None):
        first, count = TEXT_PARTS[half]

        r = at16(zz * WIN + first, count)
        v = s.gt[yy, r, :] + s.gtcrecv[yy, r, :].astype(F32)
        if add is not None:
            v = v + add[zz].astype(F32)
        s.ysend[at, r, :] = v.astype(BF)
        send(copy(s.ysend.at[at, r], dst(r), group, index, to))

    def text_back_to(at, yy, zz, half, to, add=None):
        text_back(at, yy, zz, half, lambda r: s.yr.at[at - 1, r], "yr", (at - 1) * 4 + zz * 2 + half, to, add)

    for zz in (oz, zh):
        text_back(0, y2, zz, 0, lambda r, zz=zz: s.ya.at[zz], "ya", zz, yup)
        text_back(0, y2, zz, 1, lambda r, zz=zz: s.yb.at[zz], "yb", zz, ydown)
    text_grad(y3)
    send_back_twin(y3)
    back_twin_arrived(y1)
    for zz in (oz, zh):
        text_back_to(1, y1, zz, 1, yup)
    back_twin_arrived(y3)
    for zz in (oz, zh):
        text_back_to(2, y3, zz, 0, ydown)
    arrived(s.xa, "xa")
    image_back(1, 1, 0, xup, add=s.xa)
    arrived(s.xb, "xb")
    image_back(2, 2, 1, xdown, add=s.xb)
    text_grad(y)
    send_back_twin(y)
    for zz in (oz, zh):
        arrived(s.ya.at[zz], "ya", zz)
        text_back_to(1, y1, zz, 0, yup, add=s.ya)
        arrived(s.yb.at[zz], "yb", zz)
        text_back_to(2, y3, zz, 1, ydown, add=s.yb)
    back_twin_arrived(y)

    for way in (0, 1):
        for half in (0, 1):
            arrived(s.xr.at[way, pl.ds(*IMAGE_PARTS[half])], "xr", way * 2 + half)

    g = s.gi[pl.ds(0, PAIRS), :] + s.xr[0].astype(F32) + s.xr[1].astype(F32)
    g = LOGIT_SCALE * g
    p = jnp.concatenate([s.imh[x, 0].astype(F32), s.imh[x, 1].astype(F32)], axis=1)
    s.dots[m] = wide(rowsum(g * p))
    s.ghalf[...] = pick(g, m)
    s.izsend[...] = pick(g, om).astype(BF)
    send(copy(s.dots.at[m], s.dots.at[m], "dots", 0, mate))
    send(copy(s.izsend, s.izrecv, "iz", 0, mate))

    def back_arrived(zz):
        for way in (0, 1):
            for half in (0, 1):
                first, count = TEXT_PARTS[half]
                r = pl.ds(pl.multiple_of(zz * WIN + first, 16), count)
                arrived(s.yr.at[way, r], "yr", way * 4 + zz * 2 + half)

    def text_sum(r):
        g = s.gt[y, r, :] + s.gtcrecv[y, r, :].astype(F32)
        return g + s.yr[0, r, :].astype(F32) + s.yr[1, r, :].astype(F32)

    back_arrived(oz)
    for half, (first, count) in enumerate(Z_PARTS):
        r = pl.ds(first, count)
        s.zsend[r, :] = text_sum(at16(oz * WIN + first, count)).astype(BF)
        send(copy(s.zsend.at[r], s.zrecv.at[r], "z", half, far))
    back_arrived(zh)

    s.gown[...] = text_sum(at16(zh * WIN, WIN))


    def text_own(first, count):
        r = pl.ds(first, count)
        g = LOGIT_SCALE * (s.gown[r, :] + s.zrecv[r, :].astype(F32))
        p = s.tproj[r, :]
        sc = s.tsc[r, :][:, :1]
        v = sc * g - (sc * sc * sc) * p * rowsum(p * g)
        v = jnp.where(own_rows(first, count), v, 0.0).astype(BF)
        s.tw[m, r, :] = v
        s.sw[m, r, :] = wide(rowsum(v.astype(F32) * p))

    for half, (first, count) in enumerate(Z_PARTS):
        r = pl.ds(first, count)
        arrived(s.zrecv.at[r], "z", half)
        text_own(first, count)
        send(copy(s.tw.at[m, r], s.tw.at[m, r], "tw", half, mate))
    send(copy(s.sw.at[m], s.sw.at[m], "sw", 0, mate))

    arrived(s.dots.at[om], "dots")
    arrived(s.izrecv, "iz")

    g = s.ghalf[...] + s.izrecv[...].astype(F32)
    sc = s.isc[...][:, :1]
    total = (s.dots[0] + s.dots[1])[:, :1]
    p = s.imh[x, m].astype(F32)
    s.pg[...] = (sc * g - (sc * sc * sc) * p * total).astype(BF)

    @pl.when(core == 1)
    def _():
        pg_copy.start()

    class Sum:
        def __init__(self, load, count, bufs, group, devices, chunks, side):
            self.load, self.chunks = load, chunks
            self.out, self.back = bufs
            self.group, self.side = group, side
            n, cols = self.used, self.cols = pl.ds(0, count), pl.ds(*COLUMNS[side])
            self.copies = [
                copy(self.out.at[at, :, n, cols], self.back.at[at, :, n, cols], group, side * 3 + at, to)
                for at, to in enumerate(devices)
            ]

        def begin(self):
            for at in (1, 0, 2):
                for half in (0, 1):
                    self.out[at, half, self.used, self.cols] = self.load(self.chunks[1 + at], half).astype(BF)
                self.copies[at].start()

        def finish(self, store):
            for at in range(3):
                arrived(self.back.at[at, :, self.used, self.cols], self.group, self.side * 3 + at)
            for half in (0, 1):
                v = self.load(self.chunks[0], half)
                for at in range(3):
                    v = v + self.back[at, half, self.used, self.cols].astype(F32)
                store(half, v)
            for c in self.copies:
                c.wait_send()

    low, high = (pl.ds(*where) for where in COLUMNS)
    bufs1, bufs2 = (s.h1send, s.h1r), (s.h2send, s.h2r)
    along_x, along_y = (xup, dev(xx=x2), xdown), (yup, dev(yy=y2), ydown)
    xs, ys = (x, x1, x2, x3), (y, y1, y2, y3)
    x_first = Sum(
        lambda c, half: s.h[pl.ds(half * NY, NY), at16(c * 32, XWIN), low].reshape(XHALF, COLUMNS[0][1]),
        XHALF, bufs1, "h1r", along_x, xs, 0,
    )
    y_second = Sum(
        lambda c, half: s.h1[at16((c * NZ + half) * XWIN, XWIN), low],
        XWIN, bufs2, "h2r", along_y, ys, 0,
    )
    y_first = Sum(lambda c, half: s.h[c * NZ + half, :, high], ZROWS, bufs1, "h1r", along_y, ys, 1)
    x_second = Sum(
        lambda c, half: s.h1[at16(half * ZROWS + c * 32, XWIN), high],
        XWIN, bufs2, "h2r", along_x, xs, 1,
    )

    def store(to, count, cols):
        def at(half, v):
            to[pl.ds(half * count, count), cols] = v

        return at

    @pl.when(core == 0)
    def _():
        arrived(s.imft, "imft")
        arrived(s.pgt, "pgt")
        h = dot(s.imf[...], s.pg[...], TN) + dot(s.imft[...], s.pgt[...], TN)
        s.h[...] = h.reshape(s.h.shape)
        x_first.begin()
        y_first.begin()

    s.gip[...] = dot(s.pg[...], s.iht[...], NN)

    s.gsend[...] = pick(s.gip[...], om).astype(BF)
    for half, where in enumerate(Z_PARTS):
        arrived(s.tw.at[om, pl.ds(*where)], "tw", half)

    send(copy(s.gsend, s.grecv, "g", 0, mate))

    def merged(a, b):
        a, b = a.astype(F32), b.astype(F32)
        both = a[STEP:, :] + b[: WIN - STEP, :]
        return jnp.concatenate([a[:STEP, :], both, b[WIN - STEP :, :]], axis=0)

    s.tpg[...] = merged(s.tw[0], s.tw[1]).astype(BF)

    @pl.when(core == 0)
    def _():
        tpg_copy.start()

    @pl.when(core == 1)
    def _():
        arrived(s.nhbt, "nhbt")
        arrived(s.tpgt, "tpgt")
        h = dot(s.tpg[...], s.nhb[...], TN) + dot(s.tpgt[...], s.nhbt[...], TN)
        s.h[...] = h.reshape(s.h.shape)
        x_first.begin()
        y_first.begin()


    g_txt[...] = dot(s.tpg[...], s.th[...], NT)

    arrived(s.sw.at[om], "sw")
    arrived(s.u.at[om], "u")

    u = (s.u[0] + s.u[1])[:1, :]
    mean = rowsum(s.tpg[...].astype(F32) * u) * (1.0 / D)
    product = merged(s.sw[0], s.sw[1])[:, :1] * (1.0 / D)
    g_txt[...] = s.rs[...][:, :1] * (g_txt[...] - mean - s.nhf[...] * product)

    x_first.finish(store(s.h1, XHALF, low))
    y_second.begin()
    y_first.finish(store(s.h1, ZROWS, high))
    x_second.begin()
    y_second.finish(store(s.h2, XWIN, low))
    x_second.finish(store(s.h2, XWIN, high))

    @pl.when(core == 0)
    def _():
        nhb_copy.wait_send()
        tpg_copy.wait_send()

    @pl.when(core == 1)
    def _():
        imf_copy.wait_send()
        pg_copy.wait_send()

    def head_far(i):
        s.h3send[rows(i), :] = s.h2[rows(i, oz * XWIN), :].astype(BF)

    each(XWIN // 16, head_far)
    send(copy(s.h3send, s.h3recv, "h3", 0, dev(zz=oz)))

    arrived(s.grecv, "g")

    def image_input(i):
        r = rows(i)
        g_img[r, :] = pick(s.gip[r, :], m) + s.grecv[r, :].astype(F32)

    each(PAIRS // 16, image_input)

    arrived(s.h3recv, "h3")

    def head_near(i):
        s.h4[rows(i), :] = s.h2[rows(i, zh * XWIN), :] + s.h3recv[rows(i), :].astype(F32)

    each(XWIN // 16, head_near)
    theirs = s.h4.at[pl.ds(pl.multiple_of(oc * 16, 16), FIN)]
    send(copy(theirs, s.finr, "fin", 0, twin))
    own = pltpu.roll(s.h4[...], lax.rem(XWIN - 4 * x - LAST * core, XWIN), 0)[:LAST, :]
    arrived(s.finr, "fin")
    got = pltpu.roll(s.finr[...], lax.rem(FIN - 4 * x - 2 * core, FIN), 0)[:LAST, :]
    g_ih[...] = jnp.where(core == 0, own, got)
    g_th[...] = jnp.where(core == 0, got, own)

    for c in sent:
        c.wait_send()


def per_device(img_feat, img_head, txt_feat, txt_head):
    vmem = pl.BlockSpec(memory_space=pltpu.VMEM)
    g_img, g_ih, g_txt, g_th = pl.pallas_call(
        kernel,
        out_shape=(
            jax.ShapeDtypeStruct((PAIRS, HALF), F32),
            jax.ShapeDtypeStruct((LAST, HALF), F32),
            jax.ShapeDtypeStruct((PAIRS, HALF), F32),
            jax.ShapeDtypeStruct((LAST, HALF), F32),
        ),
        in_specs=[pl.BlockSpec(memory_space=pl.ANY)] * 4,
        out_specs=(vmem,) * 4,
        scratch_shapes=[pltpu.VMEM(shape, kind) for shape, kind in SCRATCH.values()]
        + [pltpu.SemaphoreType.DMA((total_sends,)), pltpu.SemaphoreType.DMA((total_recvs,))]
        + [pltpu.SemaphoreType.DMA((4,))],
        compiler_params=pltpu.CompilerParams(
            collective_id=0, has_side_effects=True, vmem_limit_bytes=60 * 1024 * 1024
        ),
        cost_estimate=pl.CostEstimate(flops=14 * 10**9, bytes_accessed=5 * 10**6, transcendentals=0),
    )(img_feat, img_head.T, txt_feat, txt_head)
    return g_img, g_ih, g_txt, g_th.T


def solution(mesh):
    in_specs = (P("dp", None), P(None, "mp"), P("dp", None), P("mp", None))
    out_specs = (P("dp", "mp"), P("dp", "mp"), P("dp", "mp"), P("mp", "dp"))
    return jax.shard_map(
        per_device, mesh=mesh, in_specs=in_specs, out_specs=out_specs, check_vma=False
    )
```

```python
import types

import jax
import jax.numpy as jnp
from jax import lax
from jax.experimental import pallas as pl
from jax.experimental.pallas import tpu as pltpu
from jax.sharding import PartitionSpec as P

LOGIT_SCALE = 10.0
LOGIT_BIAS = -2.5
NORM_EPS = 1e-06

NX = 4
NY = 4
NZ = 2
NC = 2
D = 1152
HALF = D // 2
PAIRS = 208
OWN = PAIRS // 2
WIN = 112
STEP = PAIRS - WIN
TC = NZ * WIN
IMGS = NX * PAIRS
YROWS = D // NY
ZROWS = YROWS // NZ
LAST = ZROWS // (NX * NC)
XWIN = 48
XHALF = NY * NZ * XWIN // 2
FIN = 32
CUT = 64
IMAGE_PARTS = ((0, WIN), (WIN, STEP))
TEXT_PARTS = ((0, CUT), (CUT, WIN - CUT))
Z_PARTS = ((0, 32), (32, 32), (64, 48))

COLUMNS = ((0, 256), (256, HALF - 256))

NN = ((1,), (0,))
NT = ((1,), (1,))
TN = ((0,), (0,))
BF = jnp.bfloat16
F32 = jnp.float32

SCRATCH = {
    "tf": ((PAIRS, D), BF),
    "th": ((HALF, D), BF),
    "imf": ((PAIRS, D), BF),
    "iht": ((HALF, D), BF),
    "nhf": ((PAIRS, HALF), F32),
    "nhb": ((PAIRS, HALF), BF),
    "rs": ((PAIRS, 128), F32),
    "tpart": ((PAIRS, D), F32),
    "tsend": ((WIN, D), BF),
    "trecv": ((WIN, D), BF),
    "u": ((2, 8, D), F32),
    "tproj": ((WIN, D), F32),
    "tsc": ((WIN, 128), F32),
    "imh": ((NX, 2, PAIRS, HALF), BF),
    "isc": ((PAIRS, 128), F32),
    "img": ((IMGS, D), BF),
    "txt": ((NY, NC * TC, D), BF),
    "w": ((NY, IMGS, NC * TC), BF),
    "gi": ((IMGS, D), F32),
    "xsend": ((3, PAIRS, D), BF),
    "xa": ((WIN, D), BF),
    "xb": ((STEP, D), BF),
    "xr": ((2, PAIRS, D), BF),
    "gtcsend": ((NY, TC, D), BF),
    "gtcrecv": ((NY, TC, D), BF),
    "gt": ((NY, TC, D), F32),
    "gtall": ((NC * TC, D), F32),
    "ysend": ((3, TC, D), BF),
    "ya": ((NZ, CUT, D), BF),
    "yb": ((NZ, WIN - CUT, D), BF),
    "yr": ((2, TC, D), BF),
    "zsend": ((WIN, D), BF),
    "zrecv": ((WIN, D), BF),
    "gown": ((WIN, D), F32),
    "tw": ((2, WIN, D), BF),
    "sw": ((2, WIN, 128), F32),
    "tpg": ((PAIRS, D), BF),
    "ghalf": ((PAIRS, HALF), F32),
    "izsend": ((PAIRS, HALF), BF),
    "izrecv": ((PAIRS, HALF), BF),
    "dots": ((2, PAIRS, 128), F32),
    "pg": ((PAIRS, HALF), BF),
    "gip": ((PAIRS, D), F32),
    "gsend": ((PAIRS, HALF), BF),
    "grecv": ((PAIRS, HALF), BF),
    "imft": ((PAIRS, D), BF),
    "nhbt": ((PAIRS, HALF), BF),
    "pgt": ((PAIRS, HALF), BF),
    "tpgt": ((PAIRS, D), BF),
    "h": ((NY * NZ, ZROWS, HALF), F32),
    "h1send": ((3, 2, XHALF, HALF), BF),
    "h1r": ((3, 2, XHALF, HALF), BF),
    "h1": ((2 * XHALF, HALF), F32),
    "h2send": ((3, 2, XWIN, HALF), BF),
    "h2r": ((3, 2, XWIN, HALF), BF),
    "h2": ((2 * XWIN, HALF), F32),
    "h3send": ((XWIN, HALF), BF),
    "h3recv": ((XWIN, HALF), BF),
    "h4": ((XWIN, HALF), F32),
    "finr": ((FIN, HALF), F32),
}

GROUPS = (
    ("t", 2), ("u", 1), ("img", NX * 4), ("txt", NY * NZ * 2), ("txtc", NY * NZ), ("xa", 1), ("xb", 1), ("xr", 4),
    ("iz", 1), ("dots", 1), ("gtc", NY), ("ya", 2), ("yb", 2), ("yr", 8), ("z", 3), ("tw", 3), ("sw", 1),
    ("g", 1), ("imft", 1), ("nhbt", 1), ("pgt", 1), ("tpgt", 1),
    ("h1r", 6), ("h2r", 6), ("h3", 1), ("fin", 1),
)
RECVS = {}
total_recvs = 0
for group, many in GROUPS:
    RECVS[group] = total_recvs
    total_recvs += many
total_sends = 160


def dot(a, b, dims):
    return lax.dot_general(a, b, (dims, ((), ())), preferred_element_type=F32)


def rows(i, first=0):
    return pl.ds(pl.multiple_of(first + i * 16, 16), 16)


def rowsum(v):
    return jnp.sum(v, -1, keepdims=True)


def wide(v):
    return jnp.broadcast_to(v, (v.shape[0], 128))


def each(count, body):
    lax.fori_loop(0, count, lambda i, c: (body(i), c)[1], 0)


def kernel(img_feat, img_head_t, txt_feat, txt_head, g_img, g_ih, g_txt, g_th, *scratch):
    s = types.SimpleNamespace(**dict(zip(SCRATCH, scratch)))
    ssem, rsem, lsem = scratch[len(SCRATCH) :]
    dp, m = lax.axis_index("dp"), lax.axis_index("mp")
    core = lax.rem(dp, NC)
    x = lax.rem(dp // NC, NX)
    zh = lax.rem(dp // (NC * NX), NZ)
    y = dp // (NC * NX * NZ)
    om, oc, oz = 1 - m, 1 - core, 1 - zh

    loads = [
        pltpu.make_async_copy(src, dst, lsem.at[at])
        for at, (src, dst) in enumerate(
            ((txt_feat, s.tf), (txt_head, s.th), (img_feat, s.imf), (img_head_t, s.iht))
        )
    ]
    for load in loads:
        load.start()

    def dev(yy=None, zz=None, xx=None, cc=None, mm=None):
        yy = y if yy is None else yy
        zz = zh if zz is None else zz
        xx = x if xx is None else xx
        cc = core if cc is None else cc
        mm = m if mm is None else mm
        return (((yy * NZ + zz) * NX + xx) * NC + cc, mm)

    def other(base, by, size):
        return lax.rem(base + by, size)

    x1, x2, x3 = (other(x, d, NX) for d in (1, 2, 3))
    y1, y2, y3 = (other(y, d, NY) for d in (1, 2, 3))
    mate, twin, far = dev(mm=om), dev(cc=oc), dev(zz=oz, mm=om)
    xup, xdown, yup, ydown = dev(xx=x1), dev(xx=x3), dev(yy=y1), dev(yy=y3)

    used = [0]
    sent = []

    def copy(src, dst, group, at, to):
        used[0] += 1
        return pltpu.make_async_remote_copy(
            src_ref=src,
            dst_ref=dst,
            send_sem=ssem.at[used[0] - 1],
            recv_sem=rsem.at[RECVS[group] + at],
            device_id=to,
            device_id_type=pl.DeviceIdType.MESH,
        )

    def send(c):
        c.start()
        sent.append(c)
        return c

    def arrived(ref, group, at=0):
        pltpu.make_async_remote_copy(
            src_ref=ref,
            dst_ref=ref,
            send_sem=ssem.at[0],
            recv_sem=rsem.at[RECVS[group] + at],
            device_id=twin,
            device_id_type=pl.DeviceIdType.MESH,
        ).wait_recv()

    def pick(whole, which):
        return jnp.where(which == 0, whole[:, :HALF], whole[:, HALF:])

    barrier = pltpu.get_barrier_semaphore()
    friends = [mate, twin, far, dev(zz=oz), xup, xdown, yup, ydown, dev(xx=x2), dev(yy=y2)]
    for friend in friends:
        pl.semaphore_signal(barrier, inc=1, device_id=friend, device_id_type=pl.DeviceIdType.MESH)

    loads[0].wait()

    t = s.tf[...].astype(F32)
    t = t - rowsum(t) * (1.0 / D)
    rs = lax.rsqrt(rowsum(t * t) * (1.0 / D) + NORM_EPS)
    half = pick(t * rs, m)
    s.nhf[...] = half
    s.nhb[...] = half.astype(BF)
    s.rs[...] = wide(rs)
    loads[1].wait()
    s.tpart[...] = dot(s.nhb[...], s.th[...], NN)

    def tosend(i):
        s.tsend[rows(i), :] = s.tpart[rows(i, om * STEP), :].astype(BF)

    each(WIN // 16, tosend)
    pl.semaphore_wait(barrier, len(friends))
    for half, where in enumerate(TEXT_PARTS):
        r = pl.ds(*where)
        send(copy(s.tsend.at[r], s.trecv.at[r], "t", half, mate))

    loads[2].wait()
    loads[3].wait()
    s.imh[x, m] = dot(s.imf[...], s.iht[...], NT).astype(BF)

    def image_part(xx, half, cut):
        if cut is None:
            return s.imh.at[xx, half]
        return s.imh.at[xx, half, pl.ds(*IMAGE_PARTS[cut])]

    def send_image(xx, half, to, cut=None):
        ref = image_part(xx, half, cut)
        send(copy(ref, ref, "img", xx * 4 + half * 2 + (cut or 0), to))

    def image_arrived(xx, half, cut=None):
        arrived(image_part(xx, half, cut), "img", xx * 4 + half * 2 + (cut or 0))

    def forward_image(half):
        image_arrived(x1, half)
        send_image(x1, half, xdown, 0)
        image_arrived(x3, half)
        send_image(x3, half, xup, 1)

    for to in (mate, xup, xdown):
        send_image(x, m, to)
    s.u[m] = dot(jnp.ones((8, HALF), BF), s.th[...], NN)
    send(copy(s.u.at[m], s.u.at[m], "u", 0, mate))

    nhb_copy = copy(s.nhb, s.nhbt, "nhbt", 0, twin)
    imf_copy = copy(s.imf, s.imft, "imft", 0, twin)
    pg_copy = copy(s.pg, s.pgt, "pgt", 0, twin)
    tpg_copy = copy(s.tpg, s.tpgt, "tpgt", 0, twin)

    @pl.when(core == 0)
    def _():
        nhb_copy.start()

    @pl.when(core == 1)
    def _():
        imf_copy.start()


    def own_rows(first, count):
        row = m * STEP + first + lax.broadcasted_iota(jnp.int32, (count, 1), 0)
        return (row >= m * OWN) & (row < m * OWN + OWN)

    def at16(first, count):
        return pl.ds(pl.multiple_of(first, 16), count)

    def embed_text(first, count):
        r = pl.ds(first, count)
        p = s.tpart[at16(m * STEP + first, count), :] + s.trecv[r, :].astype(F32)
        sc = lax.rsqrt(rowsum(p * p) + NORM_EPS)
        s.tproj[r, :] = p
        s.tsc[r, :] = wide(sc)
        emb = jnp.where(own_rows(first, count), p * sc, 0.0).astype(BF)
        s.txt[y, at16(core * TC + zh * WIN + first, count), :] = emb

    def part(yy, zz, cut=None):
        first, count = (0, WIN) if cut is None else TEXT_PARTS[cut]
        return s.txt.at[yy, pl.ds(pl.multiple_of(core * TC + zz * WIN + first, 16), count)]

    def send_text(yy, zz, to, cut=None):
        ref = part(yy, zz, cut)
        send(copy(ref, ref, "txt", yy * 4 + zz * 2 + (cut or 0), to))

    def text_arrived(yy, zz, cut=None):
        arrived(part(yy, zz, cut), "txt", yy * 4 + zz * 2 + (cut or 0))

    def forward_text(zz):
        text_arrived(y1, zz, 0)
        send_text(y1, zz, ydown, 0)
        text_arrived(y3, zz, 0)
        text_arrived(y3, zz, 1)
        send_text(y3, zz, yup, 1)
        send_twin(y3, zz)
        text_arrived(y1, zz, 1)
        send_twin(y1, zz)

    def side_part(yy, cc, zz):
        return s.txt.at[yy, pl.ds(pl.multiple_of(cc * TC + zz * WIN, 16), WIN)]

    def send_twin(yy, zz):
        send(copy(part(yy, zz), part(yy, zz), "txtc", yy * NZ + zz, twin))

    def twin_arrived(yy):
        for zz in range(NZ):
            arrived(side_part(yy, oc, zz), "txtc", yy * NZ + zz)

    for half, (first, count) in enumerate(TEXT_PARTS):
        arrived(s.trecv.at[pl.ds(first, count)], "t", half)
        embed_text(first, count)
        for to in (far, yup, ydown):
            send_text(y, zh, to, half)
    send_twin(y, zh)

    def zero(i):
        s.gi[rows(i), :] = jnp.zeros((16, D), F32)

    each(IMGS // 16, zero)
    forward_image(m)

    image_arrived(x, om)
    send_image(x, om, xup)
    send_image(x, om, xdown)

    def embed_images(xx, at, own=False):
        p = jnp.concatenate([s.imh[xx, 0].astype(F32), s.imh[xx, 1].astype(F32)], axis=1)
        sc = lax.rsqrt(rowsum(p * p) + NORM_EPS)
        if own:
            s.isc[...] = wide(sc)
        s.img[pl.ds(at * PAIRS, PAIRS), :] = (p * sc).astype(BF)

    embed_images(x, 0, own=True)

    for half in (0, 1):
        text_arrived(y, oz, half)
        send_text(y, oz, yup, half)
        send_text(y, oz, ydown, half)
    send_twin(y, oz)
    forward_text(zh)

    def unit(yy, first, count, own=False):
        r = pl.ds(first, count)
        texts = s.txt[yy]
        scores = dot(s.img[r, :], texts, NT)
        weights = 0.5 + 0.5 * jnp.tanh((0.5 * LOGIT_SCALE) * scores + 0.5 * LOGIT_BIAS)
        if own:
            row = lax.broadcasted_iota(jnp.int32, (count, NC * TC), 0)
            col = lax.broadcasted_iota(jnp.int32, (count, NC * TC), 1)
            at = core * TC + zh * WIN
            match = (row - col == m * STEP - at) & (col >= at) & (col < at + WIN)
            weights = weights - match.astype(F32)
        weights = weights.astype(BF)
        s.w[yy, r, :] = weights
        s.gi[r, :] += dot(weights, texts, NN)

    forward_image(om)
    forward_text(oz)
    embed_images(x1, 1)
    embed_images(x3, 2)
    twin_arrived(y)
    unit(y, 0, 3 * PAIRS, own=True)
    twin_arrived(y1)
    unit(y1, 0, 3 * PAIRS)
    twin_arrived(y3)
    unit(y3, 0, 3 * PAIRS)
    for zz in (zh, oz):
        for half in (0, 1):
            text_arrived(y2, zz, half)
        send_twin(y2, zz)
    for half in (0, 1):
        for cut in (0, 1):
            image_arrived(x2, half, cut)
    embed_images(x2, 3)
    each(3, lambda i: unit(other(y, i + i // 2, NY), 3 * PAIRS, PAIRS))

    def text_grad(yy):
        s.gtall[...] = dot(s.w[yy], s.img[...], TN)

        s.gtcsend[yy] = s.gtall[at16(oc * TC, TC), :].astype(BF)
        s.gt[yy] = s.gtall[at16(core * TC, TC), :]

    def send_back_twin(yy):
        send(copy(s.gtcsend.at[yy], s.gtcrecv.at[yy], "gtc", yy, twin))

    def back_twin_arrived(yy):
        arrived(s.gtcrecv.at[yy], "gtc", yy)

    def text_back(at, yy, zz, half, dst, group, index, to, add=None):
        first, count = TEXT_PARTS[half]

        r = at16(zz * WIN + first, count)
        v = s.gt[yy, r, :] + s.gtcrecv[yy, r, :].astype(F32)
        if add is not None:
            v = v + add[zz].astype(F32)
        s.ysend[at, r, :] = v.astype(BF)
        send(copy(s.ysend.at[at, r], dst(r), group, index, to))

    def text_back_to(at, yy, zz, half, to, add=None):
        text_back(at, yy, zz, half, lambda r: s.yr.at[at - 1, r], "yr", (at - 1) * 4 + zz * 2 + half, to, add)

    text_grad(y1)
    send_back_twin(y1)
    text_grad(y3)
    send_back_twin(y3)

    twin_arrived(y2)
    unit(y2, 2 * PAIRS, 2 * PAIRS)

    def cast(at, place, add=None, first=0, count=PAIRS):
        v = s.gi[pl.ds(place * PAIRS + first, count), :]
        if add is not None:
            v = v + add[...].astype(F32)
        s.xsend[at, pl.ds(first, count), :] = v.astype(BF)

    for half in (0, 1):
        first, count = IMAGE_PARTS[half]
        cast(0, 3, first=first, count=count)
        to, at = ((xup, s.xa), (xdown, s.xb))[half]
        send(copy(s.xsend.at[0, pl.ds(first, count)], at, ("xa", "xb")[half], 0, to))

    def image_back(at, place, half, to, add=None):
        first, count = IMAGE_PARTS[half]
        cast(at, place, add=add, first=first, count=count)
        r = pl.ds(first, count)
        send(copy(s.xsend.at[at, r], s.xr.at[at - 1, r], "xr", (at - 1) * 2 + half, to))

    image_back(2, 2, 0, xdown)
    back_twin_arrived(y1)
    for zz in (oz, zh):
        text_back_to(1, y1, zz, 1, yup)
    back_twin_arrived(y3)
    for zz in (oz, zh):
        text_back_to(2, y3, zz, 0, ydown)
    unit(y2, 0, 2 * PAIRS)
    image_back(1, 1, 1, xup)

    def columns_of(cc):
        return s.w[y2, :, pl.ds(cc * TC, TC)]

    @pl.when(core == 0)
    def _():
        s.gtcsend[y2] = dot(columns_of(1), s.img[...], TN).astype(BF)

    @pl.when(core == 1)
    def _():
        s.gtcsend[y2] = dot(columns_of(0), s.img[...], TN).astype(BF)

    send_back_twin(y2)

    @pl.when(core == 0)
    def _():
        s.gt[y2] = dot(columns_of(0), s.img[...], TN)

    @pl.when(core == 1)
    def _():
        s.gt[y2] = dot(columns_of(1), s.img[...], TN)

    back_twin_arrived(y2)

    for zz in (oz, zh):
        text_back(0, y2, zz, 0, lambda r, zz=zz: s.ya.at[zz], "ya", zz, yup)
        text_back(0, y2, zz, 1, lambda r, zz=zz: s.yb.at[zz], "yb", zz, ydown)
    text_grad(y)
    send_back_twin(y)
    arrived(s.xa, "xa")
    image_back(1, 1, 0, xup, add=s.xa)
    arrived(s.xb, "xb")
    image_back(2, 2, 1, xdown, add=s.xb)
    for zz in (oz, zh):
        arrived(s.ya.at[zz], "ya", zz)
        text_back_to(1, y1, zz, 0, yup, add=s.ya)
        arrived(s.yb.at[zz], "yb", zz)
        text_back_to(2, y3, zz, 1, ydown, add=s.yb)
    back_twin_arrived(y)

    for way in (0, 1):
        for half in (0, 1):
            arrived(s.xr.at[way, pl.ds(*IMAGE_PARTS[half])], "xr", way * 2 + half)

    g = s.gi[pl.ds(0, PAIRS), :] + s.xr[0].astype(F32) + s.xr[1].astype(F32)
    g = LOGIT_SCALE * g
    p = jnp.concatenate([s.imh[x, 0].astype(F32), s.imh[x, 1].astype(F32)], axis=1)
    s.dots[m] = wide(rowsum(g * p))
    s.ghalf[...] = pick(g, m)
    s.izsend[...] = pick(g, om).astype(BF)
    send(copy(s.dots.at[m], s.dots.at[m], "dots", 0, mate))
    send(copy(s.izsend, s.izrecv, "iz", 0, mate))

    def back_arrived(zz):
        for way in (0, 1):
            for half in (0, 1):
                first, count = TEXT_PARTS[half]
                r = pl.ds(pl.multiple_of(zz * WIN + first, 16), count)
                arrived(s.yr.at[way, r], "yr", way * 4 + zz * 2 + half)

    def text_sum(r):
        g = s.gt[y, r, :] + s.gtcrecv[y, r, :].astype(F32)
        return g + s.yr[0, r, :].astype(F32) + s.yr[1, r, :].astype(F32)

    back_arrived(oz)
    for half, (first, count) in enumerate(Z_PARTS):
        r = pl.ds(first, count)
        s.zsend[r, :] = text_sum(at16(oz * WIN + first, count)).astype(BF)
        send(copy(s.zsend.at[r], s.zrecv.at[r], "z", half, far))
    back_arrived(zh)

    s.gown[...] = text_sum(at16(zh * WIN, WIN))


    def text_own(first, count):
        r = pl.ds(first, count)
        g = LOGIT_SCALE * (s.gown[r, :] + s.zrecv[r, :].astype(F32))
        p = s.tproj[r, :]
        sc = s.tsc[r, :][:, :1]
        v = sc * g - (sc * sc * sc) * p * rowsum(p * g)
        v = jnp.where(own_rows(first, count), v, 0.0).astype(BF)
        s.tw[m, r, :] = v
        s.sw[m, r, :] = wide(rowsum(v.astype(F32) * p))

    for half, (first, count) in enumerate(Z_PARTS):
        r = pl.ds(first, count)
        arrived(s.zrecv.at[r], "z", half)
        text_own(first, count)
        send(copy(s.tw.at[m, r], s.tw.at[m, r], "tw", half, mate))
    send(copy(s.sw.at[m], s.sw.at[m], "sw", 0, mate))

    arrived(s.dots.at[om], "dots")
    arrived(s.izrecv, "iz")

    g = s.ghalf[...] + s.izrecv[...].astype(F32)
    sc = s.isc[...][:, :1]
    total = (s.dots[0] + s.dots[1])[:, :1]
    p = s.imh[x, m].astype(F32)
    s.pg[...] = (sc * g - (sc * sc * sc) * p * total).astype(BF)

    @pl.when(core == 1)
    def _():
        pg_copy.start()

    class Sum:
        def __init__(self, load, count, bufs, group, devices, chunks, side):
            self.load, self.chunks = load, chunks
            self.out, self.back = bufs
            self.group, self.side = group, side
            n, cols = self.used, self.cols = pl.ds(0, count), pl.ds(*COLUMNS[side])
            self.copies = [
                copy(self.out.at[at, :, n, cols], self.back.at[at, :, n, cols], group, side * 3 + at, to)
                for at, to in enumerate(devices)
            ]

        def begin(self):
            for at in (1, 0, 2):
                for half in (0, 1):
                    self.out[at, half, self.used, self.cols] = self.load(self.chunks[1 + at], half).astype(BF)
                self.copies[at].start()

        def finish(self, store):
            for at in range(3):
                arrived(self.back.at[at, :, self.used, self.cols], self.group, self.side * 3 + at)
            for half in (0, 1):
                v = self.load(self.chunks[0], half)
                for at in range(3):
                    v = v + self.back[at, half, self.used, self.cols].astype(F32)
                store(half, v)
            for c in self.copies:
                c.wait_send()

    low, high = (pl.ds(*where) for where in COLUMNS)
    bufs1, bufs2 = (s.h1send, s.h1r), (s.h2send, s.h2r)
    along_x, along_y = (xup, dev(xx=x2), xdown), (yup, dev(yy=y2), ydown)
    xs, ys = (x, x1, x2, x3), (y, y1, y2, y3)
    x_first = Sum(
        lambda c, half: s.h[pl.ds(half * NY, NY), at16(c * 32, XWIN), low].reshape(XHALF, COLUMNS[0][1]),
        XHALF, bufs1, "h1r", along_x, xs, 0,
    )
    y_second = Sum(
        lambda c, half: s.h1[at16((c * NZ + half) * XWIN, XWIN), low],
        XWIN, bufs2, "h2r", along_y, ys, 0,
    )
    y_first = Sum(lambda c, half: s.h[c * NZ + half, :, high], ZROWS, bufs1, "h1r", along_y, ys, 1)
    x_second = Sum(
        lambda c, half: s.h1[at16(half * ZROWS + c * 32, XWIN), high],
        XWIN, bufs2, "h2r", along_x, xs, 1,
    )

    def store(to, count, cols):
        def at(half, v):
            to[pl.ds(half * count, count), cols] = v

        return at

    @pl.when(core == 0)
    def _():
        arrived(s.imft, "imft")
        arrived(s.pgt, "pgt")
        h = dot(s.imf[...], s.pg[...], TN) + dot(s.imft[...], s.pgt[...], TN)
        s.h[...] = h.reshape(s.h.shape)
        x_first.begin()
        y_first.begin()

    s.gip[...] = dot(s.pg[...], s.iht[...], NN)

    def image_out(i):
        s.gsend[rows(i), :] = pick(s.gip[rows(i), :], om).astype(BF)

    each(PAIRS // 16, image_out)

    for half, where in enumerate(Z_PARTS):
        arrived(s.tw.at[om, pl.ds(*where)], "tw", half)

    send(copy(s.gsend, s.grecv, "g", 0, mate))

    def merged(a, b):
        a, b = a.astype(F32), b.astype(F32)
        both = a[STEP:, :] + b[: WIN - STEP, :]
        return jnp.concatenate([a[:STEP, :], both, b[WIN - STEP :, :]], axis=0)

    s.tpg[...] = merged(s.tw[0], s.tw[1]).astype(BF)

    @pl.when(core == 0)
    def _():
        tpg_copy.start()

    @pl.when(core == 1)
    def _():
        arrived(s.nhbt, "nhbt")
        arrived(s.tpgt, "tpgt")
        h = dot(s.tpg[...], s.nhb[...], TN) + dot(s.tpgt[...], s.nhbt[...], TN)
        s.h[...] = h.reshape(s.h.shape)
        x_first.begin()
        y_first.begin()


    g_txt[...] = dot(s.tpg[...], s.th[...], NT)

    arrived(s.sw.at[om], "sw")
    arrived(s.u.at[om], "u")

    u = (s.u[0] + s.u[1])[:1, :]
    mean = rowsum(s.tpg[...].astype(F32) * u) * (1.0 / D)
    product = merged(s.sw[0], s.sw[1])[:, :1] * (1.0 / D)
    g_txt[...] = s.rs[...][:, :1] * (g_txt[...] - mean - s.nhf[...] * product)

    x_first.finish(store(s.h1, XHALF, low))
    y_second.begin()
    y_first.finish(store(s.h1, ZROWS, high))
    x_second.begin()
    y_second.finish(store(s.h2, XWIN, low))
    x_second.finish(store(s.h2, XWIN, high))

    @pl.when(core == 0)
    def _():
        nhb_copy.wait_send()
        tpg_copy.wait_send()

    @pl.when(core == 1)
    def _():
        imf_copy.wait_send()
        pg_copy.wait_send()

    def head_far(i):
        s.h3send[rows(i), :] = s.h2[rows(i, oz * XWIN), :].astype(BF)

    each(XWIN // 16, head_far)
    send(copy(s.h3send, s.h3recv, "h3", 0, dev(zz=oz)))

    arrived(s.grecv, "g")

    def image_input(i):
        r = rows(i)
        g_img[r, :] = pick(s.gip[r, :], m) + s.grecv[r, :].astype(F32)

    each(PAIRS // 16, image_input)

    arrived(s.h3recv, "h3")

    def head_near(i):
        s.h4[rows(i), :] = s.h2[rows(i, zh * XWIN), :] + s.h3recv[rows(i), :].astype(F32)

    each(XWIN // 16, head_near)
    theirs = s.h4.at[pl.ds(pl.multiple_of(oc * 16, 16), FIN)]
    send(copy(theirs, s.finr, "fin", 0, twin))
    own = pltpu.roll(s.h4[...], lax.rem(XWIN - 4 * x - LAST * core, XWIN), 0)[:LAST, :]
    arrived(s.finr, "fin")
    got = pltpu.roll(s.finr[...], lax.rem(FIN - 4 * x - 2 * core, FIN), 0)[:LAST, :]
    g_ih[...] = jnp.where(core == 0, own, got)
    g_th[...] = jnp.where(core == 0, got, own)

    for c in sent:
        c.wait_send()


def per_device(img_feat, img_head, txt_feat, txt_head):
    vmem = pl.BlockSpec(memory_space=pltpu.VMEM)
    g_img, g_ih, g_txt, g_th = pl.pallas_call(
        kernel,
        out_shape=(
            jax.ShapeDtypeStruct((PAIRS, HALF), F32),
            jax.ShapeDtypeStruct((LAST, HALF), F32),
            jax.ShapeDtypeStruct((PAIRS, HALF), F32),
            jax.ShapeDtypeStruct((LAST, HALF), F32),
        ),
        in_specs=[pl.BlockSpec(memory_space=pl.ANY)] * 4,
        out_specs=(vmem,) * 4,
        scratch_shapes=[pltpu.VMEM(shape, kind) for shape, kind in SCRATCH.values()]
        + [pltpu.SemaphoreType.DMA((total_sends,)), pltpu.SemaphoreType.DMA((total_recvs,))]
        + [pltpu.SemaphoreType.DMA((4,))],
        compiler_params=pltpu.CompilerParams(
            collective_id=0, has_side_effects=True, vmem_limit_bytes=60 * 1024 * 1024
        ),
        cost_estimate=pl.CostEstimate(flops=14 * 10**9, bytes_accessed=5 * 10**6, transcendentals=0),
    )(img_feat, img_head.T, txt_feat, txt_head)
    return g_img, g_ih, g_txt, g_th.T


def solution(mesh):
    in_specs = (P("dp", None), P(None, "mp"), P("dp", None), P("mp", None))
    out_specs = (P("dp", "mp"), P("dp", "mp"), P("dp", "mp"), P("mp", "dp"))
    return jax.shard_map(
        per_device, mesh=mesh, in_specs=in_specs, out_specs=out_specs, check_vma=False
    )
```

```python
import types

import jax
import jax.numpy as jnp
from jax import lax
from jax.experimental import pallas as pl
from jax.experimental.pallas import tpu as pltpu
from jax.sharding import PartitionSpec as P

LOGIT_SCALE = 10.0
LOGIT_BIAS = -2.5
NORM_EPS = 1e-06

NX = 4
NY = 4
NZ = 2
NC = 2
D = 1152
HALF = D // 2
PAIRS = 208
OWN = PAIRS // 2
WIN = 112
STEP = PAIRS - WIN
TC = NZ * WIN
IMGS = NX * PAIRS
YROWS = D // NY
ZROWS = YROWS // NZ
LAST = ZROWS // (NX * NC)
XWIN = 48
XHALF = NY * NZ * XWIN // 2
FIN = 32
CUT = 64
IMAGE_PARTS = ((0, WIN), (WIN, STEP))
TEXT_PARTS = ((0, CUT), (CUT, WIN - CUT))
Z_PARTS = ((0, 32), (32, 32), (64, 48))

COLUMNS = ((0, 256), (256, HALF - 256))

NN = ((1,), (0,))
NT = ((1,), (1,))
TN = ((0,), (0,))
BF = jnp.bfloat16
F32 = jnp.float32

SCRATCH = {
    "tf": ((PAIRS, D), BF),
    "th": ((HALF, D), BF),
    "imf": ((PAIRS, D), BF),
    "iht": ((HALF, D), BF),
    "nhf": ((PAIRS, HALF), F32),
    "nhb": ((PAIRS, HALF), BF),
    "rs": ((PAIRS, 128), F32),
    "tpart": ((PAIRS, D), F32),
    "tsend": ((WIN, D), BF),
    "trecv": ((WIN, D), BF),
    "u": ((2, 8, D), F32),
    "tproj": ((WIN, D), F32),
    "tsc": ((WIN, 128), F32),
    "imh": ((NX, 2, PAIRS, HALF), BF),
    "isc": ((PAIRS, 128), F32),
    "img": ((IMGS, D), BF),
    "txt": ((NY, NC * TC, D), BF),
    "w": ((NY, IMGS, NC * TC), BF),
    "gi": ((IMGS, D), F32),
    "xsend": ((3, PAIRS, D), BF),
    "xa": ((WIN, D), BF),
    "xb": ((STEP, D), BF),
    "xr": ((2, PAIRS, D), BF),
    "gtcsend": ((NY, TC, D), BF),
    "gtcrecv": ((NY, TC, D), BF),
    "gt": ((NY, TC, D), F32),
    "gtall": ((NC * TC, D), F32),
    "ysend": ((3, TC, D), BF),
    "ya": ((NZ, CUT, D), BF),
    "yb": ((NZ, WIN - CUT, D), BF),
    "yr": ((2, TC, D), BF),
    "zsend": ((WIN, D), BF),
    "zrecv": ((WIN, D), BF),
    "gown": ((WIN, D), F32),
    "tw": ((2, WIN, D), BF),
    "sw": ((2, WIN, 128), F32),
    "tpg": ((PAIRS, D), BF),
    "ghalf": ((PAIRS, HALF), F32),
    "izsend": ((PAIRS, HALF), BF),
    "izrecv": ((PAIRS, HALF), BF),
    "dots": ((2, PAIRS, 128), F32),
    "pg": ((PAIRS, HALF), BF),
    "gip": ((PAIRS, D), F32),
    "gsend": ((PAIRS, HALF), BF),
    "grecv": ((PAIRS, HALF), BF),
    "imft": ((PAIRS, D), BF),
    "nhbt": ((PAIRS, HALF), BF),
    "pgt": ((PAIRS, HALF), BF),
    "tpgt": ((PAIRS, D), BF),
    "h": ((NY * NZ, ZROWS, HALF), F32),
    "h1send": ((3, 2, XHALF, HALF), BF),
    "h1r": ((3, 2, XHALF, HALF), BF),
    "h1": ((2 * XHALF, HALF), F32),
    "h2send": ((3, 2, XWIN, HALF), BF),
    "h2r": ((3, 2, XWIN, HALF), BF),
    "h2": ((2 * XWIN, HALF), F32),
    "h3send": ((XWIN, HALF), BF),
    "h3recv": ((XWIN, HALF), BF),
    "h4": ((XWIN, HALF), F32),
    "finr": ((FIN, HALF), F32),
}

GROUPS = (
    ("t", 2), ("u", 1), ("img", NX * 4), ("txt", NY * NZ * 2), ("txtc", NY * NZ), ("xa", 1), ("xb", 1), ("xr", 4),
    ("iz", 1), ("dots", 1), ("gtc", NY), ("ya", 2), ("yb", 2), ("yr", 8), ("z", 3), ("tw", 3), ("sw", 1),
    ("g", 1), ("imft", 1), ("nhbt", 1), ("pgt", 1), ("tpgt", 1),
    ("h1r", 6), ("h2r", 6), ("h3", 1), ("fin", 1),
)
RECVS = {}
total_recvs = 0
for group, many in GROUPS:
    RECVS[group] = total_recvs
    total_recvs += many
total_sends = 160


def dot(a, b, dims):
    return lax.dot_general(a, b, (dims, ((), ())), preferred_element_type=F32)


def rows(i, first=0):
    return pl.ds(pl.multiple_of(first + i * 16, 16), 16)


def rowsum(v):
    return jnp.sum(v, -1, keepdims=True)


def wide(v):
    return jnp.broadcast_to(v, (v.shape[0], 128))


def each(count, body):
    lax.fori_loop(0, count, lambda i, c: (body(i), c)[1], 0)


def kernel(img_feat, img_head_t, txt_feat, txt_head, g_img, g_ih, g_txt, g_th, *scratch):
    s = types.SimpleNamespace(**dict(zip(SCRATCH, scratch)))
    ssem, rsem, lsem = scratch[len(SCRATCH) :]
    dp, m = lax.axis_index("dp"), lax.axis_index("mp")
    core = lax.rem(dp, NC)
    x = lax.rem(dp // NC, NX)
    zh = lax.rem(dp // (NC * NX), NZ)
    y = dp // (NC * NX * NZ)
    om, oc, oz = 1 - m, 1 - core, 1 - zh

    loads = [
        pltpu.make_async_copy(src, dst, lsem.at[at])
        for at, (src, dst) in enumerate(
            ((txt_feat, s.tf), (txt_head, s.th), (img_feat, s.imf), (img_head_t, s.iht))
        )
    ]
    for load in loads:
        load.start()

    def dev(yy=None, zz=None, xx=None, cc=None, mm=None):
        yy = y if yy is None else yy
        zz = zh if zz is None else zz
        xx = x if xx is None else xx
        cc = core if cc is None else cc
        mm = m if mm is None else mm
        return (((yy * NZ + zz) * NX + xx) * NC + cc, mm)

    def other(base, by, size):
        return lax.rem(base + by, size)

    x1, x2, x3 = (other(x, d, NX) for d in (1, 2, 3))
    y1, y2, y3 = (other(y, d, NY) for d in (1, 2, 3))
    mate, twin, far = dev(mm=om), dev(cc=oc), dev(zz=oz, mm=om)
    xup, xdown, yup, ydown = dev(xx=x1), dev(xx=x3), dev(yy=y1), dev(yy=y3)

    used = [0]
    sent = []

    def copy(src, dst, group, at, to):
        used[0] += 1
        return pltpu.make_async_remote_copy(
            src_ref=src,
            dst_ref=dst,
            send_sem=ssem.at[used[0] - 1],
            recv_sem=rsem.at[RECVS[group] + at],
            device_id=to,
            device_id_type=pl.DeviceIdType.MESH,
        )

    def send(c):
        c.start()
        sent.append(c)
        return c

    def arrived(ref, group, at=0):
        pltpu.make_async_remote_copy(
            src_ref=ref,
            dst_ref=ref,
            send_sem=ssem.at[0],
            recv_sem=rsem.at[RECVS[group] + at],
            device_id=twin,
            device_id_type=pl.DeviceIdType.MESH,
        ).wait_recv()

    def pick(whole, which):
        return jnp.where(which == 0, whole[:, :HALF], whole[:, HALF:])

    barrier = pltpu.get_barrier_semaphore()
    friends = [mate, twin, far, dev(zz=oz), xup, xdown, yup, ydown, dev(xx=x2), dev(yy=y2)]
    for friend in friends:
        pl.semaphore_signal(barrier, inc=1, device_id=friend, device_id_type=pl.DeviceIdType.MESH)

    loads[0].wait()

    t = s.tf[...].astype(F32)
    t = t - rowsum(t) * (1.0 / D)
    rs = lax.rsqrt(rowsum(t * t) * (1.0 / D) + NORM_EPS)
    half = pick(t * rs, m)
    s.nhf[...] = half
    s.nhb[...] = half.astype(BF)
    s.rs[...] = wide(rs)
    loads[1].wait()
    s.tpart[...] = dot(s.nhb[...], s.th[...], NN)

    def tosend(i):
        s.tsend[rows(i), :] = s.tpart[rows(i, om * STEP), :].astype(BF)

    each(WIN // 16, tosend)
    pl.semaphore_wait(barrier, len(friends))
    for half, where in enumerate(TEXT_PARTS):
        r = pl.ds(*where)
        send(copy(s.tsend.at[r], s.trecv.at[r], "t", half, mate))

    loads[2].wait()
    loads[3].wait()
    s.imh[x, m] = dot(s.imf[...], s.iht[...], NT).astype(BF)

    def image_part(xx, half, cut):
        if cut is None:
            return s.imh.at[xx, half]
        return s.imh.at[xx, half, pl.ds(*IMAGE_PARTS[cut])]

    def send_image(xx, half, to, cut=None):
        ref = image_part(xx, half, cut)
        send(copy(ref, ref, "img", xx * 4 + half * 2 + (cut or 0), to))

    def image_arrived(xx, half, cut=None):
        arrived(image_part(xx, half, cut), "img", xx * 4 + half * 2 + (cut or 0))

    def forward_image(half):
        image_arrived(x1, half)
        send_image(x1, half, xdown, 0)
        image_arrived(x3, half)
        send_image(x3, half, xup, 1)

    for to in (mate, xup, xdown):
        send_image(x, m, to)
    s.u[m] = dot(jnp.ones((8, HALF), BF), s.th[...], NN)
    send(copy(s.u.at[m], s.u.at[m], "u", 0, mate))

    nhb_copy = copy(s.nhb, s.nhbt, "nhbt", 0, twin)
    imf_copy = copy(s.imf, s.imft, "imft", 0, twin)
    pg_copy = copy(s.pg, s.pgt, "pgt", 0, twin)
    tpg_copy = copy(s.tpg, s.tpgt, "tpgt", 0, twin)

    @pl.when(core == 0)
    def _():
        nhb_copy.start()

    @pl.when(core == 1)
    def _():
        imf_copy.start()


    def own_rows(first, count):
        row = m * STEP + first + lax.broadcasted_iota(jnp.int32, (count, 1), 0)
        return (row >= m * OWN) & (row < m * OWN + OWN)

    def at16(first, count):
        return pl.ds(pl.multiple_of(first, 16), count)

    def embed_text(first, count):
        r = pl.ds(first, count)
        p = s.tpart[at16(m * STEP + first, count), :] + s.trecv[r, :].astype(F32)
        sc = lax.rsqrt(rowsum(p * p) + NORM_EPS)
        s.tproj[r, :] = p
        s.tsc[r, :] = wide(sc)
        emb = jnp.where(own_rows(first, count), p * sc, 0.0).astype(BF)
        s.txt[y, at16(core * TC + zh * WIN + first, count), :] = emb

    def part(yy, zz, cut=None):
        first, count = (0, WIN) if cut is None else TEXT_PARTS[cut]
        return s.txt.at[yy, pl.ds(pl.multiple_of(core * TC + zz * WIN + first, 16), count)]

    def send_text(yy, zz, to, cut=None):
        ref = part(yy, zz, cut)
        send(copy(ref, ref, "txt", yy * 4 + zz * 2 + (cut or 0), to))

    def text_arrived(yy, zz, cut=None):
        arrived(part(yy, zz, cut), "txt", yy * 4 + zz * 2 + (cut or 0))

    def forward_text(zz):
        text_arrived(y1, zz, 0)
        send_text(y1, zz, ydown, 0)
        text_arrived(y3, zz, 0)
        text_arrived(y3, zz, 1)
        send_text(y3, zz, yup, 1)
        send_twin(y3, zz)
        text_arrived(y1, zz, 1)
        send_twin(y1, zz)

    def side_part(yy, cc, zz):
        return s.txt.at[yy, pl.ds(pl.multiple_of(cc * TC + zz * WIN, 16), WIN)]

    def send_twin(yy, zz):
        send(copy(part(yy, zz), part(yy, zz), "txtc", yy * NZ + zz, twin))

    def twin_arrived(yy):
        for zz in range(NZ):
            arrived(side_part(yy, oc, zz), "txtc", yy * NZ + zz)

    for half, (first, count) in enumerate(TEXT_PARTS):
        arrived(s.trecv.at[pl.ds(first, count)], "t", half)
        embed_text(first, count)
        for to in (far, yup, ydown):
            send_text(y, zh, to, half)
    send_twin(y, zh)

    def zero(i):
        s.gi[rows(i), :] = jnp.zeros((16, D), F32)

    each(IMGS // 16, zero)
    forward_image(m)

    for half in (0, 1):
        text_arrived(y, oz, half)
        send_text(y, oz, yup, half)
        send_text(y, oz, ydown, half)
    send_twin(y, oz)

    image_arrived(x, om)
    send_image(x, om, xup)
    send_image(x, om, xdown)

    def embed_images(xx, at, own=False):
        p = jnp.concatenate([s.imh[xx, 0].astype(F32), s.imh[xx, 1].astype(F32)], axis=1)
        sc = lax.rsqrt(rowsum(p * p) + NORM_EPS)
        if own:
            s.isc[...] = wide(sc)
        s.img[pl.ds(at * PAIRS, PAIRS), :] = (p * sc).astype(BF)

    embed_images(x, 0, own=True)

    forward_text(zh)

    def unit(yy, first, count, own=False):
        r = pl.ds(first, count)
        texts = s.txt[yy]
        scores = dot(s.img[r, :], texts, NT)
        weights = 0.5 + 0.5 * jnp.tanh((0.5 * LOGIT_SCALE) * scores + 0.5 * LOGIT_BIAS)
        if own:
            row = lax.broadcasted_iota(jnp.int32, (count, NC * TC), 0)
            col = lax.broadcasted_iota(jnp.int32, (count, NC * TC), 1)
            at = core * TC + zh * WIN
            match = (row - col == m * STEP - at) & (col >= at) & (col < at + WIN)
            weights = weights - match.astype(F32)
        weights = weights.astype(BF)
        s.w[yy, r, :] = weights
        s.gi[r, :] += dot(weights, texts, NN)

    forward_image(om)
    forward_text(oz)
    embed_images(x1, 1)
    embed_images(x3, 2)
    twin_arrived(y)
    unit(y, 0, 3 * PAIRS, own=True)
    twin_arrived(y1)
    unit(y1, 0, 3 * PAIRS)
    twin_arrived(y3)
    unit(y3, 0, 3 * PAIRS)
    for zz in (zh, oz):
        for half in (0, 1):
            text_arrived(y2, zz, half)
        send_twin(y2, zz)
    for half in (0, 1):
        for cut in (0, 1):
            image_arrived(x2, half, cut)
    embed_images(x2, 3)
    each(3, lambda i: unit(other(y, i + i // 2, NY), 3 * PAIRS, PAIRS))

    twin_arrived(y2)
    unit(y2, 2 * PAIRS, 2 * PAIRS)

    def cast(at, place, add=None, first=0, count=PAIRS):
        v = s.gi[pl.ds(place * PAIRS + first, count), :]
        if add is not None:
            v = v + add[...].astype(F32)
        s.xsend[at, pl.ds(first, count), :] = v.astype(BF)

    for half in (0, 1):
        first, count = IMAGE_PARTS[half]
        cast(0, 3, first=first, count=count)
        to, at = ((xup, s.xa), (xdown, s.xb))[half]
        send(copy(s.xsend.at[0, pl.ds(first, count)], at, ("xa", "xb")[half], 0, to))

    def image_back(at, place, half, to, add=None):
        first, count = IMAGE_PARTS[half]
        cast(at, place, add=add, first=first, count=count)
        r = pl.ds(first, count)
        send(copy(s.xsend.at[at, r], s.xr.at[at - 1, r], "xr", (at - 1) * 2 + half, to))

    image_back(2, 2, 0, xdown)
    unit(y2, 0, 2 * PAIRS)
    image_back(1, 1, 1, xup)

    def text_grad(yy):
        s.gtall[...] = dot(s.w[yy], s.img[...], TN)

        def out(i):
            s.gtcsend[yy, rows(i), :] = s.gtall[rows(i, oc * TC), :].astype(BF)
            s.gt[yy, rows(i), :] = s.gtall[rows(i, core * TC), :]

        each(TC // 16, out)

    def send_back_twin(yy):
        send(copy(s.gtcsend.at[yy], s.gtcrecv.at[yy], "gtc", yy, twin))

    def back_twin_arrived(yy):
        arrived(s.gtcrecv.at[yy], "gtc", yy)

    def columns_of(cc):
        return s.w[y2, :, pl.ds(cc * TC, TC)]

    @pl.when(core == 0)
    def _():
        s.gtcsend[y2] = dot(columns_of(1), s.img[...], TN).astype(BF)

    @pl.when(core == 1)
    def _():
        s.gtcsend[y2] = dot(columns_of(0), s.img[...], TN).astype(BF)

    send_back_twin(y2)

    @pl.when(core == 0)
    def _():
        s.gt[y2] = dot(columns_of(0), s.img[...], TN)

    @pl.when(core == 1)
    def _():
        s.gt[y2] = dot(columns_of(1), s.img[...], TN)

    text_grad(y1)
    send_back_twin(y1)
    back_twin_arrived(y2)

    def text_back(at, yy, zz, half, dst, group, index, to, add=None):
        first, count = TEXT_PARTS[half]

        r = at16(zz * WIN + first, count)
        v = s.gt[yy, r, :] + s.gtcrecv[yy, r, :].astype(F32)
        if add is not None:
            v = v + add[zz].astype(F32)
        s.ysend[at, r, :] = v.astype(BF)
        send(copy(s.ysend.at[at, r], dst(r), group, index, to))

    def text_back_to(at, yy, zz, half, to, add=None):
        text_back(at, yy, zz, half, lambda r: s.yr.at[at - 1, r], "yr", (at - 1) * 4 + zz * 2 + half, to, add)

    for zz in (oz, zh):
        text_back(0, y2, zz, 0, lambda r, zz=zz: s.ya.at[zz], "ya", zz, yup)
        text_back(0, y2, zz, 1, lambda r, zz=zz: s.yb.at[zz], "yb", zz, ydown)
    text_grad(y3)
    send_back_twin(y3)
    back_twin_arrived(y1)
    for zz in (oz, zh):
        text_back_to(1, y1, zz, 1, yup)
    back_twin_arrived(y3)
    for zz in (oz, zh):
        text_back_to(2, y3, zz, 0, ydown)
    arrived(s.xa, "xa")
    image_back(1, 1, 0, xup, add=s.xa)
    arrived(s.xb, "xb")
    image_back(2, 2, 1, xdown, add=s.xb)
    text_grad(y)
    send_back_twin(y)
    for zz in (oz, zh):
        arrived(s.ya.at[zz], "ya", zz)
        text_back_to(1, y1, zz, 0, yup, add=s.ya)
        arrived(s.yb.at[zz], "yb", zz)
        text_back_to(2, y3, zz, 1, ydown, add=s.yb)
    back_twin_arrived(y)

    for way in (0, 1):
        for half in (0, 1):
            arrived(s.xr.at[way, pl.ds(*IMAGE_PARTS[half])], "xr", way * 2 + half)

    g = s.gi[pl.ds(0, PAIRS), :] + s.xr[0].astype(F32) + s.xr[1].astype(F32)
    g = LOGIT_SCALE * g
    p = jnp.concatenate([s.imh[x, 0].astype(F32), s.imh[x, 1].astype(F32)], axis=1)
    s.dots[m] = wide(rowsum(g * p))
    s.ghalf[...] = pick(g, m)
    s.izsend[...] = pick(g, om).astype(BF)
    send(copy(s.dots.at[m], s.dots.at[m], "dots", 0, mate))
    send(copy(s.izsend, s.izrecv, "iz", 0, mate))

    def back_arrived(zz):
        for way in (0, 1):
            for half in (0, 1):
                first, count = TEXT_PARTS[half]
                r = pl.ds(pl.multiple_of(zz * WIN + first, 16), count)
                arrived(s.yr.at[way, r], "yr", way * 4 + zz * 2 + half)

    def text_sum(r):
        g = s.gt[y, r, :] + s.gtcrecv[y, r, :].astype(F32)
        return g + s.yr[0, r, :].astype(F32) + s.yr[1, r, :].astype(F32)

    back_arrived(oz)
    for half, (first, count) in enumerate(Z_PARTS):
        r = pl.ds(first, count)
        s.zsend[r, :] = text_sum(at16(oz * WIN + first, count)).astype(BF)
        send(copy(s.zsend.at[r], s.zrecv.at[r], "z", half, far))
    back_arrived(zh)

    s.gown[...] = text_sum(at16(zh * WIN, WIN))


    def text_own(first, count):
        r = pl.ds(first, count)
        g = LOGIT_SCALE * (s.gown[r, :] + s.zrecv[r, :].astype(F32))
        p = s.tproj[r, :]
        sc = s.tsc[r, :][:, :1]
        v = sc * g - (sc * sc * sc) * p * rowsum(p * g)
        v = jnp.where(own_rows(first, count), v, 0.0).astype(BF)
        s.tw[m, r, :] = v
        s.sw[m, r, :] = wide(rowsum(v.astype(F32) * p))

    for half, (first, count) in enumerate(Z_PARTS):
        r = pl.ds(first, count)
        arrived(s.zrecv.at[r], "z", half)
        text_own(first, count)
        send(copy(s.tw.at[m, r], s.tw.at[m, r], "tw", half, mate))
    send(copy(s.sw.at[m], s.sw.at[m], "sw", 0, mate))

    arrived(s.dots.at[om], "dots")
    arrived(s.izrecv, "iz")

    g = s.ghalf[...] + s.izrecv[...].astype(F32)
    sc = s.isc[...][:, :1]
    total = (s.dots[0] + s.dots[1])[:, :1]
    p = s.imh[x, m].astype(F32)
    s.pg[...] = (sc * g - (sc * sc * sc) * p * total).astype(BF)

    @pl.when(core == 1)
    def _():
        pg_copy.start()

    class Sum:
        def __init__(self, load, count, bufs, group, devices, chunks, side):
            self.load, self.chunks = load, chunks
            self.out, self.back = bufs
            self.group, self.side = group, side
            n, cols = self.used, self.cols = pl.ds(0, count), pl.ds(*COLUMNS[side])
            self.copies = [
                copy(self.out.at[at, :, n, cols], self.back.at[at, :, n, cols], group, side * 3 + at, to)
                for at, to in enumerate(devices)
            ]

        def begin(self):
            for at in (1, 0, 2):
                for half in (0, 1):
                    self.out[at, half, self.used, self.cols] = self.load(self.chunks[1 + at], half).astype(BF)
                self.copies[at].start()

        def finish(self, store):
            for at in range(3):
                arrived(self.back.at[at, :, self.used, self.cols], self.group, self.side * 3 + at)
            for half in (0, 1):
                v = self.load(self.chunks[0], half)
                for at in range(3):
                    v = v + self.back[at, half, self.used, self.cols].astype(F32)
                store(half, v)
            for c in self.copies:
                c.wait_send()

    low, high = (pl.ds(*where) for where in COLUMNS)
    bufs1, bufs2 = (s.h1send, s.h1r), (s.h2send, s.h2r)
    along_x, along_y = (xup, dev(xx=x2), xdown), (yup, dev(yy=y2), ydown)
    xs, ys = (x, x1, x2, x3), (y, y1, y2, y3)
    x_first = Sum(
        lambda c, half: s.h[pl.ds(half * NY, NY), at16(c * 32, XWIN), low].reshape(XHALF, COLUMNS[0][1]),
        XHALF, bufs1, "h1r", along_x, xs, 0,
    )
    y_second = Sum(
        lambda c, half: s.h1[at16((c * NZ + half) * XWIN, XWIN), low],
        XWIN, bufs2, "h2r", along_y, ys, 0,
    )
    y_first = Sum(lambda c, half: s.h[c * NZ + half, :, high], ZROWS, bufs1, "h1r", along_y, ys, 1)
    x_second = Sum(
        lambda c, half: s.h1[at16(half * ZROWS + c * 32, XWIN), high],
        XWIN, bufs2, "h2r", along_x, xs, 1,
    )

    def store(to, count, cols):
        def at(half, v):
            to[pl.ds(half * count, count), cols] = v

        return at

    @pl.when(core == 0)
    def _():
        arrived(s.imft, "imft")
        arrived(s.pgt, "pgt")
        h = dot(s.imf[...], s.pg[...], TN) + dot(s.imft[...], s.pgt[...], TN)
        s.h[...] = h.reshape(s.h.shape)
        x_first.begin()
        y_first.begin()

    s.gip[...] = dot(s.pg[...], s.iht[...], NN)

    def image_out(i):
        s.gsend[rows(i), :] = pick(s.gip[rows(i), :], om).astype(BF)

    each(PAIRS // 16, image_out)

    for half, where in enumerate(Z_PARTS):
        arrived(s.tw.at[om, pl.ds(*where)], "tw", half)

    send(copy(s.gsend, s.grecv, "g", 0, mate))

    def merged(a, b):
        a, b = a.astype(F32), b.astype(F32)
        both = a[STEP:, :] + b[: WIN - STEP, :]
        return jnp.concatenate([a[:STEP, :], both, b[WIN - STEP :, :]], axis=0)

    s.tpg[...] = merged(s.tw[0], s.tw[1]).astype(BF)

    @pl.when(core == 0)
    def _():
        tpg_copy.start()

    @pl.when(core == 1)
    def _():
        arrived(s.nhbt, "nhbt")
        arrived(s.tpgt, "tpgt")
        h = dot(s.tpg[...], s.nhb[...], TN) + dot(s.tpgt[...], s.nhbt[...], TN)
        s.h[...] = h.reshape(s.h.shape)
        x_first.begin()
        y_first.begin()


    g_txt[...] = dot(s.tpg[...], s.th[...], NT)

    arrived(s.sw.at[om], "sw")
    arrived(s.u.at[om], "u")

    u = (s.u[0] + s.u[1])[:1, :]
    mean = rowsum(s.tpg[...].astype(F32) * u) * (1.0 / D)
    product = merged(s.sw[0], s.sw[1])[:, :1] * (1.0 / D)
    g_txt[...] = s.rs[...][:, :1] * (g_txt[...] - mean - s.nhf[...] * product)

    x_first.finish(store(s.h1, XHALF, low))
    y_second.begin()
    y_first.finish(store(s.h1, ZROWS, high))
    x_second.begin()
    y_second.finish(store(s.h2, XWIN, low))
    x_second.finish(store(s.h2, XWIN, high))

    @pl.when(core == 0)
    def _():
        nhb_copy.wait_send()
        tpg_copy.wait_send()

    @pl.when(core == 1)
    def _():
        imf_copy.wait_send()
        pg_copy.wait_send()

    def head_far(i):
        s.h3send[rows(i), :] = s.h2[rows(i, oz * XWIN), :].astype(BF)

    each(XWIN // 16, head_far)
    send(copy(s.h3send, s.h3recv, "h3", 0, dev(zz=oz)))

    arrived(s.grecv, "g")

    def image_input(i):
        r = rows(i)
        g_img[r, :] = pick(s.gip[r, :], m) + s.grecv[r, :].astype(F32)

    each(PAIRS // 16, image_input)

    arrived(s.h3recv, "h3")

    def head_near(i):
        s.h4[rows(i), :] = s.h2[rows(i, zh * XWIN), :] + s.h3recv[rows(i), :].astype(F32)

    each(XWIN // 16, head_near)
    theirs = s.h4.at[pl.ds(pl.multiple_of(oc * 16, 16), FIN)]
    send(copy(theirs, s.finr, "fin", 0, twin))
    own = pltpu.roll(s.h4[...], lax.rem(XWIN - 4 * x - LAST * core, XWIN), 0)[:LAST, :]
    arrived(s.finr, "fin")
    got = pltpu.roll(s.finr[...], lax.rem(FIN - 4 * x - 2 * core, FIN), 0)[:LAST, :]
    g_ih[...] = jnp.where(core == 0, own, got)
    g_th[...] = jnp.where(core == 0, got, own)

    for c in sent:
        c.wait_send()


def per_device(img_feat, img_head, txt_feat, txt_head):
    vmem = pl.BlockSpec(memory_space=pltpu.VMEM)
    g_img, g_ih, g_txt, g_th = pl.pallas_call(
        kernel,
        out_shape=(
            jax.ShapeDtypeStruct((PAIRS, HALF), F32),
            jax.ShapeDtypeStruct((LAST, HALF), F32),
            jax.ShapeDtypeStruct((PAIRS, HALF), F32),
            jax.ShapeDtypeStruct((LAST, HALF), F32),
        ),
        in_specs=[pl.BlockSpec(memory_space=pl.ANY)] * 4,
        out_specs=(vmem,) * 4,
        scratch_shapes=[pltpu.VMEM(shape, kind) for shape, kind in SCRATCH.values()]
        + [pltpu.SemaphoreType.DMA((total_sends,)), pltpu.SemaphoreType.DMA((total_recvs,))]
        + [pltpu.SemaphoreType.DMA((4,))],
        compiler_params=pltpu.CompilerParams(
            collective_id=0, has_side_effects=True, vmem_limit_bytes=60 * 1024 * 1024
        ),
        cost_estimate=pl.CostEstimate(flops=14 * 10**9, bytes_accessed=5 * 10**6, transcendentals=0),
    )(img_feat, img_head.T, txt_feat, txt_head)
    return g_img, g_ih, g_txt, g_th.T


def solution(mesh):
    in_specs = (P("dp", None), P(None, "mp"), P("dp", None), P("mp", None))
    out_specs = (P("dp", "mp"), P("dp", "mp"), P("dp", "mp"), P("mp", "dp"))
    return jax.shard_map(
        per_device, mesh=mesh, in_specs=in_specs, out_specs=out_specs, check_vma=False
    )
```
